32 devices in a mesh: band: 2 (over y), grid: 16 (over z, x, core).
Axes of the slice: x: 2, y: 2, z: 4, core: 2. Of those that a mesh axis runs over, the one named last changes fastest.
Arguments:
- orbitals: float32 [2, 2, 192, 192, 192], P('band', None, 'grid'), may hold values from -6 to 6
- occupations: float32 [2], P('band'), may hold values from 0.5 to 2
- ion_potential: float32 [192, 192, 192], P('grid'), may hold values from -0.6 to 0.6
- hxc_potential: float32 [192, 192, 192], P('grid'), may hold values from -0.4 to 0.4
Outputs:
- new_orbitals: float32 [2, 2, 192, 192, 192], P('band', None, 'grid')
- new_potential: float32 [192, 192, 192], P('grid')
The draws below stay inside these ranges and needn't reach their ends.
All inputs are finite; a program needn't handle non-finite values.
Results may differ from the reference program's by a relative error of at most 0.0003.
Values sent between devices are 32-bit elements; how exact they have to be, the bound alone decides.
No kernel may reach another device: no remote copies, remote signals or barrier semaphores. Data moves between devices by JAX's collectives and lax.ppermute only.
A program may use at most 128 MiB of HBM per device.

```python
import math
import jax
import jax.numpy as jnp
from jax import lax

NG = 192
BANDS = 2


def level_of(rng, shape, shards, smallest, top_value):
    loudness = 1.0
    for dim, shards_of in shards:
        heights = jax.random.uniform(jax.random.fold_in(jax.random.fold_in(rng, 6), dim), (shards_of,), jnp.float32, smallest / len(shards), top_value / len(shards))
        loudness = loudness * jnp.repeat(jnp.exp(heights), shape[dim] // shards_of).reshape((-1,) + (1,) * (len(shape) - 1 - dim))
    return loudness


def centred(rng, shape, spread, reach, cuts=(), kind=jnp.bfloat16):
    entries = jax.random.normal(rng, shape, jnp.float32) * spread
    if len(cuts) > 0:
        entries = level_of(rng, shape, cuts, -0.22, 0.18) * entries
    return jnp.clip(entries, min=-reach, max=reach).astype(kind)


def setup_inputs(seed: int = 0) -> dict:
    streams_of = jax.random.split(jax.random.key(seed), 5)
    return {
        "orbitals": centred(streams_of[0], (BANDS, 2, NG, NG, NG), 1.0, 6.0, ((0, 2), (2, 16)), jnp.float32),
        "occupations": jnp.clip(jnp.exp(math.log(2.0) - 1.3862944 * jax.random.uniform(streams_of[1], (BANDS,), jnp.float32) ** level_of(streams_of[1], (BANDS,), ((0, 2),), -0.2, 0.2)), 0.5, 2.0),
        "ion_potential": jnp.clip(jax.random.uniform(streams_of[2], (NG, NG, NG), jnp.float32, -0.6, 0.6) * level_of(streams_of[2], (NG, NG, NG), ((0, 16),), -0.4, 0.0), -0.6, 0.6),
        "hxc_potential": jnp.clip(jax.random.uniform(streams_of[3], (NG, NG, NG), jnp.float32, -0.4, 0.4) * level_of(streams_of[3], (NG, NG, NG), ((0, 16),), -0.4, 0.0), -0.4, 0.4),
    }


BESSEL_ZERO = 0.8462873527504802
BESSEL_ONE = 0.36884204609417703
BESSEL_TWO = 0.07581776248
XC_FACTOR = 0.98474502

def squares_grid():
    idx = jnp.arange(NG, dtype=jnp.int32)
    freq = jnp.where(idx < NG // 2, idx, idx - NG).astype(jnp.float32)
    sq = freq * freq
    return sq[:, None, None] + sq[None, :, None] + sq[None, None, :]

def reference(orbitals, occupations, ion_potential, hxc_potential):
    kk = squares_grid()
    kinetic = 2.0 * kk / (3.0 * (NG / 2) ** 2) - 1.0
    potential = ion_potential + hxc_potential

    def hamilton(field):
        return jnp.fft.ifftn(kinetic * jnp.fft.fftn(field)) + potential * field

    def propagate(orbital):
        psi = orbital[0] + 1j * orbital[1]
        first = hamilton(psi)
        second = 2.0 * hamilton(first) - psi
        fresh = BESSEL_ZERO * psi - 2j * BESSEL_ONE * first - 2.0 * BESSEL_TWO * second
        return jnp.stack([jnp.real(fresh), jnp.imag(fresh)]).astype(jnp.float32)
    new_orbitals = lax.map(propagate, orbitals)
    weights = occupations[:, None, None, None]
    density = lax.optimization_barrier(jnp.sum(weights * (new_orbitals[:, 0] ** 2 + new_orbitals[:, 1] ** 2), axis=0))
    kernel = jnp.where(kk > 0, NG * jnp.sqrt(jnp.float32(NG)) / 16.0 / (kk + 1.0), 0.0)
    hartree = jnp.real(jnp.fft.ifftn(kernel * jnp.fft.fftn(density)))
    new_potential = (hartree - XC_FACTOR * jnp.cbrt(density)).astype(jnp.float32)
    return (new_orbitals, new_potential)
```

```python
import functools
import math

import jax
import jax.numpy as jnp
import numpy as np
from jax import lax
from jax.experimental import pallas as pl
from jax.experimental.pallas import tpu as pltpu
from jax.sharding import PartitionSpec as P

BESSEL_ZERO = 0.8462873527504802
BESSEL_ONE = 0.36884204609417703
BESSEL_TWO = 0.07581776248
XC_FACTOR = 0.98474502
PRECISION = lax.Precision.HIGH


def kinetic_matrix(length):
    idx = np.arange(length)
    freq = np.where(idx < length // 2, idx, idx - length).astype(np.float64)
    wave = np.cos(2.0 * math.pi * (np.outer(idx, idx) % length) / length)
    row = (wave @ (freq * freq)) / length * (2.0 / (3.0 * (length / 2) ** 2))
    return row[(idx[:, None] - idx[None, :]) % length].astype(np.float32)


def real_basis(length):
    half = length // 2
    idx = np.arange(length)
    order = np.concatenate([np.arange(half + 1), np.arange(1, half)])
    angle = 2.0 * math.pi * (np.outer(order, idx) % length) / length
    table = np.where((np.arange(length) <= half)[:, None], np.cos(angle), np.sin(angle))
    scale = np.where((order == 0) | (order == half), math.sqrt(1.0 / length), math.sqrt(2.0 / length))
    return (table * scale[:, None]).astype(np.float32), (order * order).astype(np.float32)


def dot(form, left, right):
    return jnp.einsum(form, left, right, precision=PRECISION)


def general(orbitals, occupations, ion_potential, hxc_potential):
    length = orbitals.shape[-1]
    planes = orbitals.shape[2]
    grid = lax.axis_size("grid")
    bands = lax.axis_size("band")
    cells = length * length
    columns = cells // grid
    share = cells // (grid * bands)
    kin = jnp.asarray(kinetic_matrix(length))
    kin_x = kin.reshape(length, grid, planes)
    basis_np, squares = real_basis(length)
    basis = jnp.asarray(basis_np)
    basis_x = basis.reshape(length, grid, planes)

    psi = orbitals[0]
    potential = ion_potential + hxc_potential

    def scatter(fields):
        parts = fields.reshape(fields.shape[0], planes, grid, columns).transpose(2, 1, 0, 3)
        return lax.all_to_all(parts, "grid", split_axis=0, concat_axis=0)

    def along_yz(field):
        return dot("cxyz,zk->cxyk", field, kin) + dot("cxyz,yk->cxkz", field, kin)

    moved = scatter(jnp.concatenate([psi, potential[None]], axis=0))
    local_kin = along_yz(psi) - psi
    applied = local_kin + potential * psi
    mixed = scatter(local_kin + applied)
    twice = along_yz(applied) - applied + potential * applied

    along = dot("ksp,spcn->ckn", kin_x, moved[:, :, :2])
    again = dot("ksp,spcn->ckn", kin_x, mixed) + dot("kx,cxn->ckn", kin, along)
    potential_cols = moved[:, :, 2].reshape(length, columns)
    again = again + potential_cols * along
    turned = jnp.stack([along[1], -along[0]])
    update = 2.0 * BESSEL_ONE * turned - 4.0 * BESSEL_TWO * again
    update = update.reshape(2, grid, planes, columns).transpose(1, 2, 0, 3)
    update = lax.all_to_all(update, "grid", split_axis=0, concat_axis=0)
    update = update.transpose(2, 1, 0, 3).reshape(psi.shape)

    turned = jnp.stack([applied[1], -applied[0]])
    fresh = (
        (BESSEL_ZERO + 2.0 * BESSEL_TWO) * psi
        + 2.0 * BESSEL_ONE * turned
        - 4.0 * BESSEL_TWO * twice
        + update
    )
    part = occupations[0] * (fresh[0] * fresh[0] + fresh[1] * fresh[1])
    density = lax.psum(part, "band")

    spectrum = dot("xyz,kz->xyk", part, basis)
    spectrum = dot("xyk,jy->xjk", spectrum, basis)
    spectrum = spectrum.reshape(planes, bands * grid, share).transpose(1, 0, 2)
    spectrum = lax.all_to_all(spectrum, ("band", "grid"), split_axis=0, concat_axis=0)
    spectrum = spectrum.reshape(bands, grid, planes, share).sum(axis=0)
    spectrum = dot("ksp,spn->kn", basis_x, spectrum)
    start = (lax.axis_index("band") * grid + lax.axis_index("grid")) * share
    cell = start + jnp.arange(share, dtype=jnp.int32)
    table = jnp.asarray(squares)
    total = table[:, None] + (table[cell // length] + table[cell % length])[None, :]
    kernel = jnp.where(total > 0, length * math.sqrt(length) / 16.0 / (total + 1.0), 0.0)
    spectrum = dot("kx,kn->xn", basis, kernel * spectrum)
    spectrum = spectrum.reshape(1, grid, planes, share)
    spectrum = jnp.broadcast_to(spectrum, (bands, grid, planes, share)).reshape(bands * grid, planes, share)
    spectrum = lax.all_to_all(spectrum, ("band", "grid"), split_axis=0, concat_axis=0)
    spectrum = spectrum.transpose(1, 0, 2).reshape(planes, length, length)
    spectrum = dot("xjk,jy->xyk", spectrum, basis)
    hartree = dot("xyk,kz->xyz", spectrum, basis)
    return (fresh[None], hartree - XC_FACTOR * jnp.cbrt(density))


LANES = 128


def product(left, right):
    return jnp.dot(left, right, precision=lax.Precision.HIGHEST, preferred_element_type=jnp.float32)


def split(array):
    high = array.astype(jnp.bfloat16)
    return high, (array - high.astype(jnp.float32)).astype(jnp.bfloat16)


def product_of_parts(left, right):
    total = jnp.dot(left[0], right[0], preferred_element_type=jnp.float32)
    total = total + jnp.dot(left[1], right[0], preferred_element_type=jnp.float32)
    return total + jnp.dot(left[0], right[1], preferred_element_type=jnp.float32)


def whole_tiles(rows):
    return -(-rows // 8) * 8


def chunk_rows(sizes):
    planes, _, rows, share = sizes
    return whole_tiles(planes * (2 * rows + share)), whole_tiles(planes * share)


def kinetic(plane, kin):
    return product(plane, kin) + product(kin, plane)


def pack(plane, packed):
    length = plane.shape[0]
    half = length // 2
    packed[:length, :] = plane[:, :LANES]
    packed[length:, :] = jnp.concatenate([plane[:half, LANES:], plane[half:, LANES:]], axis=1)


def unpack(packed, length):
    side = length - LANES
    tail = packed[length:, :]
    right = jnp.concatenate([tail[:, :side], tail[:, side:]], axis=0)
    return jnp.concatenate([packed[:length, :], right], axis=1)


def fill(out_ref, count, chunk, used):
    if used < chunk:

        @pl.when(pl.program_id(0) == 0)
        def _():
            for to in range(count):
                out_ref[pl.ds(to * chunk + used, chunk - used), :] = jnp.zeros((chunk - used, LANES), jnp.float32)


def pack_kernel(sizes, band_ref, psi_ref, ion_ref, hxc_ref, out_ref, packed):
    planes, grid, rows, share = sizes
    plane = pl.program_id(0)
    stride = 2 * rows + share
    chunk = chunk_rows(sizes)[0]
    fill(out_ref, grid, chunk, planes * stride)
    for part in range(2):
        pack(psi_ref[0, part, 0], packed)
        for to in range(grid):
            start = to * chunk + plane * stride + part * rows
            out_ref[pl.ds(start, rows), :] = packed[pl.ds(to * rows, rows), :]
    pack(ion_ref[0] + hxc_ref[0], packed)
    band = band_ref[0]
    for to in range(grid):
        start = to * chunk + plane * stride + 2 * rows
        out_ref[pl.ds(start, share), :] = packed[pl.ds(to * rows + band * share, share), :]


def plane_kernel(sizes, psi_ref, ion_ref, hxc_ref, kin_ref, out_ref, base_ref, packed):
    planes, grid, rows, share = sizes
    plane = pl.program_id(0)
    kin = kin_ref[...]
    potential = ion_ref[0] + hxc_ref[0]
    applied = []
    for part in range(2):
        field = psi_ref[0, part, 0]
        bare = kinetic(field, kin) - field
        applied.append(bare + potential * field)
        pack(bare + applied[part], packed)
        for to in range(grid):
            start = ((to * planes + plane) * 2 + part) * rows
            out_ref[pl.ds(start, rows), :] = packed[pl.ds(to * rows, rows), :]
    for part in range(2):
        twice = kinetic(applied[part], kin) + (potential - 1.0) * applied[part]
        turned = applied[1] if part == 0 else -applied[0]
        base_ref[part, 0] = (
            (BESSEL_ZERO + 2.0 * BESSEL_TWO) * psi_ref[0, part, 0]
            + 2.0 * BESSEL_ONE * turned
            - 4.0 * BESSEL_TWO * twice
        )


def share_kernel(sizes, moved_ref, out_ref):
    planes, grid, rows, share = sizes
    length = planes * grid
    stride = 2 * rows + share
    chunk = chunk_rows(sizes)[0]
    for row in range(share):
        for source in range(grid):
            start = source * chunk + 2 * rows + row
            out_ref[pl.ds(row * length + source * planes, planes), :] = moved_ref[pl.ds(start, planes, stride=stride), :]


def along_kernel(sizes, moved_ref, kin_ref, out_ref, lines):
    planes, grid, rows, share = sizes
    stride = 2 * rows + share
    chunk = chunk_rows(sizes)[0]
    row = pl.program_id(0)
    for source in range(grid):
        for part in range(2):
            start = source * chunk + part * rows + row
            lines[pl.ds(source * planes, planes), part * LANES : (part + 1) * LANES] = moved_ref[
                pl.ds(start, planes, stride=stride), :
            ]
    out_ref[...] = product(kin_ref[...], lines[...])


def update_kernel(sizes, steps, band_ref, mixed_ref, along_ref, own_ref, other_ref, kin_ref, out_ref):
    planes, grid, rows, share = sizes
    length = planes * grid
    kin = split(kin_ref[...])
    step = pl.program_id(0)
    mine_here = band_ref[0] == step // (steps // 2)
    for inner in range(rows // steps):
        row = step * (rows // steps) + inner
        here = slice(inner * length, (inner + 1) * length)
        along = along_ref[here, :]
        mixed = jnp.concatenate(
            [mixed_ref[pl.ds(part * rows + row, length, stride=2 * rows), :] for part in range(2)], axis=1
        )
        again = product_of_parts(kin, split(mixed + along))
        potential = jnp.where(mine_here, own_ref[here, :], other_ref[here, :])
        for part in range(2):
            mine = along[:, part * LANES : (part + 1) * LANES]
            turned = along[:, LANES:] if part == 0 else -along[:, :LANES]
            twice = again[:, part * LANES : (part + 1) * LANES] + potential * mine
            out_ref[pl.ds(part * rows + row, length, stride=2 * rows), :] = (
                2.0 * BESSEL_ONE * turned - 4.0 * BESSEL_TWO * twice
            )


def fresh_kernel(sizes, occ_ref, update_ref, base_ref, basis_ref, turn_ref, fresh_ref, part_ref, out_ref, packed):
    planes, grid, rows, share = sizes
    plane = pl.program_id(0)
    length = planes * grid
    part_sum = None
    for part in range(2):
        for source in range(grid):
            start = ((source * planes + plane) * 2 + part) * rows
            packed[pl.ds(source * rows, rows), :] = update_ref[pl.ds(start, rows), :]
        fresh = base_ref[part, 0] + unpack(packed, length)
        fresh_ref[0, part, 0] = fresh
        part_sum = fresh * fresh if part_sum is None else part_sum + fresh * fresh
    part_sum = occ_ref[0] * part_sum
    pack(part_sum, packed)
    part_ref[...] = packed[...]
    pack(product(product(basis_ref[...], part_sum), turn_ref[...]), packed)
    chunk = chunk_rows(sizes)[1]
    fill(out_ref, 2 * grid, chunk, planes * share)
    for to in range(2 * grid):
        out_ref[pl.ds(to * chunk + plane * share, share), :] = packed[pl.ds(to * share, share), :]


def filter_kernel(sizes, spec_ref, cells_ref, squares_ref, basis_ref, turn_ref, out_ref, lines):
    planes, grid, rows, share = sizes
    length = planes * grid
    chunk = chunk_rows(sizes)[1]

    def places():
        for source in range(grid):
            for row in range(share):
                first, second = (
                    pl.ds((band * grid + source) * chunk + row, planes, stride=share) for band in range(2)
                )
                here = (pl.ds(source * planes, planes), slice(row * LANES, (row + 1) * LANES))
                yield first, second, here

    for first, second, here in places():
        lines[here] = spec_ref[first, :] + spec_ref[second, :]
    total = squares_ref[...] + cells_ref[...]
    scale = length * math.sqrt(length) / 16.0
    kernel = jnp.where(total > 0.0, scale / (total + 1.0), 0.0)
    field = kernel * product(basis_ref[...], lines[...])
    lines[...] = product_of_parts(split(turn_ref[...]), split(field))
    for first, second, here in places():
        piece = lines[here]
        out_ref[first, :] = piece
        out_ref[second, :] = piece
    used = planes * share
    if used < chunk:
        for to in range(2 * grid):
            out_ref[pl.ds(to * chunk + used, chunk - used), :] = jnp.zeros((chunk - used, LANES), jnp.float32)


def last_kernel(sizes, spec_ref, root_ref, basis_ref, turn_ref, out_ref, packed):
    planes, grid, rows, share = sizes
    plane = pl.program_id(0)
    length = planes * grid
    chunk = chunk_rows(sizes)[1]
    for source in range(2 * grid):
        start = source * chunk + plane * share
        packed[pl.ds(source * share, share), :] = spec_ref[pl.ds(start, share), :]
    hartree = product_of_parts(split(turn_ref[...]), split(unpack(packed, length)))
    hartree = product_of_parts(split(hartree), split(basis_ref[...]))
    out_ref[0] = hartree - unpack(root_ref, length)


def shape(*dims):
    return jax.ShapeDtypeStruct(dims, jnp.float32)


def whole(*dims):
    return pl.BlockSpec(dims, lambda *_: (0,) * len(dims))


PARAMS = pltpu.CompilerParams(vmem_limit_bytes=56 << 20)


def cost(flops, moved):
    return pl.CostEstimate(flops=flops, bytes_accessed=moved, transcendentals=0)


def packed_path(orbitals, occupations, ion_potential, hxc_potential):
    length = orbitals.shape[-1]
    planes = orbitals.shape[2]
    grid = lax.axis_size("grid")
    cell_rows = length * length // LANES
    rows = cell_rows // grid
    share = rows // 2
    sizes = (planes, grid, rows, share)
    field = planes * cell_rows
    work = 2 * planes * length**3
    band = lax.axis_index("band").astype(jnp.int32).reshape(1)
    kin = jnp.asarray(kinetic_matrix(length))
    basis_np, squares_np = real_basis(length)
    basis, turn = jnp.asarray(basis_np), jnp.asarray(basis_np.T.copy())
    smem = pl.BlockSpec(memory_space=pltpu.SMEM)
    vmem = pl.BlockSpec(memory_space=pltpu.VMEM)
    psi_spec = pl.BlockSpec((1, 2, 1, length, length), lambda i: (0, 0, i, 0, 0))
    plane_spec = pl.BlockSpec((1, length, length), lambda i: (i, 0, 0))
    pair_spec = pl.BlockSpec((2, 1, length, length), lambda i: (0, i, 0, 0))
    square = whole(length, length)
    scratch = [pltpu.VMEM((cell_rows, LANES), jnp.float32)]

    def swap(array):
        flat = array.reshape(grid, -1, LANES)
        return lax.all_to_all(flat, "grid", split_axis=0, concat_axis=0).reshape(array.shape)

    def swap_all(array):
        flat = array.reshape(2 * grid, -1, LANES)
        return lax.all_to_all(flat, ("band", "grid"), split_axis=0, concat_axis=0).reshape(array.shape)

    moved_rows, spec_rows = (count * grid for count in chunk_rows(sizes))
    spec_rows = 2 * spec_rows
    steps = 6 if rows % 6 == 0 and share % (rows // 6) == 0 else 2
    moved = pl.pallas_call(
        functools.partial(pack_kernel, sizes),
        grid=(planes,),
        in_specs=[smem, psi_spec, plane_spec, plane_spec],
        out_specs=whole(moved_rows, LANES),
        out_shape=shape(moved_rows, LANES),
        scratch_shapes=scratch,
        compiler_params=PARAMS,
        cost_estimate=cost(0, 15 << 20),
    )(band, orbitals, ion_potential, hxc_potential)
    moved = swap(moved)
    mixed, base = pl.pallas_call(
        functools.partial(plane_kernel, sizes),
        grid=(planes,),
        in_specs=[psi_spec, plane_spec, plane_spec, square],
        out_specs=[whole(2 * field, LANES), pair_spec],
        out_shape=[shape(2 * field, LANES), shape(2, planes, length, length)],
        scratch_shapes=scratch,
        compiler_params=PARAMS,
        cost_estimate=cost(8 * 6 * work, 20 << 20),
    )(orbitals, ion_potential, hxc_potential, kin)
    mixed = swap(mixed)

    own = pl.pallas_call(
        functools.partial(share_kernel, sizes),
        in_specs=[vmem],
        out_specs=vmem,
        out_shape=shape(share * length, LANES),
        compiler_params=PARAMS,
        cost_estimate=cost(0, 6 << 20),
    )(moved)
    other = lax.ppermute(own, "band", [(0, 1), (1, 0)])
    along = pl.pallas_call(
        functools.partial(along_kernel, sizes),
        grid=(rows,),
        in_specs=[whole(moved_rows, LANES), square],
        out_specs=pl.BlockSpec((length, 2 * LANES), lambda i: (i, 0)),
        out_shape=shape(rows * length, 2 * LANES),
        scratch_shapes=[pltpu.VMEM((length, 2 * LANES), jnp.float32)],
        compiler_params=PARAMS,
        cost_estimate=cost(2 * 6 * work, 10 << 20),
    )(moved, kin)
    half_spec = pl.BlockSpec((rows // steps * length, LANES), lambda i: (i % (steps // 2), 0))
    update = pl.pallas_call(
        functools.partial(update_kernel, sizes, steps),
        grid=(steps,),
        in_specs=[
            smem,
            whole(2 * field, LANES),
            pl.BlockSpec((rows // steps * length, 2 * LANES), lambda i: (i, 0)),
            half_spec,
            half_spec,
            square,
        ],
        out_specs=whole(2 * field, LANES),
        out_shape=shape(2 * field, LANES),
        compiler_params=PARAMS,
        cost_estimate=cost(2 * 3 * work, 14 << 20),
    )(band, mixed, along, own, other, kin)
    update = swap(update)

    fresh, part, spectrum = pl.pallas_call(
        functools.partial(fresh_kernel, sizes),
        grid=(planes,),
        in_specs=[smem, whole(2 * field, LANES), pair_spec, square, square],
        out_specs=[
            psi_spec,
            pl.BlockSpec((cell_rows, LANES), lambda i: (i, 0)),
            whole(spec_rows, LANES),
        ],
        out_shape=[shape(*orbitals.shape), shape(field, LANES), shape(spec_rows, LANES)],
        scratch_shapes=scratch,
        compiler_params=PARAMS,
        cost_estimate=cost(2 * 6 * work, 16 << 20),
    )(occupations, update, base, basis, turn)
    density = part + lax.ppermute(part, "band", [(0, 1), (1, 0)])
    root = XC_FACTOR * jnp.cbrt(density)

    spectrum = swap_all(spectrum)
    cells_np = squares_np[:, None] + squares_np[None, :]
    half = length // 2
    cells_np = np.concatenate(
        [cells_np[:, :LANES], np.concatenate([cells_np[:half, LANES:], cells_np[half:, LANES:]], axis=1)]
    )
    device = lax.axis_index("band") * grid + lax.axis_index("grid")
    cells = lax.dynamic_slice_in_dim(jnp.asarray(cells_np), device * share, share, axis=0)
    spectrum = pl.pallas_call(
        functools.partial(filter_kernel, sizes),
        in_specs=[vmem] * 5,
        out_specs=vmem,
        out_shape=shape(spec_rows, LANES),
        scratch_shapes=[pltpu.VMEM((length, share * LANES), jnp.float32)],
        compiler_params=PARAMS,
        cost_estimate=cost(6 * work, 5 << 20),
    )(spectrum, cells.reshape(1, share * LANES), jnp.asarray(squares_np)[:, None], basis, turn)
    spectrum, root = lax.optimization_barrier((spectrum, root))
    spectrum = swap_all(spectrum)
    potential = pl.pallas_call(
        functools.partial(last_kernel, sizes),
        grid=(planes,),
        in_specs=[
            whole(spec_rows, LANES),
            pl.BlockSpec((cell_rows, LANES), lambda i: (i, 0)),
            square,
            square,
        ],
        out_specs=plane_spec,
        out_shape=shape(planes, length, length),
        scratch_shapes=scratch,
        compiler_params=PARAMS,
        cost_estimate=cost(2 * 6 * work, 6 << 20),
    )(spectrum, root, basis, turn)
    return (fresh, potential)


def local(orbitals, occupations, ion_potential, hxc_potential):
    length = orbitals.shape[-1]
    parts = 2 * lax.axis_size("grid") * LANES
    fits = length == LANES + LANES // 2 and lax.axis_size("band") == 2 and length * length % parts == 0
    path = packed_path if fits else general
    return path(orbitals, occupations, ion_potential, hxc_potential)


def solution(mesh):
    placed = (
        P("band", None, "grid", None, None),
        P("band"),
        P("grid", None, None),
        P("grid", None, None),
    )
    return jax.shard_map(
        local,
        mesh=mesh,
        in_specs=placed,
        out_specs=(P("band", None, "grid", None, None), P("grid", None, None)),
        check_vma=False,
    )
```

```python
import functools
import math

import jax
import jax.numpy as jnp
import numpy as np
from jax import lax
from jax.experimental import pallas as pl
from jax.experimental.pallas import tpu as pltpu
from jax.sharding import PartitionSpec as P

BESSEL_ZERO = 0.8462873527504802
BESSEL_ONE = 0.36884204609417703
BESSEL_TWO = 0.07581776248
XC_FACTOR = 0.98474502
PRECISION = lax.Precision.HIGH


def kinetic_matrix(length):
    idx = np.arange(length)
    freq = np.where(idx < length // 2, idx, idx - length).astype(np.float64)
    wave = np.cos(2.0 * math.pi * (np.outer(idx, idx) % length) / length)
    row = (wave @ (freq * freq)) / length * (2.0 / (3.0 * (length / 2) ** 2))
    return row[(idx[:, None] - idx[None, :]) % length].astype(np.float32)


def real_basis(length):
    half = length // 2
    idx = np.arange(length)
    order = np.concatenate([np.arange(half + 1), np.arange(1, half)])
    angle = 2.0 * math.pi * (np.outer(order, idx) % length) / length
    table = np.where((np.arange(length) <= half)[:, None], np.cos(angle), np.sin(angle))
    scale = np.where((order == 0) | (order == half), math.sqrt(1.0 / length), math.sqrt(2.0 / length))
    return (table * scale[:, None]).astype(np.float32), (order * order).astype(np.float32)


def dot(form, left, right):
    return jnp.einsum(form, left, right, precision=PRECISION)


def general(orbitals, occupations, ion_potential, hxc_potential):
    length = orbitals.shape[-1]
    planes = orbitals.shape[2]
    grid = lax.axis_size("grid")
    bands = lax.axis_size("band")
    cells = length * length
    columns = cells // grid
    share = cells // (grid * bands)
    kin = jnp.asarray(kinetic_matrix(length))
    kin_x = kin.reshape(length, grid, planes)
    basis_np, squares = real_basis(length)
    basis = jnp.asarray(basis_np)
    basis_x = basis.reshape(length, grid, planes)

    psi = orbitals[0]
    potential = ion_potential + hxc_potential

    def scatter(fields):
        parts = fields.reshape(fields.shape[0], planes, grid, columns).transpose(2, 1, 0, 3)
        return lax.all_to_all(parts, "grid", split_axis=0, concat_axis=0)

    def along_yz(field):
        return dot("cxyz,zk->cxyk", field, kin) + dot("cxyz,yk->cxkz", field, kin)

    moved = scatter(jnp.concatenate([psi, potential[None]], axis=0))
    local_kin = along_yz(psi) - psi
    applied = local_kin + potential * psi
    mixed = scatter(local_kin + applied)
    twice = along_yz(applied) - applied + potential * applied

    along = dot("ksp,spcn->ckn", kin_x, moved[:, :, :2])
    again = dot("ksp,spcn->ckn", kin_x, mixed) + dot("kx,cxn->ckn", kin, along)
    potential_cols = moved[:, :, 2].reshape(length, columns)
    again = again + potential_cols * along
    turned = jnp.stack([along[1], -along[0]])
    update = 2.0 * BESSEL_ONE * turned - 4.0 * BESSEL_TWO * again
    update = update.reshape(2, grid, planes, columns).transpose(1, 2, 0, 3)
    update = lax.all_to_all(update, "grid", split_axis=0, concat_axis=0)
    update = update.transpose(2, 1, 0, 3).reshape(psi.shape)

    turned = jnp.stack([applied[1], -applied[0]])
    fresh = (
        (BESSEL_ZERO + 2.0 * BESSEL_TWO) * psi
        + 2.0 * BESSEL_ONE * turned
        - 4.0 * BESSEL_TWO * twice
        + update
    )
    part = occupations[0] * (fresh[0] * fresh[0] + fresh[1] * fresh[1])
    density = lax.psum(part, "band")

    spectrum = dot("xyz,kz->xyk", part, basis)
    spectrum = dot("xyk,jy->xjk", spectrum, basis)
    spectrum = spectrum.reshape(planes, bands * grid, share).transpose(1, 0, 2)
    spectrum = lax.all_to_all(spectrum, ("band", "grid"), split_axis=0, concat_axis=0)
    spectrum = spectrum.reshape(bands, grid, planes, share).sum(axis=0)
    spectrum = dot("ksp,spn->kn", basis_x, spectrum)
    start = (lax.axis_index("band") * grid + lax.axis_index("grid")) * share
    cell = start + jnp.arange(share, dtype=jnp.int32)
    table = jnp.asarray(squares)
    total = table[:, None] + (table[cell // length] + table[cell % length])[None, :]
    kernel = jnp.where(total > 0, length * math.sqrt(length) / 16.0 / (total + 1.0), 0.0)
    spectrum = dot("kx,kn->xn", basis, kernel * spectrum)
    spectrum = spectrum.reshape(1, grid, planes, share)
    spectrum = jnp.broadcast_to(spectrum, (bands, grid, planes, share)).reshape(bands * grid, planes, share)
    spectrum = lax.all_to_all(spectrum, ("band", "grid"), split_axis=0, concat_axis=0)
    spectrum = spectrum.transpose(1, 0, 2).reshape(planes, length, length)
    spectrum = dot("xjk,jy->xyk", spectrum, basis)
    hartree = dot("xyk,kz->xyz", spectrum, basis)
    return (fresh[None], hartree - XC_FACTOR * jnp.cbrt(density))


LANES = 128


def product(left, right):
    return jnp.dot(left, right, precision=lax.Precision.HIGHEST, preferred_element_type=jnp.float32)


def split(array):
    high = array.astype(jnp.bfloat16)
    return high, (array - high.astype(jnp.float32)).astype(jnp.bfloat16)


def product_of_parts(left, right):
    total = jnp.dot(left[0], right[0], preferred_element_type=jnp.float32)
    total = total + jnp.dot(left[1], right[0], preferred_element_type=jnp.float32)
    return total + jnp.dot(left[0], right[1], preferred_element_type=jnp.float32)


def whole_tiles(rows):
    return -(-rows // 8) * 8


def chunk_rows(sizes):
    planes, _, rows, share = sizes
    return whole_tiles(planes * (2 * rows + share)), whole_tiles(planes * share)


def kinetic(plane, kin):
    return product(plane, kin) + product(kin, plane)


def pack(plane, packed):
    length = plane.shape[0]
    half = length // 2
    packed[:length, :] = plane[:, :LANES]
    packed[length:, :] = jnp.concatenate([plane[:half, LANES:], plane[half:, LANES:]], axis=1)


def unpack(packed, length):
    side = length - LANES
    tail = packed[length:, :]
    right = jnp.concatenate([tail[:, :side], tail[:, side:]], axis=0)
    return jnp.concatenate([packed[:length, :], right], axis=1)


def fill(out_ref, count, chunk, used):
    if used < chunk:

        @pl.when(pl.program_id(0) == 0)
        def _():
            for to in range(count):
                out_ref[pl.ds(to * chunk + used, chunk - used), :] = jnp.zeros((chunk - used, LANES), jnp.float32)


def pack_kernel(sizes, bunch, band_ref, psi_ref, ion_ref, hxc_ref, out_ref, packed):
    planes, grid, rows, share = sizes
    stride = 2 * rows + share
    chunk = chunk_rows(sizes)[0]
    fill(out_ref, grid, chunk, planes * stride)
    band = band_ref[0]
    for inner in range(bunch):
        plane = pl.program_id(0) * bunch + inner
        for part in range(2):
            slot = packed.at[inner * 3 + part]
            pack(psi_ref[0, part, inner], slot)
            for to in range(grid):
                start = to * chunk + plane * stride + part * rows
                out_ref[pl.ds(start, rows), :] = slot[pl.ds(to * rows, rows), :]
        slot = packed.at[inner * 3 + 2]
        pack(ion_ref[inner] + hxc_ref[inner], slot)
        for to in range(grid):
            start = to * chunk + plane * stride + 2 * rows
            out_ref[pl.ds(start, share), :] = slot[pl.ds(to * rows + band * share, share), :]


def plane_kernel(sizes, bunch, psi_ref, ion_ref, hxc_ref, kin_ref, out_ref, base_ref, packed):
    planes, grid, rows, share = sizes
    kin = kin_ref[...]
    for inner in range(bunch):
        plane = pl.program_id(0) * bunch + inner
        potential = ion_ref[inner] + hxc_ref[inner]
        applied = []
        for part in range(2):
            field = psi_ref[0, part, inner]
            bare = kinetic(field, kin) - field
            applied.append(bare + potential * field)
            slot = packed.at[inner * 2 + part]
            pack(bare + applied[part], slot)
            for to in range(grid):
                start = ((to * planes + plane) * 2 + part) * rows
                out_ref[pl.ds(start, rows), :] = slot[pl.ds(to * rows, rows), :]
        for part in range(2):
            twice = kinetic(applied[part], kin) + (potential - 1.0) * applied[part]
            turned = applied[1] if part == 0 else -applied[0]
            base_ref[part, inner] = (
                (BESSEL_ZERO + 2.0 * BESSEL_TWO) * psi_ref[0, part, inner]
                + 2.0 * BESSEL_ONE * turned
                - 4.0 * BESSEL_TWO * twice
            )


def share_kernel(sizes, moved_ref, out_ref):
    planes, grid, rows, share = sizes
    length = planes * grid
    stride = 2 * rows + share
    chunk = chunk_rows(sizes)[0]
    for row in range(share):
        for source in range(grid):
            start = source * chunk + 2 * rows + row
            out_ref[pl.ds(row * length + source * planes, planes), :] = moved_ref[pl.ds(start, planes, stride=stride), :]


def along_kernel(sizes, moved_ref, kin_ref, out_ref, lines):
    planes, grid, rows, share = sizes
    stride = 2 * rows + share
    chunk = chunk_rows(sizes)[0]
    row = pl.program_id(0)
    for source in range(grid):
        for part in range(2):
            start = source * chunk + part * rows + row
            lines[pl.ds(source * planes, planes), part * LANES : (part + 1) * LANES] = moved_ref[
                pl.ds(start, planes, stride=stride), :
            ]
    out_ref[...] = product(kin_ref[...], lines[...])


def update_kernel(sizes, steps, band_ref, mixed_ref, along_ref, own_ref, other_ref, kin_ref, out_ref):
    planes, grid, rows, share = sizes
    length = planes * grid
    kin = split(kin_ref[...])
    step = pl.program_id(0)
    mine_here = band_ref[0] == step // (steps // 2)
    for inner in range(rows // steps):
        row = step * (rows // steps) + inner
        here = slice(inner * length, (inner + 1) * length)
        along = along_ref[here, :]
        mixed = jnp.concatenate(
            [mixed_ref[pl.ds(part * rows + row, length, stride=2 * rows), :] for part in range(2)], axis=1
        )
        again = product_of_parts(kin, split(mixed + along))
        potential = jnp.where(mine_here, own_ref[here, :], other_ref[here, :])
        for part in range(2):
            mine = along[:, part * LANES : (part + 1) * LANES]
            turned = along[:, LANES:] if part == 0 else -along[:, :LANES]
            twice = again[:, part * LANES : (part + 1) * LANES] + potential * mine
            out_ref[pl.ds(part * rows + row, length, stride=2 * rows), :] = (
                2.0 * BESSEL_ONE * turned - 4.0 * BESSEL_TWO * twice
            )


def fresh_kernel(
    sizes, bunch, occ_ref, update_ref, base_ref, basis_ref, turn_ref, fresh_ref, upper_ref, lower_ref, out_ref, packed
):
    planes, grid, rows, share = sizes
    length = planes * grid
    chunk = chunk_rows(sizes)[1]
    cell_rows = rows * grid
    half = cell_rows // 2
    fill(out_ref, 2 * grid, chunk, planes * share)
    for inner in range(bunch):
        plane = pl.program_id(0) * bunch + inner
        part_sum = None
        for part in range(2):
            slot = packed.at[inner * 4 + part]
            for source in range(grid):
                start = ((source * planes + plane) * 2 + part) * rows
                slot[pl.ds(source * rows, rows), :] = update_ref[pl.ds(start, rows), :]
            fresh = base_ref[part, inner] + unpack(slot, length)
            fresh_ref[0, part, inner] = fresh
            part_sum = fresh * fresh if part_sum is None else part_sum + fresh * fresh
        part_sum = occ_ref[0] * part_sum
        slot = packed.at[inner * 4 + 2]
        pack(part_sum, slot)
        upper_ref[inner * half : (inner + 1) * half, :] = slot[:half, :]
        lower_ref[inner * half : (inner + 1) * half, :] = slot[half:, :]
        slot = packed.at[inner * 4 + 3]
        pack(product(product(basis_ref[...], part_sum), turn_ref[...]), slot)
        for to in range(2 * grid):
            out_ref[pl.ds(to * chunk + plane * share, share), :] = slot[pl.ds(to * share, share), :]


def filter_kernel(sizes, spec_ref, cells_ref, squares_ref, basis_ref, turn_ref, out_ref, lines):
    planes, grid, rows, share = sizes
    length = planes * grid
    chunk = chunk_rows(sizes)[1]

    def places():
        for source in range(grid):
            for row in range(share):
                first, second = (
                    pl.ds((band * grid + source) * chunk + row, planes, stride=share) for band in range(2)
                )
                here = (pl.ds(source * planes, planes), slice(row * LANES, (row + 1) * LANES))
                yield first, second, here

    for first, second, here in places():
        lines[here] = spec_ref[first, :] + spec_ref[second, :]
    total = squares_ref[...] + cells_ref[...]
    scale = length * math.sqrt(length) / 16.0
    kernel = jnp.where(total > 0.0, scale / (total + 1.0), 0.0)
    field = kernel * product(basis_ref[...], lines[...])
    lines[...] = product_of_parts(split(turn_ref[...]), split(field))
    for first, second, here in places():
        piece = lines[here]
        out_ref[first, :] = piece
        out_ref[second, :] = piece
    used = planes * share
    if used < chunk:
        for to in range(2 * grid):
            out_ref[pl.ds(to * chunk + used, chunk - used), :] = jnp.zeros((chunk - used, LANES), jnp.float32)


def last_kernel(
    sizes, bunch, spec_ref, upper_ref, lower_ref, upper_other, lower_other, basis_ref, turn_ref, out_ref, packed
):
    planes, grid, rows, share = sizes
    length = planes * grid
    half = rows * grid // 2
    chunk = chunk_rows(sizes)[1]
    turn, basis = split(turn_ref[...]), split(basis_ref[...])
    for inner in range(bunch):
        plane = pl.program_id(0) * bunch + inner
        slot = packed.at[inner * 2]
        for source in range(2 * grid):
            start = source * chunk + plane * share
            slot[pl.ds(source * share, share), :] = spec_ref[pl.ds(start, share), :]
        hartree = product_of_parts(turn, split(unpack(slot, length)))
        hartree = product_of_parts(split(hartree), basis)
        slot = packed.at[inner * 2 + 1]
        here = slice(inner * half, (inner + 1) * half)
        slot[:half, :] = upper_ref[here, :] + upper_other[here, :]
        slot[half:, :] = lower_ref[here, :] + lower_other[here, :]
        root = jnp.exp(jnp.log(unpack(slot, length)) * (1.0 / 3.0))
        out_ref[inner] = hartree - XC_FACTOR * root


def shape(*dims):
    return jax.ShapeDtypeStruct(dims, jnp.float32)


def whole(*dims):
    return pl.BlockSpec(dims, lambda *_: (0,) * len(dims))


PARAMS = pltpu.CompilerParams(vmem_limit_bytes=56 << 20)


def cost(flops, moved):
    return pl.CostEstimate(flops=flops, bytes_accessed=moved, transcendentals=0)


def packed_path(orbitals, occupations, ion_potential, hxc_potential):
    length = orbitals.shape[-1]
    planes = orbitals.shape[2]
    grid = lax.axis_size("grid")
    cell_rows = length * length // LANES
    rows = cell_rows // grid
    share = rows // 2
    sizes = (planes, grid, rows, share)
    field = planes * cell_rows
    work = 2 * planes * length**3
    band = lax.axis_index("band").astype(jnp.int32).reshape(1)
    kin = jnp.asarray(kinetic_matrix(length))
    basis_np, squares_np = real_basis(length)
    basis, turn = jnp.asarray(basis_np), jnp.asarray(basis_np.T.copy())
    smem = pl.BlockSpec(memory_space=pltpu.SMEM)
    vmem = pl.BlockSpec(memory_space=pltpu.VMEM)
    bunch = next(count for count in (3, 2, 1) if planes % count == 0)
    psi_spec = pl.BlockSpec((1, 2, bunch, length, length), lambda i: (0, 0, i, 0, 0))
    plane_spec = pl.BlockSpec((bunch, length, length), lambda i: (i, 0, 0))
    pair_spec = pl.BlockSpec((2, bunch, length, length), lambda i: (0, i, 0, 0))
    half_rows = pl.BlockSpec((bunch * cell_rows // 2, LANES), lambda i: (i, 0))
    square = whole(length, length)

    def scratch(count):
        return [pltpu.VMEM((count * bunch, cell_rows, LANES), jnp.float32)]

    def swap(array):
        flat = array.reshape(grid, -1, LANES)
        return lax.all_to_all(flat, "grid", split_axis=0, concat_axis=0).reshape(array.shape)

    def swap_all(array):
        flat = array.reshape(2 * grid, -1, LANES)
        return lax.all_to_all(flat, ("band", "grid"), split_axis=0, concat_axis=0).reshape(array.shape)

    moved_rows, spec_rows = (count * grid for count in chunk_rows(sizes))
    spec_rows = 2 * spec_rows
    steps = 6 if rows % 6 == 0 and share % (rows // 6) == 0 else 2
    moved = pl.pallas_call(
        functools.partial(pack_kernel, sizes, bunch),
        grid=(planes // bunch,),
        in_specs=[smem, psi_spec, plane_spec, plane_spec],
        out_specs=whole(moved_rows, LANES),
        out_shape=shape(moved_rows, LANES),
        scratch_shapes=scratch(3),
        compiler_params=PARAMS,
        cost_estimate=cost(0, 15 << 20),
    )(band, orbitals, ion_potential, hxc_potential)
    moved = swap(moved)
    mixed, base = pl.pallas_call(
        functools.partial(plane_kernel, sizes, bunch),
        grid=(planes // bunch,),
        in_specs=[psi_spec, plane_spec, plane_spec, square],
        out_specs=[whole(2 * field, LANES), pair_spec],
        out_shape=[shape(2 * field, LANES), shape(2, planes, length, length)],
        scratch_shapes=scratch(2),
        compiler_params=PARAMS,
        cost_estimate=cost(8 * 6 * work, 20 << 20),
    )(orbitals, ion_potential, hxc_potential, kin)
    mixed = swap(mixed)

    own = pl.pallas_call(
        functools.partial(share_kernel, sizes),
        in_specs=[vmem],
        out_specs=vmem,
        out_shape=shape(share * length, LANES),
        compiler_params=PARAMS,
        cost_estimate=cost(0, 6 << 20),
    )(moved)
    other = lax.ppermute(own, "band", [(0, 1), (1, 0)])
    along = pl.pallas_call(
        functools.partial(along_kernel, sizes),
        grid=(rows,),
        in_specs=[whole(moved_rows, LANES), square],
        out_specs=pl.BlockSpec((length, 2 * LANES), lambda i: (i, 0)),
        out_shape=shape(rows * length, 2 * LANES),
        scratch_shapes=[pltpu.VMEM((length, 2 * LANES), jnp.float32)],
        compiler_params=PARAMS,
        cost_estimate=cost(2 * 6 * work, 10 << 20),
    )(moved, kin)
    half_spec = pl.BlockSpec((rows // steps * length, LANES), lambda i: (i % (steps // 2), 0))
    update = pl.pallas_call(
        functools.partial(update_kernel, sizes, steps),
        grid=(steps,),
        in_specs=[
            smem,
            whole(2 * field, LANES),
            pl.BlockSpec((rows // steps * length, 2 * LANES), lambda i: (i, 0)),
            half_spec,
            half_spec,
            square,
        ],
        out_specs=whole(2 * field, LANES),
        out_shape=shape(2 * field, LANES),
        compiler_params=PARAMS,
        cost_estimate=cost(2 * 3 * work, 14 << 20),
    )(band, mixed, along, own, other, kin)
    update = swap(update)

    fresh, upper, lower, spectrum = pl.pallas_call(
        functools.partial(fresh_kernel, sizes, bunch),
        grid=(planes // bunch,),
        in_specs=[smem, whole(2 * field, LANES), pair_spec, square, square],
        out_specs=[
            psi_spec,
            half_rows,
            half_rows,
            whole(spec_rows, LANES),
        ],
        out_shape=[
            shape(*orbitals.shape),
            shape(field // 2, LANES),
            shape(field // 2, LANES),
            shape(spec_rows, LANES),
        ],
        scratch_shapes=scratch(4),
        compiler_params=PARAMS,
        cost_estimate=cost(2 * 6 * work, 16 << 20),
    )(occupations, update, base, basis, turn)
    upper_other = lax.ppermute(upper, "band", [(0, 1), (1, 0)])
    lower_other = lax.ppermute(lower, "band", [(0, 1), (1, 0)])

    spectrum = swap_all(spectrum)
    cells_np = squares_np[:, None] + squares_np[None, :]
    half = length // 2
    cells_np = np.concatenate(
        [cells_np[:, :LANES], np.concatenate([cells_np[:half, LANES:], cells_np[half:, LANES:]], axis=1)]
    )
    device = lax.axis_index("band") * grid + lax.axis_index("grid")
    cells = lax.dynamic_slice_in_dim(jnp.asarray(cells_np), device * share, share, axis=0)
    spectrum = pl.pallas_call(
        functools.partial(filter_kernel, sizes),
        in_specs=[vmem] * 5,
        out_specs=vmem,
        out_shape=shape(spec_rows, LANES),
        scratch_shapes=[pltpu.VMEM((length, share * LANES), jnp.float32)],
        compiler_params=PARAMS,
        cost_estimate=cost(6 * work, 5 << 20),
    )(spectrum, cells.reshape(1, share * LANES), jnp.asarray(squares_np)[:, None], basis, turn)
    spectrum, upper_other = lax.optimization_barrier((spectrum, upper_other))
    spectrum = swap_all(spectrum)
    potential = pl.pallas_call(
        functools.partial(last_kernel, sizes, bunch),
        grid=(planes // bunch,),
        in_specs=[
            whole(spec_rows, LANES),
            half_rows,
            half_rows,
            half_rows,
            half_rows,
            square,
            square,
        ],
        out_specs=plane_spec,
        out_shape=shape(planes, length, length),
        scratch_shapes=scratch(2),
        compiler_params=PARAMS,
        cost_estimate=cost(2 * 6 * work, 6 << 20),
    )(spectrum, upper, lower, upper_other, lower_other, basis, turn)
    return (fresh, potential)


def local(orbitals, occupations, ion_potential, hxc_potential):
    length = orbitals.shape[-1]
    parts = 2 * lax.axis_size("grid") * LANES
    fits = length == LANES + LANES // 2 and lax.axis_size("band") == 2 and length * length % parts == 0
    path = packed_path if fits else general
    return path(orbitals, occupations, ion_potential, hxc_potential)


def solution(mesh):
    placed = (
        P("band", None, "grid", None, None),
        P("band"),
        P("grid", None, None),
        P("grid", None, None),
    )
    return jax.shard_map(
        local,
        mesh=mesh,
        in_specs=placed,
        out_specs=(P("band", None, "grid", None, None), P("grid", None, None)),
        check_vma=False,
    )
```

```python
import functools
import math

import jax
import jax.numpy as jnp
import numpy as np
from jax import lax
from jax.experimental import pallas as pl
from jax.experimental.pallas import tpu as pltpu
from jax.sharding import PartitionSpec as P

BESSEL_ZERO = 0.8462873527504802
BESSEL_ONE = 0.36884204609417703
BESSEL_TWO = 0.07581776248
XC_FACTOR = 0.98474502
PRECISION = lax.Precision.HIGH


def kinetic_matrix(length):
    idx = np.arange(length)
    freq = np.where(idx < length // 2, idx, idx - length).astype(np.float64)
    wave = np.cos(2.0 * math.pi * (np.outer(idx, idx) % length) / length)
    row = (wave @ (freq * freq)) / length * (2.0 / (3.0 * (length / 2) ** 2))
    return row[(idx[:, None] - idx[None, :]) % length].astype(np.float32)


def real_basis(length):
    half = length // 2
    idx = np.arange(length)
    order = np.concatenate([np.arange(half + 1), np.arange(1, half)])
    angle = 2.0 * math.pi * (np.outer(order, idx) % length) / length
    table = np.where((np.arange(length) <= half)[:, None], np.cos(angle), np.sin(angle))
    scale = np.where((order == 0) | (order == half), math.sqrt(1.0 / length), math.sqrt(2.0 / length))
    return (table * scale[:, None]).astype(np.float32), (order * order).astype(np.float32)


def dot(form, left, right):
    return jnp.einsum(form, left, right, precision=PRECISION)


def general(orbitals, occupations, ion_potential, hxc_potential):
    length = orbitals.shape[-1]
    planes = orbitals.shape[2]
    grid = lax.axis_size("grid")
    bands = lax.axis_size("band")
    cells = length * length
    columns = cells // grid
    share = cells // (grid * bands)
    kin = jnp.asarray(kinetic_matrix(length))
    kin_x = kin.reshape(length, grid, planes)
    basis_np, squares = real_basis(length)
    basis = jnp.asarray(basis_np)
    basis_x = basis.reshape(length, grid, planes)

    psi = orbitals[0]
    potential = ion_potential + hxc_potential

    def scatter(fields):
        parts = fields.reshape(fields.shape[0], planes, grid, columns).transpose(2, 1, 0, 3)
        return lax.all_to_all(parts, "grid", split_axis=0, concat_axis=0)

    def along_yz(field):
        return dot("cxyz,zk->cxyk", field, kin) + dot("cxyz,yk->cxkz", field, kin)

    moved = scatter(jnp.concatenate([psi, potential[None]], axis=0))
    local_kin = along_yz(psi) - psi
    applied = local_kin + potential * psi
    mixed = scatter(local_kin + applied)
    twice = along_yz(applied) - applied + potential * applied

    along = dot("ksp,spcn->ckn", kin_x, moved[:, :, :2])
    again = dot("ksp,spcn->ckn", kin_x, mixed) + dot("kx,cxn->ckn", kin, along)
    potential_cols = moved[:, :, 2].reshape(length, columns)
    again = again + potential_cols * along
    turned = jnp.stack([along[1], -along[0]])
    update = 2.0 * BESSEL_ONE * turned - 4.0 * BESSEL_TWO * again
    update = update.reshape(2, grid, planes, columns).transpose(1, 2, 0, 3)
    update = lax.all_to_all(update, "grid", split_axis=0, concat_axis=0)
    update = update.transpose(2, 1, 0, 3).reshape(psi.shape)

    turned = jnp.stack([applied[1], -applied[0]])
    fresh = (
        (BESSEL_ZERO + 2.0 * BESSEL_TWO) * psi
        + 2.0 * BESSEL_ONE * turned
        - 4.0 * BESSEL_TWO * twice
        + update
    )
    part = occupations[0] * (fresh[0] * fresh[0] + fresh[1] * fresh[1])
    density = lax.psum(part, "band")

    spectrum = dot("xyz,kz->xyk", part, basis)
    spectrum = dot("xyk,jy->xjk", spectrum, basis)
    spectrum = spectrum.reshape(planes, bands * grid, share).transpose(1, 0, 2)
    spectrum = lax.all_to_all(spectrum, ("band", "grid"), split_axis=0, concat_axis=0)
    spectrum = spectrum.reshape(bands, grid, planes, share).sum(axis=0)
    spectrum = dot("ksp,spn->kn", basis_x, spectrum)
    start = (lax.axis_index("band") * grid + lax.axis_index("grid")) * share
    cell = start + jnp.arange(share, dtype=jnp.int32)
    table = jnp.asarray(squares)
    total = table[:, None] + (table[cell // length] + table[cell % length])[None, :]
    kernel = jnp.where(total > 0, length * math.sqrt(length) / 16.0 / (total + 1.0), 0.0)
    spectrum = dot("kx,kn->xn", basis, kernel * spectrum)
    spectrum = spectrum.reshape(1, grid, planes, share)
    spectrum = jnp.broadcast_to(spectrum, (bands, grid, planes, share)).reshape(bands * grid, planes, share)
    spectrum = lax.all_to_all(spectrum, ("band", "grid"), split_axis=0, concat_axis=0)
    spectrum = spectrum.transpose(1, 0, 2).reshape(planes, length, length)
    spectrum = dot("xjk,jy->xyk", spectrum, basis)
    hartree = dot("xyk,kz->xyz", spectrum, basis)
    return (fresh[None], hartree - XC_FACTOR * jnp.cbrt(density))


LANES = 128


def product(left, right):
    return jnp.dot(left, right, precision=lax.Precision.HIGHEST, preferred_element_type=jnp.float32)


def split(array):
    high = array.astype(jnp.bfloat16)
    return high, (array - high.astype(jnp.float32)).astype(jnp.bfloat16)


def product_of_parts(left, right):
    total = jnp.dot(left[0], right[0], preferred_element_type=jnp.float32)
    total = total + jnp.dot(left[1], right[0], preferred_element_type=jnp.float32)
    return total + jnp.dot(left[0], right[1], preferred_element_type=jnp.float32)


def whole_tiles(rows):
    return -(-rows // 8) * 8


def chunk_rows(sizes):
    planes, _, rows, share = sizes
    return whole_tiles(planes * (2 * rows + share)), whole_tiles(planes * share)


def kinetic(plane, kin):
    return product(plane, kin) + product(kin, plane)


def pack(plane, packed):
    length = plane.shape[0]
    half = length // 2
    packed[:length, :] = plane[:, :LANES]
    packed[length:, :] = jnp.concatenate([plane[:half, LANES:], plane[half:, LANES:]], axis=1)


def unpack(packed, length):
    side = length - LANES
    tail = packed[length:, :]
    right = jnp.concatenate([tail[:, :side], tail[:, side:]], axis=0)
    return jnp.concatenate([packed[:length, :], right], axis=1)


def fill(out_ref, count, chunk, used):
    if used < chunk:

        @pl.when(pl.program_id(0) == 0)
        def _():
            for to in range(count):
                out_ref[pl.ds(to * chunk + used, chunk - used), :] = jnp.zeros((chunk - used, LANES), jnp.float32)


def pack_kernel(sizes, bunch, place_ref, psi_ref, ion_ref, hxc_ref, *refs):
    planes, grid, rows, share = sizes
    *out_refs, packed = refs
    stride = 2 * rows + share
    band, mine = place_ref[0], place_ref[1]
    for out_ref in out_refs:
        fill(out_ref, 1, chunk_rows(sizes)[0], planes * stride)
    for inner in range(bunch):
        first = (pl.program_id(0) * bunch + inner) * stride
        for part in range(2):
            slot = packed.at[inner * 3 + part]
            pack(psi_ref[0, part, inner], slot)
            for turn, out_ref in enumerate(out_refs):
                start = (mine ^ turn) * rows
                out_ref[pl.ds(first + part * rows, rows), :] = slot[pl.ds(start, rows), :]
        slot = packed.at[inner * 3 + 2]
        pack(ion_ref[inner] + hxc_ref[inner], slot)
        for turn, out_ref in enumerate(out_refs):
            start = (mine ^ turn) * rows + band * share
            out_ref[pl.ds(first + 2 * rows, share), :] = slot[pl.ds(start, share), :]


def plane_kernel(sizes, bunch, place_ref, psi_ref, ion_ref, hxc_ref, kin_ref, *refs):
    planes, grid, rows, share = sizes
    *out_refs, base_ref, packed = refs
    mine = place_ref[1]
    kin = kin_ref[...]
    for inner in range(bunch):
        plane = pl.program_id(0) * bunch + inner
        potential = ion_ref[inner] + hxc_ref[inner]
        applied = []
        for part in range(2):
            field = psi_ref[0, part, inner]
            bare = kinetic(field, kin) - field
            applied.append(bare + potential * field)
            slot = packed.at[inner * 2 + part]
            pack(bare + applied[part], slot)
            for turn, out_ref in enumerate(out_refs):
                start = (mine ^ turn) * rows
                out_ref[pl.ds((plane * 2 + part) * rows, rows), :] = slot[pl.ds(start, rows), :]
        for part in range(2):
            twice = kinetic(applied[part], kin) + (potential - 1.0) * applied[part]
            turned = applied[1] if part == 0 else -applied[0]
            base_ref[part, inner] = (
                (BESSEL_ZERO + 2.0 * BESSEL_TWO) * psi_ref[0, part, inner]
                + 2.0 * BESSEL_ONE * turned
                - 4.0 * BESSEL_TWO * twice
            )


def share_kernel(sizes, place_ref, *refs):
    planes, grid, rows, share = sizes
    *moved_refs, out_ref = refs
    length = planes * grid
    stride = 2 * rows + share
    for turn, moved_ref in enumerate(moved_refs):
        first = (place_ref[1] ^ turn) * planes
        for row in range(share):
            out_ref[pl.ds(row * length + first, planes), :] = moved_ref[pl.ds(2 * rows + row, planes, stride=stride), :]


def along_kernel(sizes, place_ref, *refs):
    planes, grid, rows, share = sizes
    *moved_refs, kin_ref, out_ref, lines = refs
    stride = 2 * rows + share
    row = pl.program_id(0)
    for turn, moved_ref in enumerate(moved_refs):
        first = (place_ref[1] ^ turn) * planes
        for part in range(2):
            lines[part, pl.ds(first, planes), :] = moved_ref[pl.ds(part * rows + row, planes, stride=stride), :]
    out_ref[...] = product(kin_ref[...], jnp.concatenate([lines[0], lines[1]], axis=1))


def update_kernel(sizes, steps, place_ref, along_ref, own_ref, other_ref, kin_ref, *refs):
    planes, grid, rows, share = sizes
    mixed_refs, out_refs, lines = refs[:grid], refs[grid : 2 * grid], refs[-1]
    length = planes * grid
    kin = split(kin_ref[...])
    step = pl.program_id(0)
    mine_here = place_ref[0] == step // (steps // 2)
    for inner in range(rows // steps):
        row = step * (rows // steps) + inner
        here = slice(inner * length, (inner + 1) * length)
        slot = lines.at[inner]
        for turn, mixed_ref in enumerate(mixed_refs):
            first = (place_ref[1] ^ turn) * planes
            for part in range(2):
                slot[part, pl.ds(first, planes), :] = mixed_ref[pl.ds(part * rows + row, planes, stride=2 * rows), :]
        along = along_ref[here, :]
        again = product_of_parts(kin, split(jnp.concatenate([slot[0], slot[1]], axis=1) + along))
        potential = jnp.where(mine_here, own_ref[here, :], other_ref[here, :])
        for part in range(2):
            mine = along[:, part * LANES : (part + 1) * LANES]
            turned = along[:, LANES:] if part == 0 else -along[:, :LANES]
            twice = again[:, part * LANES : (part + 1) * LANES] + potential * mine
            slot[part] = 2.0 * BESSEL_ONE * turned - 4.0 * BESSEL_TWO * twice
        for turn, out_ref in enumerate(out_refs):
            first = (place_ref[1] ^ turn) * planes
            for part in range(2):
                out_ref[pl.ds(part * rows + row, planes, stride=2 * rows), :] = slot[part, pl.ds(first, planes), :]


def fresh_kernel(sizes, bunch, place_ref, occ_ref, base_ref, basis_ref, turn_ref, *refs):
    planes, grid, rows, share = sizes
    update_refs = refs[:grid]
    fresh_ref, upper_ref, lower_ref, out_ref, packed = refs[grid:]
    length = planes * grid
    chunk = chunk_rows(sizes)[1]
    cell_rows = rows * grid
    half = cell_rows // 2
    fill(out_ref, 2 * grid, chunk, planes * share)
    for inner in range(bunch):
        plane = pl.program_id(0) * bunch + inner
        part_sum = None
        for part in range(2):
            slot = packed.at[inner * 4 + part]
            for turn, update_ref in enumerate(update_refs):
                start = (place_ref[1] ^ turn) * rows
                slot[pl.ds(start, rows), :] = update_ref[pl.ds((plane * 2 + part) * rows, rows), :]
            fresh = base_ref[part, inner] + unpack(slot, length)
            fresh_ref[0, part, inner] = fresh
            part_sum = fresh * fresh if part_sum is None else part_sum + fresh * fresh
        part_sum = occ_ref[0] * part_sum
        slot = packed.at[inner * 4 + 2]
        pack(part_sum, slot)
        upper_ref[inner * half : (inner + 1) * half, :] = slot[:half, :]
        lower_ref[inner * half : (inner + 1) * half, :] = slot[half:, :]
        slot = packed.at[inner * 4 + 3]
        pack(product(product(basis_ref[...], part_sum), turn_ref[...]), slot)
        for to in range(2 * grid):
            out_ref[pl.ds(to * chunk + plane * share, share), :] = slot[pl.ds(to * share, share), :]


def filter_kernel(sizes, spec_ref, cells_ref, squares_ref, basis_ref, turn_ref, out_ref, lines):
    planes, grid, rows, share = sizes
    length = planes * grid
    chunk = chunk_rows(sizes)[1]

    def places():
        for source in range(grid):
            for row in range(share):
                first, second = (
                    pl.ds((band * grid + source) * chunk + row, planes, stride=share) for band in range(2)
                )
                here = (pl.ds(source * planes, planes), slice(row * LANES, (row + 1) * LANES))
                yield first, second, here

    for first, second, here in places():
        lines[here] = spec_ref[first, :] + spec_ref[second, :]
    total = squares_ref[...] + cells_ref[...]
    scale = length * math.sqrt(length) / 16.0
    kernel = jnp.where(total > 0.0, scale / (total + 1.0), 0.0)
    field = kernel * product(basis_ref[...], lines[...])
    lines[...] = product_of_parts(split(turn_ref[...]), split(field))
    for first, second, here in places():
        piece = lines[here]
        out_ref[first, :] = piece
        out_ref[second, :] = piece
    used = planes * share
    if used < chunk:
        for to in range(2 * grid):
            out_ref[pl.ds(to * chunk + used, chunk - used), :] = jnp.zeros((chunk - used, LANES), jnp.float32)


def last_kernel(
    sizes, bunch, spec_ref, upper_ref, lower_ref, upper_other, lower_other, basis_ref, turn_ref, out_ref, packed
):
    planes, grid, rows, share = sizes
    length = planes * grid
    half = rows * grid // 2
    chunk = chunk_rows(sizes)[1]
    turn, basis = split(turn_ref[...]), split(basis_ref[...])
    for inner in range(bunch):
        plane = pl.program_id(0) * bunch + inner
        slot = packed.at[inner * 2]
        for source in range(2 * grid):
            start = source * chunk + plane * share
            slot[pl.ds(source * share, share), :] = spec_ref[pl.ds(start, share), :]
        hartree = product_of_parts(turn, split(unpack(slot, length)))
        hartree = product_of_parts(split(hartree), basis)
        slot = packed.at[inner * 2 + 1]
        here = slice(inner * half, (inner + 1) * half)
        slot[:half, :] = upper_ref[here, :] + upper_other[here, :]
        slot[half:, :] = lower_ref[here, :] + lower_other[here, :]
        root = jnp.exp(jnp.log(unpack(slot, length)) * (1.0 / 3.0))
        out_ref[inner] = hartree - XC_FACTOR * root


def shape(*dims):
    return jax.ShapeDtypeStruct(dims, jnp.float32)


def whole(*dims):
    return pl.BlockSpec(dims, lambda *_: (0,) * len(dims))


PARAMS = pltpu.CompilerParams(vmem_limit_bytes=56 << 20)


def cost(flops, moved):
    return pl.CostEstimate(flops=flops, bytes_accessed=moved, transcendentals=0)


def packed_path(orbitals, occupations, ion_potential, hxc_potential):
    length = orbitals.shape[-1]
    planes = orbitals.shape[2]
    grid = lax.axis_size("grid")
    cell_rows = length * length // LANES
    rows = cell_rows // grid
    share = rows // 2
    sizes = (planes, grid, rows, share)
    field = planes * cell_rows
    work = 2 * planes * length**3
    place = jnp.stack([lax.axis_index("band"), lax.axis_index("grid")]).astype(jnp.int32)
    kin = jnp.asarray(kinetic_matrix(length))
    basis_np, squares_np = real_basis(length)
    basis, turn = jnp.asarray(basis_np), jnp.asarray(basis_np.T.copy())
    smem = pl.BlockSpec(memory_space=pltpu.SMEM)
    vmem = pl.BlockSpec(memory_space=pltpu.VMEM)
    bunch = next(count for count in (3, 2, 1) if planes % count == 0)
    psi_spec = pl.BlockSpec((1, 2, bunch, length, length), lambda i: (0, 0, i, 0, 0))
    plane_spec = pl.BlockSpec((bunch, length, length), lambda i: (i, 0, 0))
    pair_spec = pl.BlockSpec((2, bunch, length, length), lambda i: (0, i, 0, 0))
    half_rows = pl.BlockSpec((bunch * cell_rows // 2, LANES), lambda i: (i, 0))
    square = whole(length, length)

    def scratch(count):
        return [pltpu.VMEM((count * bunch, cell_rows, LANES), jnp.float32)]

    def swap(pieces):
        swapped = list(pieces)
        for turn in sorted(range(1, grid), key=lambda k: -k):
            pairs = [(place, place ^ turn) for place in range(grid)]
            swapped[turn] = lax.ppermute(pieces[turn], "grid", pairs)
        return swapped

    def swap_all(array):
        flat = array.reshape(2 * grid, -1, LANES)
        return lax.all_to_all(flat, ("band", "grid"), split_axis=0, concat_axis=0).reshape(array.shape)

    moved_rows, spec_rows = chunk_rows(sizes)
    spec_rows = 2 * grid * spec_rows
    mixed_rows = 2 * planes * rows
    steps = 6 if rows % 6 == 0 and share % (rows // 6) == 0 else 2
    moved = pl.pallas_call(
        functools.partial(pack_kernel, sizes, bunch),
        grid=(planes // bunch,),
        in_specs=[smem, psi_spec, plane_spec, plane_spec],
        out_specs=[whole(moved_rows, LANES)] * grid,
        out_shape=[shape(moved_rows, LANES)] * grid,
        scratch_shapes=scratch(3),
        compiler_params=PARAMS,
        cost_estimate=cost(0, 15 << 20),
    )(place, orbitals, ion_potential, hxc_potential)
    moved = swap(moved)
    *mixed, base = pl.pallas_call(
        functools.partial(plane_kernel, sizes, bunch),
        grid=(planes // bunch,),
        in_specs=[smem, psi_spec, plane_spec, plane_spec, square],
        out_specs=[whole(mixed_rows, LANES)] * grid + [pair_spec],
        out_shape=[shape(mixed_rows, LANES)] * grid + [shape(2, planes, length, length)],
        scratch_shapes=scratch(2),
        compiler_params=PARAMS,
        cost_estimate=cost(8 * 6 * work, 20 << 20),
    )(place, orbitals, ion_potential, hxc_potential, kin)
    mixed = swap(mixed)

    own = pl.pallas_call(
        functools.partial(share_kernel, sizes),
        in_specs=[smem] + [vmem] * grid,
        out_specs=vmem,
        out_shape=shape(share * length, LANES),
        compiler_params=PARAMS,
        cost_estimate=cost(0, 6 << 20),
    )(place, *moved)
    other = lax.ppermute(own, "band", [(0, 1), (1, 0)])
    along = pl.pallas_call(
        functools.partial(along_kernel, sizes),
        grid=(rows,),
        in_specs=[smem] + [whole(moved_rows, LANES)] * grid + [square],
        out_specs=pl.BlockSpec((length, 2 * LANES), lambda i: (i, 0)),
        out_shape=shape(rows * length, 2 * LANES),
        scratch_shapes=[pltpu.VMEM((2, length, LANES), jnp.float32)],
        compiler_params=PARAMS,
        cost_estimate=cost(2 * 6 * work, 10 << 20),
    )(place, *moved, kin)
    half_spec = pl.BlockSpec((rows // steps * length, LANES), lambda i: (i % (steps // 2), 0))
    update = pl.pallas_call(
        functools.partial(update_kernel, sizes, steps),
        grid=(steps,),
        in_specs=[
            smem,
            pl.BlockSpec((rows // steps * length, 2 * LANES), lambda i: (i, 0)),
            half_spec,
            half_spec,
            square,
        ]
        + [whole(mixed_rows, LANES)] * grid,
        out_specs=[whole(mixed_rows, LANES)] * grid,
        out_shape=[shape(mixed_rows, LANES)] * grid,
        scratch_shapes=[pltpu.VMEM((rows // steps, 2, length, LANES), jnp.float32)],
        compiler_params=PARAMS,
        cost_estimate=cost(2 * 3 * work, 14 << 20),
    )(place, along, own, other, kin, *mixed)
    update = swap(update)

    fresh, upper, lower, spectrum = pl.pallas_call(
        functools.partial(fresh_kernel, sizes, bunch),
        grid=(planes // bunch,),
        in_specs=[smem, smem, pair_spec, square, square] + [whole(mixed_rows, LANES)] * grid,
        out_specs=[
            psi_spec,
            half_rows,
            half_rows,
            whole(spec_rows, LANES),
        ],
        out_shape=[
            shape(*orbitals.shape),
            shape(field // 2, LANES),
            shape(field // 2, LANES),
            shape(spec_rows, LANES),
        ],
        scratch_shapes=scratch(4),
        compiler_params=PARAMS,
        cost_estimate=cost(2 * 6 * work, 16 << 20),
    )(place, occupations, base, basis, turn, *update)
    upper_other = lax.ppermute(upper, "band", [(0, 1), (1, 0)])
    lower_other = lax.ppermute(lower, "band", [(0, 1), (1, 0)])

    spectrum = swap_all(spectrum)
    cells_np = squares_np[:, None] + squares_np[None, :]
    half = length // 2
    cells_np = np.concatenate(
        [cells_np[:, :LANES], np.concatenate([cells_np[:half, LANES:], cells_np[half:, LANES:]], axis=1)]
    )
    device = lax.axis_index("band") * grid + lax.axis_index("grid")
    cells = lax.dynamic_slice_in_dim(jnp.asarray(cells_np), device * share, share, axis=0)
    spectrum = pl.pallas_call(
        functools.partial(filter_kernel, sizes),
        in_specs=[vmem] * 5,
        out_specs=vmem,
        out_shape=shape(spec_rows, LANES),
        scratch_shapes=[pltpu.VMEM((length, share * LANES), jnp.float32)],
        compiler_params=PARAMS,
        cost_estimate=cost(6 * work, 5 << 20),
    )(spectrum, cells.reshape(1, share * LANES), jnp.asarray(squares_np)[:, None], basis, turn)
    spectrum, upper_other = lax.optimization_barrier((spectrum, upper_other))
    spectrum = swap_all(spectrum)
    potential = pl.pallas_call(
        functools.partial(last_kernel, sizes, bunch),
        grid=(planes // bunch,),
        in_specs=[
            whole(spec_rows, LANES),
            half_rows,
            half_rows,
            half_rows,
            half_rows,
            square,
            square,
        ],
        out_specs=plane_spec,
        out_shape=shape(planes, length, length),
        scratch_shapes=scratch(2),
        compiler_params=PARAMS,
        cost_estimate=cost(2 * 6 * work, 6 << 20),
    )(spectrum, upper, lower, upper_other, lower_other, basis, turn)
    return (fresh, potential)


def local(orbitals, occupations, ion_potential, hxc_potential):
    length = orbitals.shape[-1]
    parts = 2 * lax.axis_size("grid") * LANES
    fits = lax.axis_size("grid") & (lax.axis_size("grid") - 1) == 0
    fits = fits and length == LANES + LANES // 2 and lax.axis_size("band") == 2 and length * length % parts == 0
    path = packed_path if fits else general
    return path(orbitals, occupations, ion_potential, hxc_potential)


def solution(mesh):
    placed = (
        P("band", None, "grid", None, None),
        P("band"),
        P("grid", None, None),
        P("grid", None, None),
    )
    return jax.shard_map(
        local,
        mesh=mesh,
        in_specs=placed,
        out_specs=(P("band", None, "grid", None, None), P("grid", None, None)),
        check_vma=False,
    )
```

```python
import functools
import math

import jax
import jax.numpy as jnp
import numpy as np
from jax import lax
from jax.experimental import pallas as pl
from jax.experimental.pallas import tpu as pltpu
from jax.sharding import PartitionSpec as P

BESSEL_ZERO = 0.8462873527504802
BESSEL_ONE = 0.36884204609417703
BESSEL_TWO = 0.07581776248
XC_FACTOR = 0.98474502
PRECISION = lax.Precision.HIGH


def kinetic_matrix(length):
    idx = np.arange(length)
    freq = np.where(idx < length // 2, idx, idx - length).astype(np.float64)
    wave = np.cos(2.0 * math.pi * (np.outer(idx, idx) % length) / length)
    row = (wave @ (freq * freq)) / length * (2.0 / (3.0 * (length / 2) ** 2))
    return row[(idx[:, None] - idx[None, :]) % length].astype(np.float32)


def real_basis(length):
    half = length // 2
    idx = np.arange(length)
    order = np.concatenate([np.arange(half + 1), np.arange(1, half)])
    angle = 2.0 * math.pi * (np.outer(order, idx) % length) / length
    table = np.where((np.arange(length) <= half)[:, None], np.cos(angle), np.sin(angle))
    scale = np.where((order == 0) | (order == half), math.sqrt(1.0 / length), math.sqrt(2.0 / length))
    return (table * scale[:, None]).astype(np.float32), (order * order).astype(np.float32)


def dot(form, left, right):
    return jnp.einsum(form, left, right, precision=PRECISION)


def general(orbitals, occupations, ion_potential, hxc_potential):
    length = orbitals.shape[-1]
    planes = orbitals.shape[2]
    grid = lax.axis_size("grid")
    bands = lax.axis_size("band")
    cells = length * length
    columns = cells // grid
    share = cells // (grid * bands)
    kin = jnp.asarray(kinetic_matrix(length))
    kin_x = kin.reshape(length, grid, planes)
    basis_np, squares = real_basis(length)
    basis = jnp.asarray(basis_np)
    basis_x = basis.reshape(length, grid, planes)

    psi = orbitals[0]
    potential = ion_potential + hxc_potential

    def scatter(fields):
        parts = fields.reshape(fields.shape[0], planes, grid, columns).transpose(2, 1, 0, 3)
        return lax.all_to_all(parts, "grid", split_axis=0, concat_axis=0)

    def along_yz(field):
        return dot("cxyz,zk->cxyk", field, kin) + dot("cxyz,yk->cxkz", field, kin)

    moved = scatter(jnp.concatenate([psi, potential[None]], axis=0))
    local_kin = along_yz(psi) - psi
    applied = local_kin + potential * psi
    mixed = scatter(local_kin + applied)
    twice = along_yz(applied) - applied + potential * applied

    along = dot("ksp,spcn->ckn", kin_x, moved[:, :, :2])
    again = dot("ksp,spcn->ckn", kin_x, mixed) + dot("kx,cxn->ckn", kin, along)
    potential_cols = moved[:, :, 2].reshape(length, columns)
    again = again + potential_cols * along
    turned = jnp.stack([along[1], -along[0]])
    update = 2.0 * BESSEL_ONE * turned - 4.0 * BESSEL_TWO * again
    update = update.reshape(2, grid, planes, columns).transpose(1, 2, 0, 3)
    update = lax.all_to_all(update, "grid", split_axis=0, concat_axis=0)
    update = update.transpose(2, 1, 0, 3).reshape(psi.shape)

    turned = jnp.stack([applied[1], -applied[0]])
    fresh = (
        (BESSEL_ZERO + 2.0 * BESSEL_TWO) * psi
        + 2.0 * BESSEL_ONE * turned
        - 4.0 * BESSEL_TWO * twice
        + update
    )
    part = occupations[0] * (fresh[0] * fresh[0] + fresh[1] * fresh[1])
    density = lax.psum(part, "band")

    spectrum = dot("xyz,kz->xyk", part, basis)
    spectrum = dot("xyk,jy->xjk", spectrum, basis)
    spectrum = spectrum.reshape(planes, bands * grid, share).transpose(1, 0, 2)
    spectrum = lax.all_to_all(spectrum, ("band", "grid"), split_axis=0, concat_axis=0)
    spectrum = spectrum.reshape(bands, grid, planes, share).sum(axis=0)
    spectrum = dot("ksp,spn->kn", basis_x, spectrum)
    start = (lax.axis_index("band") * grid + lax.axis_index("grid")) * share
    cell = start + jnp.arange(share, dtype=jnp.int32)
    table = jnp.asarray(squares)
    total = table[:, None] + (table[cell // length] + table[cell % length])[None, :]
    kernel = jnp.where(total > 0, length * math.sqrt(length) / 16.0 / (total + 1.0), 0.0)
    spectrum = dot("kx,kn->xn", basis, kernel * spectrum)
    spectrum = spectrum.reshape(1, grid, planes, share)
    spectrum = jnp.broadcast_to(spectrum, (bands, grid, planes, share)).reshape(bands * grid, planes, share)
    spectrum = lax.all_to_all(spectrum, ("band", "grid"), split_axis=0, concat_axis=0)
    spectrum = spectrum.transpose(1, 0, 2).reshape(planes, length, length)
    spectrum = dot("xjk,jy->xyk", spectrum, basis)
    hartree = dot("xyk,kz->xyz", spectrum, basis)
    return (fresh[None], hartree - XC_FACTOR * jnp.cbrt(density))


LANES = 128


def product(left, right):
    return jnp.dot(left, right, precision=lax.Precision.HIGHEST, preferred_element_type=jnp.float32)


def split(array):
    high = array.astype(jnp.bfloat16)
    return high, (array - high.astype(jnp.float32)).astype(jnp.bfloat16)


def product_of_parts(left, right):
    total = jnp.dot(left[0], right[0], preferred_element_type=jnp.float32)
    total = total + jnp.dot(left[1], right[0], preferred_element_type=jnp.float32)
    return total + jnp.dot(left[0], right[1], preferred_element_type=jnp.float32)


def whole_tiles(rows):
    return -(-rows // 8) * 8


def chunk_rows(sizes):
    planes, _, rows, share = sizes
    return whole_tiles(planes * (2 * rows + share)), whole_tiles(planes * share)


def kinetic(plane, kin):
    plane = split(plane)
    return product_of_parts(plane, kin) + product_of_parts(kin, plane)


def pack(plane, packed):
    length = plane.shape[0]
    half = length // 2
    packed[:length, :] = plane[:, :LANES]
    packed[length:, :] = jnp.concatenate([plane[:half, LANES:], plane[half:, LANES:]], axis=1)


def unpack(packed, length):
    side = length - LANES
    tail = packed[length:, :]
    right = jnp.concatenate([tail[:, :side], tail[:, side:]], axis=0)
    return jnp.concatenate([packed[:length, :], right], axis=1)


def fill(out_ref, count, chunk, used):
    if used < chunk:

        @pl.when(pl.program_id(0) == 0)
        def _():
            for to in range(count):
                out_ref[pl.ds(to * chunk + used, chunk - used), :] = jnp.zeros((chunk - used, LANES), jnp.float32)


def pack_kernel(sizes, bunch, turns, place_ref, psi_ref, ion_ref, hxc_ref, *refs):
    planes, grid, rows, share = sizes
    *out_refs, packed = refs
    stride = 2 * rows + share
    band, mine = place_ref[0], place_ref[1]
    for out_ref in out_refs:
        fill(out_ref, 1, chunk_rows(sizes)[0], planes * stride)
    for inner in range(bunch):
        first = (pl.program_id(0) * bunch + inner) * stride
        for part in range(2):
            slot = packed.at[inner * 3 + part]
            pack(psi_ref[0, part, inner], slot)
            for turn, out_ref in zip(turns, out_refs):
                start = (mine ^ turn) * rows
                out_ref[pl.ds(first + part * rows, rows), :] = slot[pl.ds(start, rows), :]
        slot = packed.at[inner * 3 + 2]
        pack(ion_ref[inner] + hxc_ref[inner], slot)
        for turn, out_ref in zip(turns, out_refs):
            start = (mine ^ turn) * rows + band * share
            out_ref[pl.ds(first + 2 * rows, share), :] = slot[pl.ds(start, share), :]


def plane_kernel(sizes, bunch, turns, place_ref, psi_ref, ion_ref, hxc_ref, kin_ref, *refs):
    planes, grid, rows, share = sizes
    *out_refs, base_ref, packed = refs
    mine = place_ref[1]
    kin = split(kin_ref[...])
    for inner in range(bunch):
        plane = pl.program_id(0) * bunch + inner
        potential = ion_ref[inner] + hxc_ref[inner]
        applied = []
        for part in range(2):
            field = psi_ref[0, part, inner]
            bare = kinetic(field, kin) - field
            applied.append(bare + potential * field)
            slot = packed.at[inner * 2 + part]
            pack(bare + applied[part], slot)
            for turn, out_ref in zip(turns, out_refs):
                start = (mine ^ turn) * rows
                out_ref[pl.ds((plane * 2 + part) * rows, rows), :] = slot[pl.ds(start, rows), :]
        for part in range(2):
            twice = kinetic(applied[part], kin) + (potential - 1.0) * applied[part]
            turned = applied[1] if part == 0 else -applied[0]
            base_ref[part, inner] = (
                (BESSEL_ZERO + 2.0 * BESSEL_TWO) * psi_ref[0, part, inner]
                + 2.0 * BESSEL_ONE * turned
                - 4.0 * BESSEL_TWO * twice
            )


def share_kernel(sizes, turns, place_ref, *refs):
    planes, grid, rows, share = sizes
    *moved_refs, out_ref = refs
    length = planes * grid
    stride = 2 * rows + share
    for turn, moved_ref in zip(turns, moved_refs):
        first = (place_ref[1] ^ turn) * planes
        for row in range(share):
            out_ref[pl.ds(row * length + first, planes), :] = moved_ref[pl.ds(2 * rows + row, planes, stride=stride), :]


def along_kernel(sizes, turns, place_ref, *refs):
    planes, grid, rows, share = sizes
    *moved_refs, kin_ref, out_ref, lines = refs
    stride = 2 * rows + share
    row = pl.program_id(0)
    for turn, moved_ref in zip(turns, moved_refs):
        first = (place_ref[1] ^ turn) * planes
        for part in range(2):
            lines[part, pl.ds(first, planes), :] = moved_ref[pl.ds(part * rows + row, planes, stride=stride), :]
    out_ref[...] = product(kin_ref[...], jnp.concatenate([lines[0], lines[1]], axis=1))


def update_kernel(sizes, steps, turns, place_ref, along_ref, own_ref, other_ref, kin_ref, *refs):
    planes, grid, rows, share = sizes
    *mixed_refs, out_ref, lines = refs
    length = planes * grid
    kin = split(kin_ref[...])
    step = pl.program_id(0)
    mine_here = place_ref[0] == step // (steps // 2)
    for inner in range(rows // steps):
        row = step * (rows // steps) + inner
        here = slice(inner * length, (inner + 1) * length)
        slot = lines.at[inner]
        for turn, mixed_ref in zip(turns, mixed_refs):
            first = (place_ref[1] ^ turn) * planes
            for part in range(2):
                slot[part, pl.ds(first, planes), :] = mixed_ref[pl.ds(part * rows + row, planes, stride=2 * rows), :]
        along = along_ref[here, :]
        again = product_of_parts(kin, split(jnp.concatenate([slot[0], slot[1]], axis=1) + along))
        potential = jnp.where(mine_here, own_ref[here, :], other_ref[here, :])
        for part in range(2):
            mine = along[:, part * LANES : (part + 1) * LANES]
            turned = along[:, LANES:] if part == 0 else -along[:, :LANES]
            twice = again[:, part * LANES : (part + 1) * LANES] + potential * mine
            out_ref[pl.ds(part * rows + row, length, stride=2 * rows), :] = (
                2.0 * BESSEL_ONE * turned - 4.0 * BESSEL_TWO * twice
            )


def fresh_kernel(
    sizes, bunch, occ_ref, update_ref, base_ref, basis_ref, turn_ref, fresh_ref, upper_ref, lower_ref, out_ref, packed
):
    planes, grid, rows, share = sizes
    length = planes * grid
    chunk = chunk_rows(sizes)[1]
    cell_rows = rows * grid
    half = cell_rows // 2
    fill(out_ref, 2 * grid, chunk, planes * share)
    for inner in range(bunch):
        plane = pl.program_id(0) * bunch + inner
        part_sum = None
        for part in range(2):
            slot = packed.at[inner * 4 + part]
            for source in range(grid):
                start = ((source * planes + plane) * 2 + part) * rows
                slot[pl.ds(source * rows, rows), :] = update_ref[pl.ds(start, rows), :]
            fresh = base_ref[part, inner] + unpack(slot, length)
            fresh_ref[0, part, inner] = fresh
            part_sum = fresh * fresh if part_sum is None else part_sum + fresh * fresh
        part_sum = occ_ref[0] * part_sum
        slot = packed.at[inner * 4 + 2]
        pack(part_sum, slot)
        upper_ref[inner * half : (inner + 1) * half, :] = slot[:half, :]
        lower_ref[inner * half : (inner + 1) * half, :] = slot[half:, :]
        slot = packed.at[inner * 4 + 3]
        pack(product(product(basis_ref[...], part_sum), turn_ref[...]), slot)
        for to in range(2 * grid):
            out_ref[pl.ds(to * chunk + plane * share, share), :] = slot[pl.ds(to * share, share), :]


def filter_kernel(sizes, spec_ref, cells_ref, squares_ref, basis_ref, turn_ref, out_ref, lines):
    planes, grid, rows, share = sizes
    length = planes * grid
    chunk = chunk_rows(sizes)[1]

    def places():
        for source in range(grid):
            for row in range(share):
                first, second = (
                    pl.ds((band * grid + source) * chunk + row, planes, stride=share) for band in range(2)
                )
                here = (pl.ds(source * planes, planes), slice(row * LANES, (row + 1) * LANES))
                yield first, second, here

    for first, second, here in places():
        lines[here] = spec_ref[first, :] + spec_ref[second, :]
    total = squares_ref[...] + cells_ref[...]
    scale = length * math.sqrt(length) / 16.0
    kernel = jnp.where(total > 0.0, scale / (total + 1.0), 0.0)
    field = kernel * product(basis_ref[...], lines[...])
    lines[...] = product_of_parts(split(turn_ref[...]), split(field))
    for first, second, here in places():
        piece = lines[here]
        out_ref[first, :] = piece
        out_ref[second, :] = piece
    used = planes * share
    if used < chunk:
        for to in range(2 * grid):
            out_ref[pl.ds(to * chunk + used, chunk - used), :] = jnp.zeros((chunk - used, LANES), jnp.float32)


def last_kernel(
    sizes, bunch, spec_ref, upper_ref, lower_ref, upper_other, lower_other, basis_ref, turn_ref, out_ref, packed
):
    planes, grid, rows, share = sizes
    length = planes * grid
    half = rows * grid // 2
    chunk = chunk_rows(sizes)[1]
    turn, basis = split(turn_ref[...]), split(basis_ref[...])
    for inner in range(bunch):
        plane = pl.program_id(0) * bunch + inner
        slot = packed.at[inner * 2]
        for source in range(2 * grid):
            start = source * chunk + plane * share
            slot[pl.ds(source * share, share), :] = spec_ref[pl.ds(start, share), :]
        hartree = product_of_parts(turn, split(unpack(slot, length)))
        hartree = product_of_parts(split(hartree), basis)
        slot = packed.at[inner * 2 + 1]
        here = slice(inner * half, (inner + 1) * half)
        slot[:half, :] = upper_ref[here, :] + upper_other[here, :]
        slot[half:, :] = lower_ref[here, :] + lower_other[here, :]
        root = jnp.exp(jnp.log(unpack(slot, length)) * (1.0 / 3.0))
        out_ref[inner] = hartree - XC_FACTOR * root


def shape(*dims):
    return jax.ShapeDtypeStruct(dims, jnp.float32)


def whole(*dims):
    return pl.BlockSpec(dims, lambda *_: (0,) * len(dims))


PARAMS = pltpu.CompilerParams(vmem_limit_bytes=56 << 20)


def cost(flops, moved):
    return pl.CostEstimate(flops=flops, bytes_accessed=moved, transcendentals=0)


def turn_order(grid):
    order = [0]
    for near in range(grid // 2):
        order += [near + grid // 2] if near == 0 else [near, near + grid // 2]
    return order


def packed_path(orbitals, occupations, ion_potential, hxc_potential):
    length = orbitals.shape[-1]
    planes = orbitals.shape[2]
    grid = lax.axis_size("grid")
    cell_rows = length * length // LANES
    rows = cell_rows // grid
    share = rows // 2
    sizes = (planes, grid, rows, share)
    field = planes * cell_rows
    work = 2 * planes * length**3
    place = jnp.stack([lax.axis_index("band"), lax.axis_index("grid")]).astype(jnp.int32)
    kin = jnp.asarray(kinetic_matrix(length))
    basis_np, squares_np = real_basis(length)
    basis, turn = jnp.asarray(basis_np), jnp.asarray(basis_np.T.copy())
    smem = pl.BlockSpec(memory_space=pltpu.SMEM)
    vmem = pl.BlockSpec(memory_space=pltpu.VMEM)
    bunch = next(count for count in (3, 2, 1) if planes % count == 0)
    psi_spec = pl.BlockSpec((1, 2, bunch, length, length), lambda i: (0, 0, i, 0, 0))
    plane_spec = pl.BlockSpec((bunch, length, length), lambda i: (i, 0, 0))
    pair_spec = pl.BlockSpec((2, bunch, length, length), lambda i: (0, i, 0, 0))
    half_rows = pl.BlockSpec((bunch * cell_rows // 2, LANES), lambda i: (i, 0))
    square = whole(length, length)

    def scratch(count):
        return [pltpu.VMEM((count * bunch, cell_rows, LANES), jnp.float32)]

    def swap_pieces(turns, pieces):
        return [
            lax.ppermute(piece, "grid", [(place, place ^ turn) for place in range(grid)]) if turn else piece
            for turn, piece in zip(turns, pieces)
        ]

    def swap(array):
        flat = array.reshape(grid, -1, LANES)
        return lax.all_to_all(flat, "grid", split_axis=0, concat_axis=0).reshape(array.shape)

    def swap_all(array):
        flat = array.reshape(2 * grid, -1, LANES)
        return lax.all_to_all(flat, ("band", "grid"), split_axis=0, concat_axis=0).reshape(array.shape)

    turns = turn_order(grid)
    moved_rows, spec_rows = chunk_rows(sizes)
    spec_rows = 2 * grid * spec_rows
    mixed_rows = 2 * planes * rows
    steps = 6 if rows % 6 == 0 and share % (rows // 6) == 0 else 2
    moved = pl.pallas_call(
        functools.partial(pack_kernel, sizes, bunch, turns),
        grid=(planes // bunch,),
        in_specs=[smem, psi_spec, plane_spec, plane_spec],
        out_specs=[whole(moved_rows, LANES)] * grid,
        out_shape=[shape(moved_rows, LANES)] * grid,
        scratch_shapes=scratch(3),
        compiler_params=PARAMS,
        cost_estimate=cost(0, 15 << 20),
    )(place, orbitals, ion_potential, hxc_potential)
    *mixed, base = pl.pallas_call(
        functools.partial(plane_kernel, sizes, bunch, turns),
        grid=(planes // bunch,),
        in_specs=[smem, psi_spec, plane_spec, plane_spec, square],
        out_specs=[whole(mixed_rows, LANES)] * grid + [pair_spec],
        out_shape=[shape(mixed_rows, LANES)] * grid + [shape(2, planes, length, length)],
        scratch_shapes=scratch(2),
        compiler_params=PARAMS,
        cost_estimate=cost(8 * 3 * work, 20 << 20),
    )(place, orbitals, ion_potential, hxc_potential, kin)
    late = range(6, grid)
    held = lax.optimization_barrier(([moved[k] for k in late], base))
    base = held[1]
    moved = list(moved)
    for k, piece in zip(late, held[0]):
        moved[k] = piece
    moved = swap_pieces(turns, moved)
    mixed = swap_pieces(turns, mixed)

    own = pl.pallas_call(
        functools.partial(share_kernel, sizes, turns),
        in_specs=[smem] + [vmem] * grid,
        out_specs=vmem,
        out_shape=shape(share * length, LANES),
        compiler_params=PARAMS,
        cost_estimate=cost(0, 6 << 20),
    )(place, *moved)
    other = lax.ppermute(own, "band", [(0, 1), (1, 0)])
    along = pl.pallas_call(
        functools.partial(along_kernel, sizes, turns),
        grid=(rows,),
        in_specs=[smem] + [whole(moved_rows, LANES)] * grid + [square],
        out_specs=pl.BlockSpec((length, 2 * LANES), lambda i: (i, 0)),
        out_shape=shape(rows * length, 2 * LANES),
        scratch_shapes=[pltpu.VMEM((2, length, LANES), jnp.float32)],
        compiler_params=PARAMS,
        cost_estimate=cost(2 * 6 * work, 10 << 20),
    )(place, *moved, kin)
    half_spec = pl.BlockSpec((rows // steps * length, LANES), lambda i: (i % (steps // 2), 0))
    update = pl.pallas_call(
        functools.partial(update_kernel, sizes, steps, turns),
        grid=(steps,),
        in_specs=[
            smem,
            pl.BlockSpec((rows // steps * length, 2 * LANES), lambda i: (i, 0)),
            half_spec,
            half_spec,
            square,
        ]
        + [whole(mixed_rows, LANES)] * grid,
        out_specs=whole(2 * field, LANES),
        out_shape=shape(2 * field, LANES),
        scratch_shapes=[pltpu.VMEM((rows // steps, 2, length, LANES), jnp.float32)],
        compiler_params=PARAMS,
        cost_estimate=cost(2 * 3 * work, 14 << 20),
    )(place, along, own, other, kin, *mixed)
    update = swap(update)

    fresh, upper, lower, spectrum = pl.pallas_call(
        functools.partial(fresh_kernel, sizes, bunch),
        grid=(planes // bunch,),
        in_specs=[smem, whole(2 * field, LANES), pair_spec, square, square],
        out_specs=[
            psi_spec,
            half_rows,
            half_rows,
            whole(spec_rows, LANES),
        ],
        out_shape=[
            shape(*orbitals.shape),
            shape(field // 2, LANES),
            shape(field // 2, LANES),
            shape(spec_rows, LANES),
        ],
        scratch_shapes=scratch(4),
        compiler_params=PARAMS,
        cost_estimate=cost(2 * 6 * work, 16 << 20),
    )(occupations, update, base, basis, turn)
    upper_other = lax.ppermute(upper, "band", [(0, 1), (1, 0)])
    lower_other = lax.ppermute(lower, "band", [(0, 1), (1, 0)])

    spectrum = swap_all(spectrum)
    cells_np = squares_np[:, None] + squares_np[None, :]
    half = length // 2
    cells_np = np.concatenate(
        [cells_np[:, :LANES], np.concatenate([cells_np[:half, LANES:], cells_np[half:, LANES:]], axis=1)]
    )
    device = lax.axis_index("band") * grid + lax.axis_index("grid")
    cells = lax.dynamic_slice_in_dim(jnp.asarray(cells_np), device * share, share, axis=0)
    spectrum = pl.pallas_call(
        functools.partial(filter_kernel, sizes),
        in_specs=[vmem] * 5,
        out_specs=vmem,
        out_shape=shape(spec_rows, LANES),
        scratch_shapes=[pltpu.VMEM((length, share * LANES), jnp.float32)],
        compiler_params=PARAMS,
        cost_estimate=cost(6 * work, 5 << 20),
    )(spectrum, cells.reshape(1, share * LANES), jnp.asarray(squares_np)[:, None], basis, turn)
    spectrum, upper_other = lax.optimization_barrier((spectrum, upper_other))
    spectrum = swap_all(spectrum)
    potential = pl.pallas_call(
        functools.partial(last_kernel, sizes, bunch),
        grid=(planes // bunch,),
        in_specs=[
            whole(spec_rows, LANES),
            half_rows,
            half_rows,
            half_rows,
            half_rows,
            square,
            square,
        ],
        out_specs=plane_spec,
        out_shape=shape(planes, length, length),
        scratch_shapes=scratch(2),
        compiler_params=PARAMS,
        cost_estimate=cost(2 * 6 * work, 6 << 20),
    )(spectrum, upper, lower, upper_other, lower_other, basis, turn)
    return (fresh, potential)


def local(orbitals, occupations, ion_potential, hxc_potential):
    length = orbitals.shape[-1]
    parts = 2 * lax.axis_size("grid") * LANES
    fits = lax.axis_size("grid") & (lax.axis_size("grid") - 1) == 0
    fits = fits and length == LANES + LANES // 2 and lax.axis_size("band") == 2 and length * length % parts == 0
    path = packed_path if fits else general
    return path(orbitals, occupations, ion_potential, hxc_potential)


def solution(mesh):
    placed = (
        P("band", None, "grid", None, None),
        P("band"),
        P("grid", None, None),
        P("grid", None, None),
    )
    return jax.shard_map(
        local,
        mesh=mesh,
        in_specs=placed,
        out_specs=(P("band", None, "grid", None, None), P("grid", None, None)),
        check_vma=False,
    )
```

```python
import functools
import math

import jax
import jax.numpy as jnp
import numpy as np
from jax import lax
from jax.experimental import pallas as pl
from jax.experimental.pallas import tpu as pltpu
from jax.sharding import PartitionSpec as P

BESSEL_ZERO = 0.8462873527504802
BESSEL_ONE = 0.36884204609417703
BESSEL_TWO = 0.07581776248
XC_FACTOR = 0.98474502
PRECISION = lax.Precision.HIGH


def kinetic_matrix(length):
    idx = np.arange(length)
    freq = np.where(idx < length // 2, idx, idx - length).astype(np.float64)
    wave = np.cos(2.0 * math.pi * (np.outer(idx, idx) % length) / length)
    row = (wave @ (freq * freq)) / length * (2.0 / (3.0 * (length / 2) ** 2))
    return row[(idx[:, None] - idx[None, :]) % length].astype(np.float32)


def real_basis(length):
    half = length // 2
    idx = np.arange(length)
    order = np.concatenate([np.arange(half + 1), np.arange(1, half)])
    angle = 2.0 * math.pi * (np.outer(order, idx) % length) / length
    table = np.where((np.arange(length) <= half)[:, None], np.cos(angle), np.sin(angle))
    scale = np.where((order == 0) | (order == half), math.sqrt(1.0 / length), math.sqrt(2.0 / length))
    return (table * scale[:, None]).astype(np.float32), (order * order).astype(np.float32)


def dot(form, left, right):
    return jnp.einsum(form, left, right, precision=PRECISION)


def general(orbitals, occupations, ion_potential, hxc_potential):
    length = orbitals.shape[-1]
    planes = orbitals.shape[2]
    grid = lax.axis_size("grid")
    bands = lax.axis_size("band")
    cells = length * length
    columns = cells // grid
    share = cells // (grid * bands)
    kin = jnp.asarray(kinetic_matrix(length))
    kin_x = kin.reshape(length, grid, planes)
    basis_np, squares = real_basis(length)
    basis = jnp.asarray(basis_np)
    basis_x = basis.reshape(length, grid, planes)

    psi = orbitals[0]
    potential = ion_potential + hxc_potential

    def scatter(fields):
        parts = fields.reshape(fields.shape[0], planes, grid, columns).transpose(2, 1, 0, 3)
        return lax.all_to_all(parts, "grid", split_axis=0, concat_axis=0)

    def along_yz(field):
        return dot("cxyz,zk->cxyk", field, kin) + dot("cxyz,yk->cxkz", field, kin)

    moved = scatter(jnp.concatenate([psi, potential[None]], axis=0))
    local_kin = along_yz(psi) - psi
    applied = local_kin + potential * psi
    mixed = scatter(local_kin + applied)
    twice = along_yz(applied) - applied + potential * applied

    along = dot("ksp,spcn->ckn", kin_x, moved[:, :, :2])
    again = dot("ksp,spcn->ckn", kin_x, mixed) + dot("kx,cxn->ckn", kin, along)
    potential_cols = moved[:, :, 2].reshape(length, columns)
    again = again + potential_cols * along
    turned = jnp.stack([along[1], -along[0]])
    update = 2.0 * BESSEL_ONE * turned - 4.0 * BESSEL_TWO * again
    update = update.reshape(2, grid, planes, columns).transpose(1, 2, 0, 3)
    update = lax.all_to_all(update, "grid", split_axis=0, concat_axis=0)
    update = update.transpose(2, 1, 0, 3).reshape(psi.shape)

    turned = jnp.stack([applied[1], -applied[0]])
    fresh = (
        (BESSEL_ZERO + 2.0 * BESSEL_TWO) * psi
        + 2.0 * BESSEL_ONE * turned
        - 4.0 * BESSEL_TWO * twice
        + update
    )
    part = occupations[0] * (fresh[0] * fresh[0] + fresh[1] * fresh[1])
    density = lax.psum(part, "band")

    spectrum = dot("xyz,kz->xyk", part, basis)
    spectrum = dot("xyk,jy->xjk", spectrum, basis)
    spectrum = spectrum.reshape(planes, bands * grid, share).transpose(1, 0, 2)
    spectrum = lax.all_to_all(spectrum, ("band", "grid"), split_axis=0, concat_axis=0)
    spectrum = spectrum.reshape(bands, grid, planes, share).sum(axis=0)
    spectrum = dot("ksp,spn->kn", basis_x, spectrum)
    start = (lax.axis_index("band") * grid + lax.axis_index("grid")) * share
    cell = start + jnp.arange(share, dtype=jnp.int32)
    table = jnp.asarray(squares)
    total = table[:, None] + (table[cell // length] + table[cell % length])[None, :]
    kernel = jnp.where(total > 0, length * math.sqrt(length) / 16.0 / (total + 1.0), 0.0)
    spectrum = dot("kx,kn->xn", basis, kernel * spectrum)
    spectrum = spectrum.reshape(1, grid, planes, share)
    spectrum = jnp.broadcast_to(spectrum, (bands, grid, planes, share)).reshape(bands * grid, planes, share)
    spectrum = lax.all_to_all(spectrum, ("band", "grid"), split_axis=0, concat_axis=0)
    spectrum = spectrum.transpose(1, 0, 2).reshape(planes, length, length)
    spectrum = dot("xjk,jy->xyk", spectrum, basis)
    hartree = dot("xyk,kz->xyz", spectrum, basis)
    return (fresh[None], hartree - XC_FACTOR * jnp.cbrt(density))


LANES = 128


def product(left, right):
    return jnp.dot(left, right, precision=lax.Precision.HIGHEST, preferred_element_type=jnp.float32)


def split(array):
    high = array.astype(jnp.bfloat16)
    return high, (array - high.astype(jnp.float32)).astype(jnp.bfloat16)


def product_of_parts(left, right):
    total = jnp.dot(left[0], right[0], preferred_element_type=jnp.float32)
    total = total + jnp.dot(left[1], right[0], preferred_element_type=jnp.float32)
    return total + jnp.dot(left[0], right[1], preferred_element_type=jnp.float32)


def whole_tiles(rows):
    return -(-rows // 8) * 8


def chunk_rows(sizes):
    planes, _, rows, share = sizes
    return whole_tiles(planes * (2 * rows + share)), whole_tiles(planes * share)


def kinetic(plane, kin):
    plane = split(plane)
    return product_of_parts(plane, kin) + product_of_parts(kin, plane)


def pack(plane, packed):
    length = plane.shape[0]
    half = length // 2
    packed[:length, :] = plane[:, :LANES]
    packed[length:, :] = jnp.concatenate([plane[:half, LANES:], plane[half:, LANES:]], axis=1)


def unpack(packed, length):
    side = length - LANES
    tail = packed[length:, :]
    right = jnp.concatenate([tail[:, :side], tail[:, side:]], axis=0)
    return jnp.concatenate([packed[:length, :], right], axis=1)


def fill(out_ref, count, chunk, used):
    if used < chunk:

        @pl.when(pl.program_id(0) == 0)
        def _():
            for to in range(count):
                out_ref[pl.ds(to * chunk + used, chunk - used), :] = jnp.zeros((chunk - used, LANES), jnp.float32)


def pack_kernel(sizes, bunch, turns, place_ref, psi_ref, ion_ref, hxc_ref, *refs):
    planes, grid, rows, share = sizes
    *out_refs, packed = refs
    stride = 2 * rows + share
    band, mine = place_ref[0] // grid, place_ref[0] % grid
    for out_ref in out_refs:
        fill(out_ref, 1, chunk_rows(sizes)[0], planes * stride)
    for inner in range(bunch):
        first = (pl.program_id(0) * bunch + inner) * stride
        for part in range(2):
            slot = packed.at[inner * 3 + part]
            pack(psi_ref[0, part, inner], slot)
            for turn, out_ref in zip(turns, out_refs):
                start = (mine ^ turn) * rows
                out_ref[pl.ds(first + part * rows, rows), :] = slot[pl.ds(start, rows), :]
        slot = packed.at[inner * 3 + 2]
        pack(ion_ref[inner] + hxc_ref[inner], slot)
        for turn, out_ref in zip(turns, out_refs):
            start = (mine ^ turn) * rows + band * share
            out_ref[pl.ds(first + 2 * rows, share), :] = slot[pl.ds(start, share), :]


def plane_kernel(sizes, bunch, turns, place_ref, psi_ref, ion_ref, hxc_ref, kin_ref, *refs):
    planes, grid, rows, share = sizes
    *out_refs, base_ref, packed = refs
    mine = place_ref[0] % grid
    kin = split(kin_ref[...])
    for inner in range(bunch):
        plane = pl.program_id(0) * bunch + inner
        potential = ion_ref[inner] + hxc_ref[inner]
        applied = []
        for part in range(2):
            field = psi_ref[0, part, inner]
            bare = kinetic(field, kin) - field
            applied.append(bare + potential * field)
            slot = packed.at[inner * 2 + part]
            pack(bare + applied[part], slot)
            for turn, out_ref in zip(turns, out_refs):
                start = (mine ^ turn) * rows
                out_ref[pl.ds((plane * 2 + part) * rows, rows), :] = slot[pl.ds(start, rows), :]
        for part in range(2):
            twice = kinetic(applied[part], kin) + (potential - 1.0) * applied[part]
            turned = applied[1] if part == 0 else -applied[0]
            base_ref[part, inner] = (
                (BESSEL_ZERO + 2.0 * BESSEL_TWO) * psi_ref[0, part, inner]
                + 2.0 * BESSEL_ONE * turned
                - 4.0 * BESSEL_TWO * twice
            )


def share_kernel(sizes, turns, place_ref, *refs):
    planes, grid, rows, share = sizes
    *moved_refs, out_ref = refs
    length = planes * grid
    stride = 2 * rows + share
    for turn, moved_ref in zip(turns, moved_refs):
        first = (place_ref[0] % grid ^ turn) * planes
        for row in range(share):
            out_ref[pl.ds(row * length + first, planes), :] = moved_ref[pl.ds(2 * rows + row, planes, stride=stride), :]


def along_kernel(sizes, turns, place_ref, *refs):
    planes, grid, rows, share = sizes
    *moved_refs, kin_ref, out_ref, lines = refs
    stride = 2 * rows + share
    row = pl.program_id(0)
    for turn, moved_ref in zip(turns, moved_refs):
        first = (place_ref[0] % grid ^ turn) * planes
        for part in range(2):
            lines[part, pl.ds(first, planes), :] = moved_ref[pl.ds(part * rows + row, planes, stride=stride), :]
    out_ref[...] = product(kin_ref[...], jnp.concatenate([lines[0], lines[1]], axis=1))


def update_kernel(sizes, steps, turns, place_ref, along_ref, own_ref, other_ref, kin_ref, *refs):
    planes, grid, rows, share = sizes
    *mixed_refs, out_ref, lines = refs
    length = planes * grid
    kin = split(kin_ref[...])
    step = pl.program_id(0)
    mine_here = place_ref[0] // grid == step // (steps // 2)
    for inner in range(rows // steps):
        row = step * (rows // steps) + inner
        here = slice(inner * length, (inner + 1) * length)
        slot = lines.at[inner]
        for turn, mixed_ref in zip(turns, mixed_refs):
            first = (place_ref[0] % grid ^ turn) * planes
            for part in range(2):
                slot[part, pl.ds(first, planes), :] = mixed_ref[pl.ds(part * rows + row, planes, stride=2 * rows), :]
        along = along_ref[here, :]
        again = product_of_parts(kin, split(jnp.concatenate([slot[0], slot[1]], axis=1) + along))
        potential = jnp.where(mine_here, own_ref[here, :], other_ref[here, :])
        for part in range(2):
            mine = along[:, part * LANES : (part + 1) * LANES]
            turned = along[:, LANES:] if part == 0 else -along[:, :LANES]
            twice = again[:, part * LANES : (part + 1) * LANES] + potential * mine
            out_ref[pl.ds(part * rows + row, length, stride=2 * rows), :] = (
                2.0 * BESSEL_ONE * turned - 4.0 * BESSEL_TWO * twice
            )


def fresh_kernel(
    sizes, bunch, occ_ref, update_ref, base_ref, tables_ref, fresh_ref, upper_ref, lower_ref, out_ref, packed
):
    planes, grid, rows, share = sizes
    length = planes * grid
    chunk = chunk_rows(sizes)[1]
    cell_rows = rows * grid
    half = cell_rows // 2
    fill(out_ref, 2 * grid, chunk, planes * share)
    for inner in range(bunch):
        plane = pl.program_id(0) * bunch + inner
        part_sum = None
        for part in range(2):
            slot = packed.at[inner * 4 + part]
            for source in range(grid):
                start = ((source * planes + plane) * 2 + part) * rows
                slot[pl.ds(source * rows, rows), :] = update_ref[pl.ds(start, rows), :]
            fresh = base_ref[part, inner] + unpack(slot, length)
            fresh_ref[0, part, inner] = fresh
            part_sum = fresh * fresh if part_sum is None else part_sum + fresh * fresh
        part_sum = occ_ref[0] * part_sum
        slot = packed.at[inner * 4 + 2]
        pack(part_sum, slot)
        upper_ref[inner * half : (inner + 1) * half, :] = slot[:half, :]
        lower_ref[inner * half : (inner + 1) * half, :] = slot[half:, :]
        slot = packed.at[inner * 4 + 3]
        pack(product(product(tables_ref[0], part_sum), tables_ref[1]), slot)
        for to in range(2 * grid):
            out_ref[pl.ds(to * chunk + plane * share, share), :] = slot[pl.ds(to * share, share), :]


def filter_kernel(sizes, spec_ref, cells_ref, tables_ref, out_ref, lines):
    planes, grid, rows, share = sizes
    length = planes * grid
    chunk = chunk_rows(sizes)[1]

    def places():
        for source in range(grid):
            for row in range(share):
                first, second = (
                    pl.ds((band * grid + source) * chunk + row, planes, stride=share) for band in range(2)
                )
                here = (pl.ds(source * planes, planes), slice(row * LANES, (row + 1) * LANES))
                yield first, second, here

    for first, second, here in places():
        lines[here] = spec_ref[first, :] + spec_ref[second, :]
    index = lax.broadcasted_iota(jnp.int32, lines.shape, 0)
    order = jnp.where(index <= length // 2, index, index - length // 2).astype(jnp.float32)
    total = order * order + cells_ref[...]
    scale = length * math.sqrt(length) / 16.0
    kernel = jnp.where(total > 0.0, scale / (total + 1.0), 0.0)
    field = kernel * product(tables_ref[0], lines[...])
    lines[...] = product_of_parts(split(tables_ref[1]), split(field))
    for first, second, here in places():
        piece = lines[here]
        out_ref[first, :] = piece
        out_ref[second, :] = piece
    used = planes * share
    if used < chunk:
        for to in range(2 * grid):
            out_ref[pl.ds(to * chunk + used, chunk - used), :] = jnp.zeros((chunk - used, LANES), jnp.float32)


def last_kernel(
    sizes, bunch, spec_ref, upper_ref, lower_ref, upper_other, lower_other, tables_ref, out_ref, packed
):
    planes, grid, rows, share = sizes
    length = planes * grid
    half = rows * grid // 2
    chunk = chunk_rows(sizes)[1]
    turn, basis = split(tables_ref[1]), split(tables_ref[0])
    for inner in range(bunch):
        plane = pl.program_id(0) * bunch + inner
        slot = packed.at[inner * 2]
        for source in range(2 * grid):
            start = source * chunk + plane * share
            slot[pl.ds(source * share, share), :] = spec_ref[pl.ds(start, share), :]
        hartree = product_of_parts(turn, split(unpack(slot, length)))
        hartree = product_of_parts(split(hartree), basis)
        slot = packed.at[inner * 2 + 1]
        here = slice(inner * half, (inner + 1) * half)
        slot[:half, :] = upper_ref[here, :] + upper_other[here, :]
        slot[half:, :] = lower_ref[here, :] + lower_other[here, :]
        root = jnp.exp(jnp.log(unpack(slot, length)) * (1.0 / 3.0))
        out_ref[inner] = hartree - XC_FACTOR * root


def shape(*dims):
    return jax.ShapeDtypeStruct(dims, jnp.float32)


def whole(*dims):
    return pl.BlockSpec(dims, lambda *_: (0,) * len(dims))


SMALL = pltpu.CompilerParams(vmem_limit_bytes=24 << 20)
PARAMS = pltpu.CompilerParams(vmem_limit_bytes=54 << 20)


def cost(flops, moved):
    return pl.CostEstimate(flops=flops, bytes_accessed=moved, transcendentals=0)


def turn_orders(grid):
    half = grid // 2
    near, far = list(range(1, half)), list(range(half, grid))
    first, second = [], far[:3]
    for index in range(half):
        first += far[index : index + 1] + (near[index : index + 1] if index < half - 4 else [])
    first += near[half - 4 :]
    for index in range(3, half):
        second += near[index - 3 : index - 2] + far[index : index + 1]
    second = second[:-1] + near[half - 3 :] + second[-1:]
    return [0] + first, [0] + second


def packed_path(orbitals, occupations, ion_potential, hxc_potential):
    length = orbitals.shape[-1]
    planes = orbitals.shape[2]
    grid = lax.axis_size("grid")
    cell_rows = length * length // LANES
    rows = cell_rows // grid
    share = rows // 2
    sizes = (planes, grid, rows, share)
    field = planes * cell_rows
    work = 2 * planes * length**3
    place = lax.axis_index(("band", "grid")).astype(jnp.int32).reshape(1)
    kin = jnp.asarray(kinetic_matrix(length))
    basis_np, squares_np = real_basis(length)
    tables = jnp.asarray(np.stack([basis_np, basis_np.T]))
    smem = pl.BlockSpec(memory_space=pltpu.SMEM)
    vmem = pl.BlockSpec(memory_space=pltpu.VMEM)
    bunch = next(count for count in (3, 2, 1) if planes % count == 0)
    psi_spec = pl.BlockSpec((1, 2, bunch, length, length), lambda i: (0, 0, i, 0, 0))
    plane_spec = pl.BlockSpec((bunch, length, length), lambda i: (i, 0, 0))
    pair_spec = pl.BlockSpec((2, bunch, length, length), lambda i: (0, i, 0, 0))
    half_rows = pl.BlockSpec((bunch * cell_rows // 2, LANES), lambda i: (i, 0))
    square = whole(length, length)
    table_spec = whole(2, length, length)

    def scratch(count):
        return [pltpu.VMEM((count * bunch, cell_rows, LANES), jnp.float32)]

    def swap_pieces(turns, pieces):
        return [
            lax.ppermute(piece, "grid", [(place, place ^ turn) for place in range(grid)]) if turn else piece
            for turn, piece in zip(turns, pieces)
        ]

    def swap(array):
        flat = array.reshape(grid, -1, LANES)
        return lax.all_to_all(flat, "grid", split_axis=0, concat_axis=0).reshape(array.shape)

    def swap_all(array):
        flat = array.reshape(2 * grid, -1, LANES)
        return lax.all_to_all(flat, ("band", "grid"), split_axis=0, concat_axis=0).reshape(array.shape)

    first_turns, turns = turn_orders(grid)
    moved_rows, spec_rows = chunk_rows(sizes)
    spec_rows = 2 * grid * spec_rows
    mixed_rows = 2 * planes * rows
    steps = 6 if rows % 6 == 0 and share % (rows // 6) == 0 else 2
    moved = pl.pallas_call(
        functools.partial(pack_kernel, sizes, bunch, first_turns),
        grid=(planes // bunch,),
        in_specs=[smem, psi_spec, plane_spec, plane_spec],
        out_specs=[whole(moved_rows, LANES)] * grid,
        out_shape=[shape(moved_rows, LANES)] * grid,
        scratch_shapes=scratch(3),
        compiler_params=PARAMS,
        cost_estimate=cost(0, 15 << 20),
    )(place, orbitals, ion_potential, hxc_potential)
    *mixed, base = pl.pallas_call(
        functools.partial(plane_kernel, sizes, bunch, turns),
        grid=(planes // bunch,),
        in_specs=[smem, psi_spec, plane_spec, plane_spec, square],
        out_specs=[whole(mixed_rows, LANES)] * grid + [pair_spec],
        out_shape=[shape(mixed_rows, LANES)] * grid + [shape(2, planes, length, length)],
        scratch_shapes=scratch(2),
        compiler_params=PARAMS,
        cost_estimate=cost(8 * 3 * work, 20 << 20),
    )(place, orbitals, ion_potential, hxc_potential, kin)
    late = range(6, grid)
    held = lax.optimization_barrier(([moved[k] for k in late], base))
    base = held[1]
    moved = list(moved)
    for k, piece in zip(late, held[0]):
        moved[k] = piece
    moved = swap_pieces(first_turns, moved)

    own = pl.pallas_call(
        functools.partial(share_kernel, sizes, first_turns),
        in_specs=[smem] + [vmem] * grid,
        out_specs=vmem,
        out_shape=shape(share * length, LANES),
        compiler_params=PARAMS,
        cost_estimate=cost(0, 6 << 20),
    )(place, *moved)
    other = lax.ppermute(own, "band", [(0, 1), (1, 0)])
    along = pl.pallas_call(
        functools.partial(along_kernel, sizes, first_turns),
        grid=(rows,),
        in_specs=[smem] + [whole(moved_rows, LANES)] * grid + [square],
        out_specs=pl.BlockSpec((length, 2 * LANES), lambda i: (i, 0)),
        out_shape=shape(rows * length, 2 * LANES),
        scratch_shapes=[pltpu.VMEM((2, length, LANES), jnp.float32)],
        compiler_params=PARAMS,
        cost_estimate=cost(2 * 6 * work, 10 << 20),
    )(place, *moved, kin)
    late = range(5, grid)
    held = lax.optimization_barrier(([mixed[k] for k in late], along))
    along = held[1]
    for k, piece in zip(late, held[0]):
        mixed[k] = piece
    mixed = swap_pieces(turns, mixed)
    half_spec = pl.BlockSpec((rows // steps * length, LANES), lambda i: (i % (steps // 2), 0))
    update = pl.pallas_call(
        functools.partial(update_kernel, sizes, steps, turns),
        grid=(steps,),
        in_specs=[
            smem,
            pl.BlockSpec((rows // steps * length, 2 * LANES), lambda i: (i, 0)),
            half_spec,
            half_spec,
            square,
        ]
        + [whole(mixed_rows, LANES)] * grid,
        out_specs=whole(2 * field, LANES),
        out_shape=shape(2 * field, LANES),
        scratch_shapes=[pltpu.VMEM((rows // steps, 2, length, LANES), jnp.float32)],
        compiler_params=PARAMS,
        cost_estimate=cost(2 * 3 * work, 14 << 20),
    )(place, along, own, other, kin, *mixed)
    update = swap(update)

    fresh, upper, lower, spectrum = pl.pallas_call(
        functools.partial(fresh_kernel, sizes, bunch),
        grid=(planes // bunch,),
        in_specs=[smem, vmem, pair_spec, table_spec],
        out_specs=[
            psi_spec,
            half_rows,
            half_rows,
            whole(spec_rows, LANES),
        ],
        out_shape=[
            shape(*orbitals.shape),
            shape(field // 2, LANES),
            shape(field // 2, LANES),
            shape(spec_rows, LANES),
        ],
        scratch_shapes=scratch(4),
        compiler_params=SMALL,
        cost_estimate=cost(2 * 6 * work, 16 << 20),
    )(occupations, update, base, tables)
    upper_other = lax.ppermute(upper, "band", [(0, 1), (1, 0)])
    lower_other = lax.ppermute(lower, "band", [(0, 1), (1, 0)])

    spectrum = swap_all(spectrum)
    cells_np = squares_np[:, None] + squares_np[None, :]
    half = length // 2
    cells_np = np.concatenate(
        [cells_np[:, :LANES], np.concatenate([cells_np[:half, LANES:], cells_np[half:, LANES:]], axis=1)]
    )
    device = lax.axis_index("band") * grid + lax.axis_index("grid")
    cells = lax.dynamic_slice_in_dim(jnp.asarray(cells_np), device * share, share, axis=0)
    spectrum = pl.pallas_call(
        functools.partial(filter_kernel, sizes),
        in_specs=[vmem] * 3,
        out_specs=vmem,
        out_shape=shape(spec_rows, LANES),
        scratch_shapes=[pltpu.VMEM((length, share * LANES), jnp.float32)],
        compiler_params=SMALL,
        cost_estimate=cost(6 * work, 5 << 20),
    )(spectrum, cells.reshape(1, share * LANES), tables)
    spectrum, upper_other = lax.optimization_barrier((spectrum, upper_other))
    spectrum = swap_all(spectrum)
    potential = pl.pallas_call(
        functools.partial(last_kernel, sizes, bunch),
        grid=(planes // bunch,),
        in_specs=[
            vmem,
            half_rows,
            half_rows,
            half_rows,
            half_rows,
            table_spec,
        ],
        out_specs=plane_spec,
        out_shape=shape(planes, length, length),
        scratch_shapes=scratch(2),
        compiler_params=PARAMS,
        cost_estimate=cost(2 * 6 * work, 6 << 20),
    )(spectrum, upper, lower, upper_other, lower_other, tables)
    return (fresh, potential)


def local(orbitals, occupations, ion_potential, hxc_potential):
    length = orbitals.shape[-1]
    parts = 2 * lax.axis_size("grid") * LANES
    fits = lax.axis_size("grid") & (lax.axis_size("grid") - 1) == 0
    fits = fits and length == LANES + LANES // 2 and lax.axis_size("band") == 2 and length * length % parts == 0
    path = packed_path if fits else general
    return path(orbitals, occupations, ion_potential, hxc_potential)


def solution(mesh):
    placed = (
        P("band", None, "grid", None, None),
        P("band"),
        P("grid", None, None),
        P("grid", None, None),
    )
    return jax.shard_map(
        local,
        mesh=mesh,
        in_specs=placed,
        out_specs=(P("band", None, "grid", None, None), P("grid", None, None)),
        check_vma=False,
    )
```

```python
import functools
import math

import jax
import jax.numpy as jnp
import numpy as np
from jax import lax
from jax.experimental import pallas as pl
from jax.experimental.pallas import tpu as pltpu
from jax.sharding import PartitionSpec as P

BESSEL_ZERO = 0.8462873527504802
BESSEL_ONE = 0.36884204609417703
BESSEL_TWO = 0.07581776248
XC_FACTOR = 0.98474502
PRECISION = lax.Precision.HIGH


def kinetic_matrix(length):
    idx = np.arange(length)
    freq = np.where(idx < length // 2, idx, idx - length).astype(np.float64)
    wave = np.cos(2.0 * math.pi * (np.outer(idx, idx) % length) / length)
    row = (wave @ (freq * freq)) / length * (2.0 / (3.0 * (length / 2) ** 2))
    return row[(idx[:, None] - idx[None, :]) % length].astype(np.float32)


def real_basis(length):
    half = length // 2
    idx = np.arange(length)
    order = np.concatenate([np.arange(half + 1), np.arange(1, half)])
    angle = 2.0 * math.pi * (np.outer(order, idx) % length) / length
    table = np.where((np.arange(length) <= half)[:, None], np.cos(angle), np.sin(angle))
    scale = np.where((order == 0) | (order == half), math.sqrt(1.0 / length), math.sqrt(2.0 / length))
    return (table * scale[:, None]).astype(np.float32), (order * order).astype(np.float32)


def dot(form, left, right):
    return jnp.einsum(form, left, right, precision=PRECISION)


def general(orbitals, occupations, ion_potential, hxc_potential):
    length = orbitals.shape[-1]
    planes = orbitals.shape[2]
    grid = lax.axis_size("grid")
    bands = lax.axis_size("band")
    cells = length * length
    columns = cells // grid
    share = cells // (grid * bands)
    kin = jnp.asarray(kinetic_matrix(length))
    kin_x = kin.reshape(length, grid, planes)
    basis_np, squares = real_basis(length)
    basis = jnp.asarray(basis_np)
    basis_x = basis.reshape(length, grid, planes)

    psi = orbitals[0]
    potential = ion_potential + hxc_potential

    def scatter(fields):
        parts = fields.reshape(fields.shape[0], planes, grid, columns).transpose(2, 1, 0, 3)
        return lax.all_to_all(parts, "grid", split_axis=0, concat_axis=0)

    def along_yz(field):
        return dot("cxyz,zk->cxyk", field, kin) + dot("cxyz,yk->cxkz", field, kin)

    moved = scatter(jnp.concatenate([psi, potential[None]], axis=0))
    local_kin = along_yz(psi) - psi
    applied = local_kin + potential * psi
    mixed = scatter(local_kin + applied)
    twice = along_yz(applied) - applied + potential * applied

    along = dot("ksp,spcn->ckn", kin_x, moved[:, :, :2])
    again = dot("ksp,spcn->ckn", kin_x, mixed) + dot("kx,cxn->ckn", kin, along)
    potential_cols = moved[:, :, 2].reshape(length, columns)
    again = again + potential_cols * along
    turned = jnp.stack([along[1], -along[0]])
    update = 2.0 * BESSEL_ONE * turned - 4.0 * BESSEL_TWO * again
    update = update.reshape(2, grid, planes, columns).transpose(1, 2, 0, 3)
    update = lax.all_to_all(update, "grid", split_axis=0, concat_axis=0)
    update = update.transpose(2, 1, 0, 3).reshape(psi.shape)

    turned = jnp.stack([applied[1], -applied[0]])
    fresh = (
        (BESSEL_ZERO + 2.0 * BESSEL_TWO) * psi
        + 2.0 * BESSEL_ONE * turned
        - 4.0 * BESSEL_TWO * twice
        + update
    )
    part = occupations[0] * (fresh[0] * fresh[0] + fresh[1] * fresh[1])
    density = lax.psum(part, "band")

    spectrum = dot("xyz,kz->xyk", part, basis)
    spectrum = dot("xyk,jy->xjk", spectrum, basis)
    spectrum = spectrum.reshape(planes, bands * grid, share).transpose(1, 0, 2)
    spectrum = lax.all_to_all(spectrum, ("band", "grid"), split_axis=0, concat_axis=0)
    spectrum = spectrum.reshape(bands, grid, planes, share).sum(axis=0)
    spectrum = dot("ksp,spn->kn", basis_x, spectrum)
    start = (lax.axis_index("band") * grid + lax.axis_index("grid")) * share
    cell = start + jnp.arange(share, dtype=jnp.int32)
    table = jnp.asarray(squares)
    total = table[:, None] + (table[cell // length] + table[cell % length])[None, :]
    kernel = jnp.where(total > 0, length * math.sqrt(length) / 16.0 / (total + 1.0), 0.0)
    spectrum = dot("kx,kn->xn", basis, kernel * spectrum)
    spectrum = spectrum.reshape(1, grid, planes, share)
    spectrum = jnp.broadcast_to(spectrum, (bands, grid, planes, share)).reshape(bands * grid, planes, share)
    spectrum = lax.all_to_all(spectrum, ("band", "grid"), split_axis=0, concat_axis=0)
    spectrum = spectrum.transpose(1, 0, 2).reshape(planes, length, length)
    spectrum = dot("xjk,jy->xyk", spectrum, basis)
    hartree = dot("xyk,kz->xyz", spectrum, basis)
    return (fresh[None], hartree - XC_FACTOR * jnp.cbrt(density))


LANES = 128


def product(left, right):
    return jnp.dot(left, right, precision=lax.Precision.HIGHEST, preferred_element_type=jnp.float32)


def split(array):
    high = array.astype(jnp.bfloat16)
    return high, (array - high.astype(jnp.float32)).astype(jnp.bfloat16)


def product_of_parts(left, right):
    total = jnp.dot(left[0], right[0], preferred_element_type=jnp.float32)
    total = total + jnp.dot(left[1], right[0], preferred_element_type=jnp.float32)
    return total + jnp.dot(left[0], right[1], preferred_element_type=jnp.float32)


def whole_tiles(rows):
    return -(-rows // 8) * 8


def chunk_rows(sizes):
    planes, _, rows, share = sizes
    return whole_tiles(planes * (2 * rows + share)), whole_tiles(planes * share)


def kinetic(plane, kin):
    plane = split(plane)
    return product_of_parts(plane, kin) + product_of_parts(kin, plane)


def pack(plane, packed):
    length = plane.shape[0]
    half = length // 2
    packed[:length, :] = plane[:, :LANES]
    packed[length:, :] = jnp.concatenate([plane[:half, LANES:], plane[half:, LANES:]], axis=1)


def unpack(packed, length):
    side = length - LANES
    tail = packed[length:, :]
    right = jnp.concatenate([tail[:, :side], tail[:, side:]], axis=0)
    return jnp.concatenate([packed[:length, :], right], axis=1)


def fill(out_ref, count, chunk, used):
    if used < chunk:

        @pl.when(pl.program_id(0) == 0)
        def _():
            for to in range(count):
                out_ref[pl.ds(to * chunk + used, chunk - used), :] = jnp.zeros((chunk - used, LANES), jnp.float32)


def pack_kernel(sizes, bunch, turns, place_ref, psi_ref, ion_ref, hxc_ref, *refs):
    planes, grid, rows, share = sizes
    *out_refs, packed = refs
    stride = 2 * rows + share
    band, mine = place_ref[0] // grid, place_ref[0] % grid
    for out_ref in out_refs:
        fill(out_ref, 1, chunk_rows(sizes)[0], planes * stride)
    for inner in range(bunch):
        first = (pl.program_id(0) * bunch + inner) * stride
        for part in range(2):
            slot = packed.at[inner * 3 + part]
            pack(psi_ref[0, part, inner], slot)
            for turn, out_ref in zip(turns, out_refs):
                start = (mine ^ turn) * rows
                out_ref[pl.ds(first + part * rows, rows), :] = slot[pl.ds(start, rows), :]
        slot = packed.at[inner * 3 + 2]
        pack(ion_ref[inner] + hxc_ref[inner], slot)
        for turn, out_ref in zip(turns, out_refs):
            start = (mine ^ turn) * rows + band * share
            out_ref[pl.ds(first + 2 * rows, share), :] = slot[pl.ds(start, share), :]


def plane_kernel(sizes, bunch, turns, place_ref, psi_ref, ion_ref, hxc_ref, kin_ref, *refs):
    planes, grid, rows, share = sizes
    *out_refs, base_ref, packed = refs
    mine = place_ref[0] % grid
    kin = split(kin_ref[...])
    for inner in range(bunch):
        plane = pl.program_id(0) * bunch + inner
        potential = ion_ref[inner] + hxc_ref[inner]
        applied = []
        for part in range(2):
            field = psi_ref[0, part, inner]
            bare = kinetic(field, kin) - field
            applied.append(bare + potential * field)
            slot = packed.at[inner * 2 + part]
            pack(bare + applied[part], slot)
            for turn, out_ref in zip(turns, out_refs):
                start = (mine ^ turn) * rows
                out_ref[pl.ds((plane * 2 + part) * rows, rows), :] = slot[pl.ds(start, rows), :]
        for part in range(2):
            twice = kinetic(applied[part], kin) + (potential - 1.0) * applied[part]
            turned = applied[1] if part == 0 else -applied[0]
            base_ref[part, inner] = (
                (BESSEL_ZERO + 2.0 * BESSEL_TWO) * psi_ref[0, part, inner]
                + 2.0 * BESSEL_ONE * turned
                - 4.0 * BESSEL_TWO * twice
            )


def share_kernel(sizes, turns, place_ref, *refs):
    planes, grid, rows, share = sizes
    *moved_refs, out_ref = refs
    length = planes * grid
    stride = 2 * rows + share
    for turn, moved_ref in zip(turns, moved_refs):
        first = (place_ref[0] % grid ^ turn) * planes
        for row in range(share):
            out_ref[pl.ds(row * length + first, planes), :] = moved_ref[pl.ds(2 * rows + row, planes, stride=stride), :]


def along_kernel(sizes, turns, place_ref, *refs):
    planes, grid, rows, share = sizes
    *moved_refs, kin_ref, out_ref, lines = refs
    stride = 2 * rows + share
    row = pl.program_id(0)
    for turn, moved_ref in zip(turns, moved_refs):
        first = (place_ref[0] % grid ^ turn) * planes
        for part in range(2):
            lines[part, pl.ds(first, planes), :] = moved_ref[pl.ds(part * rows + row, planes, stride=stride), :]
    out_ref[...] = product(kin_ref[...], jnp.concatenate([lines[0], lines[1]], axis=1))


def update_kernel(sizes, steps, turns, place_ref, along_ref, own_ref, other_ref, kin_ref, *refs):
    planes, grid, rows, share = sizes
    *mixed_refs, out_ref, lines = refs
    length = planes * grid
    kin = split(kin_ref[...])
    step = pl.program_id(0)
    mine_here = place_ref[0] // grid == step // (steps // 2)
    for inner in range(rows // steps):
        row = step * (rows // steps) + inner
        here = slice(inner * length, (inner + 1) * length)
        slot = lines.at[inner]
        for turn, mixed_ref in zip(turns, mixed_refs):
            first = (place_ref[0] % grid ^ turn) * planes
            for part in range(2):
                slot[part, pl.ds(first, planes), :] = mixed_ref[pl.ds(part * rows + row, planes, stride=2 * rows), :]
        along = along_ref[here, :]
        again = product_of_parts(kin, split(jnp.concatenate([slot[0], slot[1]], axis=1) + along))
        potential = jnp.where(mine_here, own_ref[here, :], other_ref[here, :])
        for part in range(2):
            mine = along[:, part * LANES : (part + 1) * LANES]
            turned = along[:, LANES:] if part == 0 else -along[:, :LANES]
            twice = again[:, part * LANES : (part + 1) * LANES] + potential * mine
            out_ref[pl.ds(part * rows + row, length, stride=2 * rows), :] = (
                2.0 * BESSEL_ONE * turned - 4.0 * BESSEL_TWO * twice
            )


def fresh_kernel(
    sizes, bunch, occ_ref, update_ref, base_ref, tables_ref, fresh_ref, upper_ref, lower_ref, out_ref, packed
):
    planes, grid, rows, share = sizes
    length = planes * grid
    chunk = chunk_rows(sizes)[1]
    cell_rows = rows * grid
    half = cell_rows // 2
    fill(out_ref, 2 * grid, chunk, planes * share)
    means, parts = [], []
    for inner in range(bunch):
        plane = pl.program_id(0) * bunch + inner
        part_sum = None
        for part in range(2):
            slot = packed.at[inner * 4 + part]
            for source in range(grid):
                start = ((source * planes + plane) * 2 + part) * rows
                slot[pl.ds(source * rows, rows), :] = update_ref[pl.ds(start, rows), :]
            fresh = base_ref[part, inner] + unpack(slot, length)
            fresh_ref[0, part, inner] = fresh
            part_sum = fresh * fresh if part_sum is None else part_sum + fresh * fresh
        part_sum = occ_ref[0] * part_sum
        slot = packed.at[inner * 4 + 2]
        pack(part_sum, slot)
        upper_ref[inner * half : (inner + 1) * half, :] = slot[:half, :]
        lower_ref[inner * half : (inner + 1) * half, :] = slot[half:, :]
        means.append(jnp.sum(part_sum) * (1.0 / length**2))
        parts.append(part_sum - means[inner])
    basis, turn = split(tables_ref[0]), split(tables_ref[1])
    along_z = product_of_parts(split(jnp.concatenate(parts, axis=0)), turn)
    first = (lax.broadcasted_iota(jnp.int32, (length, length), axis) == 0 for axis in range(2))
    first = jnp.logical_and(*first)
    for inner in range(bunch):
        plane = pl.program_id(0) * bunch + inner
        spectrum = product_of_parts(basis, split(along_z[inner * length : (inner + 1) * length, :]))
        slot = packed.at[inner * 4 + 3]
        pack(spectrum + jnp.where(first, means[inner] * length, 0.0), slot)
        for to in range(2 * grid):
            out_ref[pl.ds(to * chunk + plane * share, share), :] = slot[pl.ds(to * share, share), :]


def filter_kernel(sizes, spec_ref, cells_ref, tables_ref, out_ref, lines):
    planes, grid, rows, share = sizes
    length = planes * grid
    chunk = chunk_rows(sizes)[1]

    def places():
        for source in range(grid):
            for row in range(share):
                first, second = (
                    pl.ds((band * grid + source) * chunk + row, planes, stride=share) for band in range(2)
                )
                here = (pl.ds(source * planes, planes), slice(row * LANES, (row + 1) * LANES))
                yield first, second, here

    for first, second, here in places():
        lines[here] = spec_ref[first, :] + spec_ref[second, :]
    index = lax.broadcasted_iota(jnp.int32, lines.shape, 0)
    order = jnp.where(index <= length // 2, index, index - length // 2).astype(jnp.float32)
    total = order * order + cells_ref[...]
    scale = length * math.sqrt(length) / 16.0
    kernel = jnp.where(total > 0.0, scale / (total + 1.0), 0.0)
    field = kernel * product(tables_ref[0], lines[...])
    lines[...] = product_of_parts(split(tables_ref[1]), split(field))
    for first, second, here in places():
        piece = lines[here]
        out_ref[first, :] = piece
        out_ref[second, :] = piece
    used = planes * share
    if used < chunk:
        for to in range(2 * grid):
            out_ref[pl.ds(to * chunk + used, chunk - used), :] = jnp.zeros((chunk - used, LANES), jnp.float32)


def last_kernel(
    sizes, bunch, spec_ref, upper_ref, lower_ref, upper_other, lower_other, tables_ref, out_ref, packed
):
    planes, grid, rows, share = sizes
    length = planes * grid
    half = rows * grid // 2
    chunk = chunk_rows(sizes)[1]
    turn, basis = split(tables_ref[1]), split(tables_ref[0])
    lines = []
    for inner in range(bunch):
        plane = pl.program_id(0) * bunch + inner
        slot = packed.at[inner * 2]
        for source in range(2 * grid):
            start = source * chunk + plane * share
            slot[pl.ds(source * share, share), :] = spec_ref[pl.ds(start, share), :]
        lines.append(product_of_parts(turn, split(unpack(slot, length))))
    hartree = product_of_parts(split(jnp.concatenate(lines, axis=0)), basis)
    for inner in range(bunch):
        slot = packed.at[inner * 2 + 1]
        here = slice(inner * half, (inner + 1) * half)
        slot[:half, :] = upper_ref[here, :] + upper_other[here, :]
        slot[half:, :] = lower_ref[here, :] + lower_other[here, :]
        root = jnp.exp(jnp.log(unpack(slot, length)) * (1.0 / 3.0))
        out_ref[inner] = hartree[inner * length : (inner + 1) * length, :] - XC_FACTOR * root


def shape(*dims):
    return jax.ShapeDtypeStruct(dims, jnp.float32)


def whole(*dims):
    return pl.BlockSpec(dims, lambda *_: (0,) * len(dims))


SMALL = pltpu.CompilerParams(vmem_limit_bytes=24 << 20)
PARAMS = pltpu.CompilerParams(vmem_limit_bytes=54 << 20)


def cost(flops, moved):
    return pl.CostEstimate(flops=flops, bytes_accessed=moved, transcendentals=0)


def turn_orders(grid):
    half = grid // 2
    near, far = list(range(1, half)), list(range(half, grid))
    first, second = [], far[:3]
    for index in range(half):
        first += far[index : index + 1] + (near[index : index + 1] if index < half - 4 else [])
    first += near[half - 4 :]
    for index in range(3, half):
        second += near[index - 3 : index - 2] + far[index : index + 1]
    second += near[half - 3 :]
    return [0] + first, [0] + second


def packed_path(orbitals, occupations, ion_potential, hxc_potential):
    length = orbitals.shape[-1]
    planes = orbitals.shape[2]
    grid = lax.axis_size("grid")
    cell_rows = length * length // LANES
    rows = cell_rows // grid
    share = rows // 2
    sizes = (planes, grid, rows, share)
    field = planes * cell_rows
    work = 2 * planes * length**3
    place = lax.axis_index(("band", "grid")).astype(jnp.int32).reshape(1)
    kin = jnp.asarray(kinetic_matrix(length))
    basis_np, squares_np = real_basis(length)
    tables = jnp.asarray(np.stack([basis_np, basis_np.T]))
    smem = pl.BlockSpec(memory_space=pltpu.SMEM)
    vmem = pl.BlockSpec(memory_space=pltpu.VMEM)
    bunch = next(count for count in (3, 2, 1) if planes % count == 0)
    psi_spec = pl.BlockSpec((1, 2, bunch, length, length), lambda i: (0, 0, i, 0, 0))
    plane_spec = pl.BlockSpec((bunch, length, length), lambda i: (i, 0, 0))
    pair_spec = pl.BlockSpec((2, bunch, length, length), lambda i: (0, i, 0, 0))
    half_rows = pl.BlockSpec((bunch * cell_rows // 2, LANES), lambda i: (i, 0))
    square = whole(length, length)
    table_spec = whole(2, length, length)

    def scratch(count):
        return [pltpu.VMEM((count * bunch, cell_rows, LANES), jnp.float32)]

    def swap_pieces(turns, pieces):
        return [
            lax.ppermute(piece, "grid", [(place, place ^ turn) for place in range(grid)]) if turn else piece
            for turn, piece in zip(turns, pieces)
        ]

    def swap(array):
        flat = array.reshape(grid, -1, LANES)
        return lax.all_to_all(flat, "grid", split_axis=0, concat_axis=0).reshape(array.shape)

    def swap_all(array):
        flat = array.reshape(2 * grid, -1, LANES)
        return lax.all_to_all(flat, ("band", "grid"), split_axis=0, concat_axis=0).reshape(array.shape)

    first_turns, turns = turn_orders(grid)
    moved_rows, spec_rows = chunk_rows(sizes)
    spec_rows = 2 * grid * spec_rows
    mixed_rows = 2 * planes * rows
    steps = 6 if rows % 6 == 0 and share % (rows // 6) == 0 else 2
    moved = pl.pallas_call(
        functools.partial(pack_kernel, sizes, bunch, first_turns),
        grid=(planes // bunch,),
        in_specs=[smem, psi_spec, plane_spec, plane_spec],
        out_specs=[whole(moved_rows, LANES)] * grid,
        out_shape=[shape(moved_rows, LANES)] * grid,
        scratch_shapes=scratch(3),
        compiler_params=PARAMS,
        cost_estimate=cost(0, 15 << 20),
    )(place, orbitals, ion_potential, hxc_potential)
    *mixed, base = pl.pallas_call(
        functools.partial(plane_kernel, sizes, bunch, turns),
        grid=(planes // bunch,),
        in_specs=[smem, psi_spec, plane_spec, plane_spec, square],
        out_specs=[whole(mixed_rows, LANES)] * grid + [pair_spec],
        out_shape=[shape(mixed_rows, LANES)] * grid + [shape(2, planes, length, length)],
        scratch_shapes=scratch(2),
        compiler_params=PARAMS,
        cost_estimate=cost(8 * 3 * work, 20 << 20),
    )(place, orbitals, ion_potential, hxc_potential, kin)
    late = range(6, grid)
    held = lax.optimization_barrier(([moved[k] for k in late], base))
    base = held[1]
    moved = list(moved)
    for k, piece in zip(late, held[0]):
        moved[k] = piece
    moved = swap_pieces(first_turns, moved)

    own = pl.pallas_call(
        functools.partial(share_kernel, sizes, first_turns),
        in_specs=[smem] + [vmem] * grid,
        out_specs=vmem,
        out_shape=shape(share * length, LANES),
        compiler_params=PARAMS,
        cost_estimate=cost(0, 6 << 20),
    )(place, *moved)
    other = lax.ppermute(own, "band", [(0, 1), (1, 0)])
    along = pl.pallas_call(
        functools.partial(along_kernel, sizes, first_turns),
        grid=(rows,),
        in_specs=[smem] + [whole(moved_rows, LANES)] * grid + [square],
        out_specs=pl.BlockSpec((length, 2 * LANES), lambda i: (i, 0)),
        out_shape=shape(rows * length, 2 * LANES),
        scratch_shapes=[pltpu.VMEM((2, length, LANES), jnp.float32)],
        compiler_params=PARAMS,
        cost_estimate=cost(2 * 6 * work, 10 << 20),
    )(place, *moved, kin)
    mixed = swap_pieces(turns, mixed)
    half_spec = pl.BlockSpec((rows // steps * length, LANES), lambda i: (i % (steps // 2), 0))
    update = pl.pallas_call(
        functools.partial(update_kernel, sizes, steps, turns),
        grid=(steps,),
        in_specs=[
            smem,
            pl.BlockSpec((rows // steps * length, 2 * LANES), lambda i: (i, 0)),
            half_spec,
            half_spec,
            square,
        ]
        + [whole(mixed_rows, LANES)] * grid,
        out_specs=whole(2 * field, LANES),
        out_shape=shape(2 * field, LANES),
        scratch_shapes=[pltpu.VMEM((rows // steps, 2, length, LANES), jnp.float32)],
        compiler_params=PARAMS,
        cost_estimate=cost(2 * 3 * work, 14 << 20),
    )(place, along, own, other, kin, *mixed)
    update = swap(update)

    fresh, upper, lower, spectrum = pl.pallas_call(
        functools.partial(fresh_kernel, sizes, bunch),
        grid=(planes // bunch,),
        in_specs=[smem, vmem, pair_spec, table_spec],
        out_specs=[
            psi_spec,
            half_rows,
            half_rows,
            whole(spec_rows, LANES),
        ],
        out_shape=[
            shape(*orbitals.shape),
            shape(field // 2, LANES),
            shape(field // 2, LANES),
            shape(spec_rows, LANES),
        ],
        scratch_shapes=scratch(4),
        compiler_params=PARAMS,
        cost_estimate=cost(2 * 6 * work, 16 << 20),
    )(occupations, update, base, tables)
    upper_other = lax.ppermute(upper, "band", [(0, 1), (1, 0)])
    lower_other = lax.ppermute(lower, "band", [(0, 1), (1, 0)])

    spectrum = swap_all(spectrum)
    cells_np = squares_np[:, None] + squares_np[None, :]
    half = length // 2
    cells_np = np.concatenate(
        [cells_np[:, :LANES], np.concatenate([cells_np[:half, LANES:], cells_np[half:, LANES:]], axis=1)]
    )
    device = lax.axis_index("band") * grid + lax.axis_index("grid")
    cells = lax.dynamic_slice_in_dim(jnp.asarray(cells_np), device * share, share, axis=0)
    spectrum = pl.pallas_call(
        functools.partial(filter_kernel, sizes),
        in_specs=[vmem] * 3,
        out_specs=vmem,
        out_shape=shape(spec_rows, LANES),
        scratch_shapes=[pltpu.VMEM((length, share * LANES), jnp.float32)],
        compiler_params=SMALL,
        cost_estimate=cost(6 * work, 5 << 20),
    )(spectrum, cells.reshape(1, share * LANES), tables)
    spectrum, upper_other = lax.optimization_barrier((spectrum, upper_other))
    spectrum = swap_all(spectrum)
    potential = pl.pallas_call(
        functools.partial(last_kernel, sizes, bunch),
        grid=(planes // bunch,),
        in_specs=[
            vmem,
            half_rows,
            half_rows,
            half_rows,
            half_rows,
            table_spec,
        ],
        out_specs=plane_spec,
        out_shape=shape(planes, length, length),
        scratch_shapes=scratch(2),
        compiler_params=PARAMS,
        cost_estimate=cost(2 * 6 * work, 6 << 20),
    )(spectrum, upper, lower, upper_other, lower_other, tables)
    return (fresh, potential)


def local(orbitals, occupations, ion_potential, hxc_potential):
    length = orbitals.shape[-1]
    parts = 2 * lax.axis_size("grid") * LANES
    fits = lax.axis_size("grid") & (lax.axis_size("grid") - 1) == 0
    fits = fits and length == LANES + LANES // 2 and lax.axis_size("band") == 2 and length * length % parts == 0
    path = packed_path if fits else general
    return path(orbitals, occupations, ion_potential, hxc_potential)


def solution(mesh):
    placed = (
        P("band", None, "grid", None, None),
        P("band"),
        P("grid", None, None),
        P("grid", None, None),
    )
    return jax.shard_map(
        local,
        mesh=mesh,
        in_specs=placed,
        out_specs=(P("band", None, "grid", None, None), P("grid", None, None)),
        check_vma=False,
    )
```

```python
import functools
import math

import jax
import jax.numpy as jnp
import numpy as np
from jax import lax
from jax.experimental import pallas as pl
from jax.experimental.pallas import tpu as pltpu
from jax.sharding import PartitionSpec as P

BESSEL_ZERO = 0.8462873527504802
BESSEL_ONE = 0.36884204609417703
BESSEL_TWO = 0.07581776248
XC_FACTOR = 0.98474502
PRECISION = lax.Precision.HIGH


def kinetic_matrix(length):
    idx = np.arange(length)
    freq = np.where(idx < length // 2, idx, idx - length).astype(np.float64)
    wave = np.cos(2.0 * math.pi * (np.outer(idx, idx) % length) / length)
    row = (wave @ (freq * freq)) / length * (2.0 / (3.0 * (length / 2) ** 2))
    return row[(idx[:, None] - idx[None, :]) % length].astype(np.float32)


def real_basis(length):
    half = length // 2
    idx = np.arange(length)
    order = np.concatenate([np.arange(half + 1), np.arange(1, half)])
    angle = 2.0 * math.pi * (np.outer(order, idx) % length) / length
    table = np.where((np.arange(length) <= half)[:, None], np.cos(angle), np.sin(angle))
    scale = np.where((order == 0) | (order == half), math.sqrt(1.0 / length), math.sqrt(2.0 / length))
    return (table * scale[:, None]).astype(np.float32), (order * order).astype(np.float32)


def dot(form, left, right):
    return jnp.einsum(form, left, right, precision=PRECISION)


def general(orbitals, occupations, ion_potential, hxc_potential):
    length = orbitals.shape[-1]
    planes = orbitals.shape[2]
    grid = lax.axis_size("grid")
    bands = lax.axis_size("band")
    cells = length * length
    columns = cells // grid
    share = cells // (grid * bands)
    kin = jnp.asarray(kinetic_matrix(length))
    kin_x = kin.reshape(length, grid, planes)
    basis_np, squares = real_basis(length)
    basis = jnp.asarray(basis_np)
    basis_x = basis.reshape(length, grid, planes)

    psi = orbitals[0]
    potential = ion_potential + hxc_potential

    def scatter(fields):
        parts = fields.reshape(fields.shape[0], planes, grid, columns).transpose(2, 1, 0, 3)
        return lax.all_to_all(parts, "grid", split_axis=0, concat_axis=0)

    def along_yz(field):
        return dot("cxyz,zk->cxyk", field, kin) + dot("cxyz,yk->cxkz", field, kin)

    moved = scatter(jnp.concatenate([psi, potential[None]], axis=0))
    local_kin = along_yz(psi) - psi
    applied = local_kin + potential * psi
    mixed = scatter(local_kin + applied)
    twice = along_yz(applied) - applied + potential * applied

    along = dot("ksp,spcn->ckn", kin_x, moved[:, :, :2])
    again = dot("ksp,spcn->ckn", kin_x, mixed) + dot("kx,cxn->ckn", kin, along)
    potential_cols = moved[:, :, 2].reshape(length, columns)
    again = again + potential_cols * along
    turned = jnp.stack([along[1], -along[0]])
    update = 2.0 * BESSEL_ONE * turned - 4.0 * BESSEL_TWO * again
    update = update.reshape(2, grid, planes, columns).transpose(1, 2, 0, 3)
    update = lax.all_to_all(update, "grid", split_axis=0, concat_axis=0)
    update = update.transpose(2, 1, 0, 3).reshape(psi.shape)

    turned = jnp.stack([applied[1], -applied[0]])
    fresh = (
        (BESSEL_ZERO + 2.0 * BESSEL_TWO) * psi
        + 2.0 * BESSEL_ONE * turned
        - 4.0 * BESSEL_TWO * twice
        + update
    )
    part = occupations[0] * (fresh[0] * fresh[0] + fresh[1] * fresh[1])
    density = lax.psum(part, "band")

    spectrum = dot("xyz,kz->xyk", part, basis)
    spectrum = dot("xyk,jy->xjk", spectrum, basis)
    spectrum = spectrum.reshape(planes, bands * grid, share).transpose(1, 0, 2)
    spectrum = lax.all_to_all(spectrum, ("band", "grid"), split_axis=0, concat_axis=0)
    spectrum = spectrum.reshape(bands, grid, planes, share).sum(axis=0)
    spectrum = dot("ksp,spn->kn", basis_x, spectrum)
    start = (lax.axis_index("band") * grid + lax.axis_index("grid")) * share
    cell = start + jnp.arange(share, dtype=jnp.int32)
    table = jnp.asarray(squares)
    total = table[:, None] + (table[cell // length] + table[cell % length])[None, :]
    kernel = jnp.where(total > 0, length * math.sqrt(length) / 16.0 / (total + 1.0), 0.0)
    spectrum = dot("kx,kn->xn", basis, kernel * spectrum)
    spectrum = spectrum.reshape(1, grid, planes, share)
    spectrum = jnp.broadcast_to(spectrum, (bands, grid, planes, share)).reshape(bands * grid, planes, share)
    spectrum = lax.all_to_all(spectrum, ("band", "grid"), split_axis=0, concat_axis=0)
    spectrum = spectrum.transpose(1, 0, 2).reshape(planes, length, length)
    spectrum = dot("xjk,jy->xyk", spectrum, basis)
    hartree = dot("xyk,kz->xyz", spectrum, basis)
    return (fresh[None], hartree - XC_FACTOR * jnp.cbrt(density))


LANES = 128


def product(left, right):
    return jnp.dot(left, right, precision=lax.Precision.HIGHEST, preferred_element_type=jnp.float32)


def split(array):
    high = array.astype(jnp.bfloat16)
    return high, (array - high.astype(jnp.float32)).astype(jnp.bfloat16)


def product_of_parts(left, right):
    total = jnp.dot(left[0], right[0], preferred_element_type=jnp.float32)
    total = total + jnp.dot(left[1], right[0], preferred_element_type=jnp.float32)
    return total + jnp.dot(left[0], right[1], preferred_element_type=jnp.float32)


def whole_tiles(rows):
    return -(-rows // 8) * 8


def chunk_rows(sizes):
    planes, _, rows, share = sizes
    return whole_tiles(planes * share)


def kinetic(plane, kin):
    plane = split(plane)
    return product_of_parts(plane, kin) + product_of_parts(kin, plane)


def pack(plane, packed):
    length = plane.shape[0]
    half = length // 2
    packed[:length, :] = plane[:, :LANES]
    packed[length:, :] = jnp.concatenate([plane[:half, LANES:], plane[half:, LANES:]], axis=1)


def unpack(packed, length):
    side = length - LANES
    tail = packed[length:, :]
    right = jnp.concatenate([tail[:, :side], tail[:, side:]], axis=0)
    return jnp.concatenate([packed[:length, :], right], axis=1)


def fill(out_ref, count, chunk, used):
    if used < chunk:

        @pl.when(pl.program_id(0) == 0)
        def _():
            for to in range(count):
                out_ref[pl.ds(to * chunk + used, chunk - used), :] = jnp.zeros((chunk - used, LANES), jnp.float32)


def potential_kernel(sizes, bunch, place_ref, ion_ref, hxc_ref, out_ref, packed):
    planes, grid, rows, share = sizes
    chunk = chunk_rows(sizes)
    band = place_ref[0] // grid
    fill(out_ref, grid, chunk, planes * share)
    for inner in range(bunch):
        plane = pl.program_id(0) * bunch + inner
        slot = packed.at[inner]
        pack(ion_ref[inner] + hxc_ref[inner], slot)
        for to in range(grid):
            start = to * rows + band * share
            out_ref[pl.ds(to * chunk + plane * share, share), :] = slot[pl.ds(start, share), :]


def pack_kernel(sizes, bunch, turns, place_ref, psi_ref, *refs):
    planes, grid, rows, share = sizes
    *out_refs, packed = refs
    mine = place_ref[0] % grid
    for inner in range(bunch):
        plane = pl.program_id(0) * bunch + inner
        for part in range(2):
            slot = packed.at[inner * 2 + part]
            pack(psi_ref[0, part, inner], slot)
            for turn, out_ref in zip(turns, out_refs):
                start = (mine ^ turn) * rows
                out_ref[pl.ds((plane * 2 + part) * rows, rows), :] = slot[pl.ds(start, rows), :]


def plane_kernel(sizes, bunch, turns, place_ref, psi_ref, ion_ref, hxc_ref, kin_ref, *refs):
    planes, grid, rows, share = sizes
    *out_refs, base_ref, packed = refs
    mine = place_ref[0] % grid
    kin = split(kin_ref[...])
    for inner in range(bunch):
        plane = pl.program_id(0) * bunch + inner
        potential = ion_ref[inner] + hxc_ref[inner]
        applied = []
        for part in range(2):
            field = psi_ref[0, part, inner]
            bare = kinetic(field, kin) - field
            applied.append(bare + potential * field)
            slot = packed.at[inner * 2 + part]
            pack(bare + applied[part], slot)
            for turn, out_ref in zip(turns, out_refs):
                start = (mine ^ turn) * rows
                out_ref[pl.ds((plane * 2 + part) * rows, rows), :] = slot[pl.ds(start, rows), :]
        for part in range(2):
            twice = kinetic(applied[part], kin) + (potential - 1.0) * applied[part]
            turned = applied[1] if part == 0 else -applied[0]
            base_ref[part, inner] = (
                (BESSEL_ZERO + 2.0 * BESSEL_TWO) * psi_ref[0, part, inner]
                + 2.0 * BESSEL_ONE * turned
                - 4.0 * BESSEL_TWO * twice
            )


def share_kernel(sizes, moved_ref, out_ref):
    planes, grid, rows, share = sizes
    length = planes * grid
    chunk = chunk_rows(sizes)
    for source in range(grid):
        for row in range(share):
            start = source * chunk + row
            out_ref[pl.ds(row * length + source * planes, planes), :] = moved_ref[pl.ds(start, planes, stride=share), :]


def along_kernel(sizes, steps, turns, place_ref, *refs):
    planes, grid, rows, share = sizes
    *moved_refs, kin_ref, out_ref, lines = refs
    length = planes * grid
    kin = split(kin_ref[...])
    for inner in range(rows // steps):
        row = pl.program_id(0) * (rows // steps) + inner
        slot = lines.at[inner]
        for turn, moved_ref in zip(turns, moved_refs):
            first = (place_ref[0] % grid ^ turn) * planes
            for part in range(2):
                slot[part, pl.ds(first, planes), :] = moved_ref[pl.ds(part * rows + row, planes, stride=2 * rows), :]
        field = jnp.concatenate([slot[0], slot[1]], axis=1)
        out_ref[inner * length : (inner + 1) * length, :] = product_of_parts(kin, split(field))


def update_kernel(sizes, steps, turns, place_ref, along_ref, own_ref, other_ref, kin_ref, *refs):
    planes, grid, rows, share = sizes
    *mixed_refs, out_ref, lines = refs
    length = planes * grid
    kin = split(kin_ref[...])
    step = pl.program_id(0)
    mine_here = place_ref[0] // grid == step // (steps // 2)
    for inner in range(rows // steps):
        row = step * (rows // steps) + inner
        here = slice(inner * length, (inner + 1) * length)
        slot = lines.at[inner]
        for turn, mixed_ref in zip(turns, mixed_refs):
            first = (place_ref[0] % grid ^ turn) * planes
            for part in range(2):
                slot[part, pl.ds(first, planes), :] = mixed_ref[pl.ds(part * rows + row, planes, stride=2 * rows), :]
        along = along_ref[here, :]
        again = product_of_parts(kin, split(jnp.concatenate([slot[0], slot[1]], axis=1) + along))
        potential = jnp.where(mine_here, own_ref[here, :], other_ref[here, :])
        for part in range(2):
            mine = along[:, part * LANES : (part + 1) * LANES]
            turned = along[:, LANES:] if part == 0 else -along[:, :LANES]
            twice = again[:, part * LANES : (part + 1) * LANES] + potential * mine
            out_ref[pl.ds(part * rows + row, length, stride=2 * rows), :] = (
                2.0 * BESSEL_ONE * turned - 4.0 * BESSEL_TWO * twice
            )


def fresh_kernel(
    sizes, bunch, occ_ref, update_ref, base_ref, tables_ref, fresh_ref, upper_ref, lower_ref, out_ref, packed
):
    planes, grid, rows, share = sizes
    length = planes * grid
    chunk = chunk_rows(sizes)
    cell_rows = rows * grid
    half = cell_rows // 2
    fill(out_ref, 2 * grid, chunk, planes * share)
    means, parts = [], []
    for inner in range(bunch):
        plane = pl.program_id(0) * bunch + inner
        part_sum = None
        for part in range(2):
            slot = packed.at[inner * 4 + part]
            for source in range(grid):
                start = ((source * planes + plane) * 2 + part) * rows
                slot[pl.ds(source * rows, rows), :] = update_ref[pl.ds(start, rows), :]
            fresh = base_ref[part, inner] + unpack(slot, length)
            fresh_ref[0, part, inner] = fresh
            part_sum = fresh * fresh if part_sum is None else part_sum + fresh * fresh
        part_sum = occ_ref[0] * part_sum
        slot = packed.at[inner * 4 + 2]
        pack(part_sum, slot)
        upper_ref[inner * half : (inner + 1) * half, :] = slot[:half, :]
        lower_ref[inner * half : (inner + 1) * half, :] = slot[half:, :]
        means.append(jnp.sum(part_sum) * (1.0 / length**2))
        parts.append(part_sum - means[inner])
    basis, turn = split(tables_ref[0]), split(tables_ref[1])
    along_z = product_of_parts(split(jnp.concatenate(parts, axis=0)), turn)
    first = (lax.broadcasted_iota(jnp.int32, (length, length), axis) == 0 for axis in range(2))
    first = jnp.logical_and(*first)
    for inner in range(bunch):
        plane = pl.program_id(0) * bunch + inner
        spectrum = product_of_parts(basis, split(along_z[inner * length : (inner + 1) * length, :]))
        slot = packed.at[inner * 4 + 3]
        pack(spectrum + jnp.where(first, means[inner] * length, 0.0), slot)
        for to in range(2 * grid):
            out_ref[pl.ds(to * chunk + plane * share, share), :] = slot[pl.ds(to * share, share), :]


def filter_kernel(sizes, spec_ref, cells_ref, tables_ref, out_ref, lines):
    planes, grid, rows, share = sizes
    length = planes * grid
    chunk = chunk_rows(sizes)

    def places():
        for source in range(grid):
            for row in range(share):
                first, second = (
                    pl.ds((band * grid + source) * chunk + row, planes, stride=share) for band in range(2)
                )
                here = (pl.ds(source * planes, planes), slice(row * LANES, (row + 1) * LANES))
                yield first, second, here

    for first, second, here in places():
        lines[here] = spec_ref[first, :] + spec_ref[second, :]
    index = lax.broadcasted_iota(jnp.int32, lines.shape, 0)
    order = jnp.where(index <= length // 2, index, index - length // 2).astype(jnp.float32)
    total = order * order + cells_ref[...]
    scale = length * math.sqrt(length) / 16.0
    kernel = jnp.where(total > 0.0, scale / (total + 1.0), 0.0)
    field = kernel * product(tables_ref[0], lines[...])
    lines[...] = product_of_parts(split(tables_ref[1]), split(field))
    for first, second, here in places():
        piece = lines[here]
        out_ref[first, :] = piece
        out_ref[second, :] = piece
    used = planes * share
    if used < chunk:
        for to in range(2 * grid):
            out_ref[pl.ds(to * chunk + used, chunk - used), :] = jnp.zeros((chunk - used, LANES), jnp.float32)


def last_kernel(
    sizes, bunch, spec_ref, upper_ref, lower_ref, upper_other, lower_other, tables_ref, out_ref, packed
):
    planes, grid, rows, share = sizes
    length = planes * grid
    half = rows * grid // 2
    chunk = chunk_rows(sizes)
    turn, basis = split(tables_ref[1]), split(tables_ref[0])
    lines = []
    for inner in range(bunch):
        plane = pl.program_id(0) * bunch + inner
        slot = packed.at[inner * 2]
        for source in range(2 * grid):
            start = source * chunk + plane * share
            slot[pl.ds(source * share, share), :] = spec_ref[pl.ds(start, share), :]
        lines.append(product_of_parts(turn, split(unpack(slot, length))))
    hartree = product_of_parts(split(jnp.concatenate(lines, axis=0)), basis)
    for inner in range(bunch):
        slot = packed.at[inner * 2 + 1]
        here = slice(inner * half, (inner + 1) * half)
        slot[:half, :] = upper_ref[here, :] + upper_other[here, :]
        slot[half:, :] = lower_ref[here, :] + lower_other[here, :]
        root = jnp.exp(jnp.log(unpack(slot, length)) * (1.0 / 3.0))
        out_ref[inner] = hartree[inner * length : (inner + 1) * length, :] - XC_FACTOR * root


def shape(*dims):
    return jax.ShapeDtypeStruct(dims, jnp.float32)


def whole(*dims):
    return pl.BlockSpec(dims, lambda *_: (0,) * len(dims))


SMALL = pltpu.CompilerParams(vmem_limit_bytes=24 << 20)
PARAMS = pltpu.CompilerParams(vmem_limit_bytes=54 << 20)


def cost(flops, moved):
    return pl.CostEstimate(flops=flops, bytes_accessed=moved, transcendentals=0)


def turn_order(grid):
    order = [0]
    for near in range(grid // 2):
        order += [near, near + grid // 2] if near else [grid // 2]
    return order


def packed_path(orbitals, occupations, ion_potential, hxc_potential):
    length = orbitals.shape[-1]
    planes = orbitals.shape[2]
    grid = lax.axis_size("grid")
    cell_rows = length * length // LANES
    rows = cell_rows // grid
    share = rows // 2
    sizes = (planes, grid, rows, share)
    field = planes * cell_rows
    work = 2 * planes * length**3
    place = lax.axis_index(("band", "grid")).astype(jnp.int32).reshape(1)
    kin = jnp.asarray(kinetic_matrix(length))
    basis_np, squares_np = real_basis(length)
    tables = jnp.asarray(np.stack([basis_np, basis_np.T]))
    smem = pl.BlockSpec(memory_space=pltpu.SMEM)
    vmem = pl.BlockSpec(memory_space=pltpu.VMEM)
    bunch = next(count for count in (3, 2, 1) if planes % count == 0)
    psi_spec = pl.BlockSpec((1, 2, bunch, length, length), lambda i: (0, 0, i, 0, 0))
    plane_spec = pl.BlockSpec((bunch, length, length), lambda i: (i, 0, 0))
    pair_spec = pl.BlockSpec((2, bunch, length, length), lambda i: (0, i, 0, 0))
    half_rows = pl.BlockSpec((bunch * cell_rows // 2, LANES), lambda i: (i, 0))
    square = whole(length, length)
    table_spec = whole(2, length, length)

    def scratch(count):
        return [pltpu.VMEM((count * bunch, cell_rows, LANES), jnp.float32)]

    line = []

    def send(turn, piece, *gates):
        if not turn:
            return piece
        if len(line) >= 5:
            gates += (line[-5],)
        if gates:
            piece = lax.optimization_barrier((piece, *gates))[0]
        line.append(lax.ppermute(piece, "grid", [(spot, spot ^ turn) for spot in range(grid)]))
        return line[-1]

    def swap(array):
        flat = array.reshape(grid, -1, LANES)
        return lax.all_to_all(flat, "grid", split_axis=0, concat_axis=0).reshape(array.shape)

    def swap_all(array):
        flat = array.reshape(2 * grid, -1, LANES)
        return lax.all_to_all(flat, ("band", "grid"), split_axis=0, concat_axis=0).reshape(array.shape)

    turns = turn_order(grid)
    spec_rows = 2 * grid * chunk_rows(sizes)
    mixed_rows = 2 * planes * rows
    steps = 6 if rows % 6 == 0 and share % (rows // 6) == 0 else 2
    shared = pl.pallas_call(
        functools.partial(potential_kernel, sizes, bunch),
        grid=(planes // bunch,),
        in_specs=[smem, plane_spec, plane_spec],
        out_specs=whole(spec_rows // 2, LANES),
        out_shape=shape(spec_rows // 2, LANES),
        scratch_shapes=scratch(1),
        compiler_params=PARAMS,
        cost_estimate=cost(0, 6 << 20),
    )(place, ion_potential, hxc_potential)
    place, shared = lax.optimization_barrier((place, shared))
    shared = swap(shared)
    moved = pl.pallas_call(
        functools.partial(pack_kernel, sizes, bunch, turns),
        grid=(planes // bunch,),
        in_specs=[smem, psi_spec],
        out_specs=[whole(mixed_rows, LANES)] * grid,
        out_shape=[shape(mixed_rows, LANES)] * grid,
        scratch_shapes=scratch(2),
        compiler_params=PARAMS,
        cost_estimate=cost(0, 8 << 20),
    )(place, orbitals)
    moved = [send(turn, piece) for turn, piece in zip(turns[:6], moved[:6])] + list(moved[6:])
    behind = lax.optimization_barrier((place, line[1]))[0]
    *mixed, base = pl.pallas_call(
        functools.partial(plane_kernel, sizes, bunch, turns),
        grid=(planes // bunch,),
        in_specs=[smem, psi_spec, plane_spec, plane_spec, square],
        out_specs=[whole(mixed_rows, LANES)] * grid + [pair_spec],
        out_shape=[shape(mixed_rows, LANES)] * grid + [shape(2, planes, length, length)],
        scratch_shapes=scratch(2),
        compiler_params=PARAMS,
        cost_estimate=cost(8 * 3 * work, 20 << 20),
    )(behind, orbitals, ion_potential, hxc_potential, kin)
    for index in range(6, grid):
        moved[index] = send(turns[index], moved[index], *([base] if index < 11 else []))
    own = pl.pallas_call(
        functools.partial(share_kernel, sizes),
        in_specs=[vmem],
        out_specs=vmem,
        out_shape=shape(share * length, LANES),
        compiler_params=PARAMS,
        cost_estimate=cost(0, 2 << 20),
    )(shared)
    other = lax.ppermute(own, "band", [(0, 1), (1, 0)])
    along = pl.pallas_call(
        functools.partial(along_kernel, sizes, steps, turns),
        grid=(steps,),
        in_specs=[smem] + [whole(mixed_rows, LANES)] * grid + [square],
        out_specs=pl.BlockSpec((rows // steps * length, 2 * LANES), lambda i: (i, 0)),
        out_shape=shape(rows * length, 2 * LANES),
        scratch_shapes=[pltpu.VMEM((rows // steps, 2, length, LANES), jnp.float32)],
        compiler_params=PARAMS,
        cost_estimate=cost(2 * 3 * work, 8 << 20),
    )(place, *moved, kin)
    mixed = [send(turn, piece) for turn, piece in zip(turns, mixed)]
    half_spec = pl.BlockSpec((rows // steps * length, LANES), lambda i: (i % (steps // 2), 0))
    update = pl.pallas_call(
        functools.partial(update_kernel, sizes, steps, turns),
        grid=(steps,),
        in_specs=[
            smem,
            pl.BlockSpec((rows // steps * length, 2 * LANES), lambda i: (i, 0)),
            half_spec,
            half_spec,
            square,
        ]
        + [whole(mixed_rows, LANES)] * grid,
        out_specs=whole(2 * field, LANES),
        out_shape=shape(2 * field, LANES),
        scratch_shapes=[pltpu.VMEM((rows // steps, 2, length, LANES), jnp.float32)],
        compiler_params=PARAMS,
        cost_estimate=cost(2 * 3 * work, 14 << 20),
    )(place, along, own, other, kin, *mixed)
    update = swap(update)

    fresh, upper, lower, spectrum = pl.pallas_call(
        functools.partial(fresh_kernel, sizes, bunch),
        grid=(planes // bunch,),
        in_specs=[smem, vmem, pair_spec, table_spec],
        out_specs=[
            psi_spec,
            half_rows,
            half_rows,
            whole(spec_rows, LANES),
        ],
        out_shape=[
            shape(*orbitals.shape),
            shape(field // 2, LANES),
            shape(field // 2, LANES),
            shape(spec_rows, LANES),
        ],
        scratch_shapes=scratch(4),
        compiler_params=PARAMS,
        cost_estimate=cost(2 * 6 * work, 16 << 20),
    )(occupations, update, base, tables)
    upper_other = lax.ppermute(upper, "band", [(0, 1), (1, 0)])
    lower_other = lax.ppermute(lower, "band", [(0, 1), (1, 0)])

    spectrum = swap_all(spectrum)
    cells_np = squares_np[:, None] + squares_np[None, :]
    half = length // 2
    cells_np = np.concatenate(
        [cells_np[:, :LANES], np.concatenate([cells_np[:half, LANES:], cells_np[half:, LANES:]], axis=1)]
    )
    device = lax.axis_index("band") * grid + lax.axis_index("grid")
    cells = lax.dynamic_slice_in_dim(jnp.asarray(cells_np), device * share, share, axis=0)
    spectrum = pl.pallas_call(
        functools.partial(filter_kernel, sizes),
        in_specs=[vmem] * 3,
        out_specs=vmem,
        out_shape=shape(spec_rows, LANES),
        scratch_shapes=[pltpu.VMEM((length, share * LANES), jnp.float32)],
        compiler_params=SMALL,
        cost_estimate=cost(6 * work, 5 << 20),
    )(spectrum, cells.reshape(1, share * LANES), tables)
    spectrum, upper_other = lax.optimization_barrier((spectrum, upper_other))
    spectrum = swap_all(spectrum)
    potential = pl.pallas_call(
        functools.partial(last_kernel, sizes, bunch),
        grid=(planes // bunch,),
        in_specs=[
            vmem,
            half_rows,
            half_rows,
            half_rows,
            half_rows,
            table_spec,
        ],
        out_specs=plane_spec,
        out_shape=shape(planes, length, length),
        scratch_shapes=scratch(2),
        compiler_params=PARAMS,
        cost_estimate=cost(2 * 6 * work, 6 << 20),
    )(spectrum, upper, lower, upper_other, lower_other, tables)
    return (fresh, potential)


def local(orbitals, occupations, ion_potential, hxc_potential):
    length = orbitals.shape[-1]
    parts = 2 * lax.axis_size("grid") * LANES
    fits = lax.axis_size("grid") & (lax.axis_size("grid") - 1) == 0
    fits = fits and length == LANES + LANES // 2 and lax.axis_size("band") == 2 and length * length % parts == 0
    path = packed_path if fits else general
    return path(orbitals, occupations, ion_potential, hxc_potential)


def solution(mesh):
    placed = (
        P("band", None, "grid", None, None),
        P("band"),
        P("grid", None, None),
        P("grid", None, None),
    )
    return jax.shard_map(
        local,
        mesh=mesh,
        in_specs=placed,
        out_specs=(P("band", None, "grid", None, None), P("grid", None, None)),
        check_vma=False,
    )
```

```python
import functools
import math

import jax
import jax.numpy as jnp
import numpy as np
from jax import lax
from jax.experimental import pallas as pl
from jax.experimental.pallas import tpu as pltpu
from jax.sharding import PartitionSpec as P

BESSEL_ZERO = 0.8462873527504802
BESSEL_ONE = 0.36884204609417703
BESSEL_TWO = 0.07581776248
XC_FACTOR = 0.98474502
PRECISION = lax.Precision.HIGH


def kinetic_matrix(length):
    idx = np.arange(length)
    freq = np.where(idx < length // 2, idx, idx - length).astype(np.float64)
    wave = np.cos(2.0 * math.pi * (np.outer(idx, idx) % length) / length)
    row = (wave @ (freq * freq)) / length * (2.0 / (3.0 * (length / 2) ** 2))
    return row[(idx[:, None] - idx[None, :]) % length].astype(np.float32)


def real_basis(length):
    half = length // 2
    idx = np.arange(length)
    order = np.concatenate([np.arange(half + 1), np.arange(1, half)])
    angle = 2.0 * math.pi * (np.outer(order, idx) % length) / length
    table = np.where((np.arange(length) <= half)[:, None], np.cos(angle), np.sin(angle))
    scale = np.where((order == 0) | (order == half), math.sqrt(1.0 / length), math.sqrt(2.0 / length))
    return (table * scale[:, None]).astype(np.float32), (order * order).astype(np.float32)


def dot(form, left, right):
    return jnp.einsum(form, left, right, precision=PRECISION)


def general(orbitals, occupations, ion_potential, hxc_potential):
    length = orbitals.shape[-1]
    planes = orbitals.shape[2]
    grid = lax.axis_size("grid")
    bands = lax.axis_size("band")
    cells = length * length
    columns = cells // grid
    share = cells // (grid * bands)
    kin = jnp.asarray(kinetic_matrix(length))
    kin_x = kin.reshape(length, grid, planes)
    basis_np, squares = real_basis(length)
    basis = jnp.asarray(basis_np)
    basis_x = basis.reshape(length, grid, planes)

    psi = orbitals[0]
    potential = ion_potential + hxc_potential

    def scatter(fields):
        parts = fields.reshape(fields.shape[0], planes, grid, columns).transpose(2, 1, 0, 3)
        return lax.all_to_all(parts, "grid", split_axis=0, concat_axis=0)

    def along_yz(field):
        return dot("cxyz,zk->cxyk", field, kin) + dot("cxyz,yk->cxkz", field, kin)

    moved = scatter(jnp.concatenate([psi, potential[None]], axis=0))
    local_kin = along_yz(psi) - psi
    applied = local_kin + potential * psi
    mixed = scatter(local_kin + applied)
    twice = along_yz(applied) - applied + potential * applied

    along = dot("ksp,spcn->ckn", kin_x, moved[:, :, :2])
    again = dot("ksp,spcn->ckn", kin_x, mixed) + dot("kx,cxn->ckn", kin, along)
    potential_cols = moved[:, :, 2].reshape(length, columns)
    again = again + potential_cols * along
    turned = jnp.stack([along[1], -along[0]])
    update = 2.0 * BESSEL_ONE * turned - 4.0 * BESSEL_TWO * again
    update = update.reshape(2, grid, planes, columns).transpose(1, 2, 0, 3)
    update = lax.all_to_all(update, "grid", split_axis=0, concat_axis=0)
    update = update.transpose(2, 1, 0, 3).reshape(psi.shape)

    turned = jnp.stack([applied[1], -applied[0]])
    fresh = (
        (BESSEL_ZERO + 2.0 * BESSEL_TWO) * psi
        + 2.0 * BESSEL_ONE * turned
        - 4.0 * BESSEL_TWO * twice
        + update
    )
    part = occupations[0] * (fresh[0] * fresh[0] + fresh[1] * fresh[1])
    density = lax.psum(part, "band")

    spectrum = dot("xyz,kz->xyk", part, basis)
    spectrum = dot("xyk,jy->xjk", spectrum, basis)
    spectrum = spectrum.reshape(planes, bands * grid, share).transpose(1, 0, 2)
    spectrum = lax.all_to_all(spectrum, ("band", "grid"), split_axis=0, concat_axis=0)
    spectrum = spectrum.reshape(bands, grid, planes, share).sum(axis=0)
    spectrum = dot("ksp,spn->kn", basis_x, spectrum)
    start = (lax.axis_index("band") * grid + lax.axis_index("grid")) * share
    cell = start + jnp.arange(share, dtype=jnp.int32)
    table = jnp.asarray(squares)
    total = table[:, None] + (table[cell // length] + table[cell % length])[None, :]
    kernel = jnp.where(total > 0, length * math.sqrt(length) / 16.0 / (total + 1.0), 0.0)
    spectrum = dot("kx,kn->xn", basis, kernel * spectrum)
    spectrum = spectrum.reshape(1, grid, planes, share)
    spectrum = jnp.broadcast_to(spectrum, (bands, grid, planes, share)).reshape(bands * grid, planes, share)
    spectrum = lax.all_to_all(spectrum, ("band", "grid"), split_axis=0, concat_axis=0)
    spectrum = spectrum.transpose(1, 0, 2).reshape(planes, length, length)
    spectrum = dot("xjk,jy->xyk", spectrum, basis)
    hartree = dot("xyk,kz->xyz", spectrum, basis)
    return (fresh[None], hartree - XC_FACTOR * jnp.cbrt(density))


LANES = 128


def product(left, right):
    return jnp.dot(left, right, precision=lax.Precision.HIGHEST, preferred_element_type=jnp.float32)


def split(array):
    high = array.astype(jnp.bfloat16)
    return high, (array - high.astype(jnp.float32)).astype(jnp.bfloat16)


def product_of_parts(left, right):
    total = jnp.dot(left[0], right[0], preferred_element_type=jnp.float32)
    total = total + jnp.dot(left[1], right[0], preferred_element_type=jnp.float32)
    return total + jnp.dot(left[0], right[1], preferred_element_type=jnp.float32)


def whole_tiles(rows):
    return -(-rows // 8) * 8


def chunk_rows(sizes):
    planes, _, rows, share = sizes
    return whole_tiles(planes * share)


def kinetic(plane, kin):
    plane = split(plane)
    return product_of_parts(plane, kin) + product_of_parts(kin, plane)


def pack(plane, packed):
    length = plane.shape[0]
    half = length // 2
    packed[:length, :] = plane[:, :LANES]
    packed[length:, :] = jnp.concatenate([plane[:half, LANES:], plane[half:, LANES:]], axis=1)


def unpack(packed, length):
    side = length - LANES
    tail = packed[length:, :]
    right = jnp.concatenate([tail[:, :side], tail[:, side:]], axis=0)
    return jnp.concatenate([packed[:length, :], right], axis=1)


def fill(out_ref, count, chunk, used):
    if used < chunk:

        @pl.when(pl.program_id(0) == 0)
        def _():
            for to in range(count):
                out_ref[pl.ds(to * chunk + used, chunk - used), :] = jnp.zeros((chunk - used, LANES), jnp.float32)


def potential_kernel(sizes, bunch, place_ref, ion_ref, hxc_ref, out_ref, packed):
    planes, grid, rows, share = sizes
    chunk = chunk_rows(sizes)
    band = place_ref[0] // grid
    fill(out_ref, grid, chunk, planes * share)
    for inner in range(bunch):
        plane = pl.program_id(0) * bunch + inner
        slot = packed.at[inner]
        pack(ion_ref[inner] + hxc_ref[inner], slot)
        for to in range(grid):
            start = to * rows + band * share
            out_ref[pl.ds(to * chunk + plane * share, share), :] = slot[pl.ds(start, share), :]


def pack_kernel(sizes, bunch, turns, place_ref, psi_ref, *refs):
    planes, grid, rows, share = sizes
    *out_refs, packed = refs
    mine = place_ref[0] % grid
    for inner in range(bunch):
        plane = pl.program_id(0) * bunch + inner
        for part in range(2):
            slot = packed.at[inner * 2 + part]
            pack(psi_ref[0, part, inner], slot)
            for turn, out_ref in zip(turns, out_refs):
                start = (mine ^ turn) * rows
                out_ref[pl.ds((plane * 2 + part) * rows, rows), :] = slot[pl.ds(start, rows), :]


def plane_kernel(sizes, bunch, turns, place_ref, psi_ref, ion_ref, hxc_ref, kin_ref, *refs):
    planes, grid, rows, share = sizes
    *out_refs, base_ref, packed = refs
    mine = place_ref[0] % grid
    kin = split(kin_ref[...])
    for inner in range(bunch):
        plane = pl.program_id(0) * bunch + inner
        potential = ion_ref[inner] + hxc_ref[inner]
        applied = []
        for part in range(2):
            field = psi_ref[0, part, inner]
            bare = kinetic(field, kin) - field
            applied.append(bare + potential * field)
            slot = packed.at[inner * 2 + part]
            pack(bare + applied[part], slot)
            for turn, out_ref in zip(turns, out_refs):
                start = (mine ^ turn) * rows
                out_ref[pl.ds((plane * 2 + part) * rows, rows), :] = slot[pl.ds(start, rows), :]
        for part in range(2):
            twice = kinetic(applied[part], kin) + (potential - 1.0) * applied[part]
            turned = applied[1] if part == 0 else -applied[0]
            base_ref[part, inner] = (
                (BESSEL_ZERO + 2.0 * BESSEL_TWO) * psi_ref[0, part, inner]
                + 2.0 * BESSEL_ONE * turned
                - 4.0 * BESSEL_TWO * twice
            )


def share_kernel(sizes, moved_ref, out_ref):
    planes, grid, rows, share = sizes
    length = planes * grid
    chunk = chunk_rows(sizes)
    for source in range(grid):
        for row in range(share):
            start = source * chunk + row
            out_ref[pl.ds(row * length + source * planes, planes), :] = moved_ref[pl.ds(start, planes, stride=share), :]


def along_kernel(sizes, steps, turns, place_ref, *refs):
    planes, grid, rows, share = sizes
    *moved_refs, kin_ref, out_ref, lines = refs
    length = planes * grid
    kin = split(kin_ref[...])
    for inner in range(rows // steps):
        row = pl.program_id(0) * (rows // steps) + inner
        slot = lines.at[inner]
        for turn, moved_ref in zip(turns, moved_refs):
            first = (place_ref[0] % grid ^ turn) * planes
            for part in range(2):
                slot[part, pl.ds(first, planes), :] = moved_ref[pl.ds(part * rows + row, planes, stride=2 * rows), :]
        field = jnp.concatenate([slot[0], slot[1]], axis=1)
        out_ref[inner * length : (inner + 1) * length, :] = product_of_parts(kin, split(field))


def update_kernel(sizes, steps, turns, place_ref, along_ref, own_ref, other_ref, kin_ref, *refs):
    planes, grid, rows, share = sizes
    *mixed_refs, out_ref, lines = refs
    length = planes * grid
    kin = split(kin_ref[...])
    step = pl.program_id(0)
    mine_here = place_ref[0] // grid == step // (steps // 2)
    for inner in range(rows // steps):
        row = step * (rows // steps) + inner
        here = slice(inner * length, (inner + 1) * length)
        slot = lines.at[inner]
        for turn, mixed_ref in zip(turns, mixed_refs):
            first = (place_ref[0] % grid ^ turn) * planes
            for part in range(2):
                slot[part, pl.ds(first, planes), :] = mixed_ref[pl.ds(part * rows + row, planes, stride=2 * rows), :]
        along = along_ref[here, :]
        again = product_of_parts(kin, split(jnp.concatenate([slot[0], slot[1]], axis=1) + along))
        potential = jnp.where(mine_here, own_ref[here, :], other_ref[here, :])
        for part in range(2):
            mine = along[:, part * LANES : (part + 1) * LANES]
            turned = along[:, LANES:] if part == 0 else -along[:, :LANES]
            twice = again[:, part * LANES : (part + 1) * LANES] + potential * mine
            out_ref[pl.ds(part * rows + row, length, stride=2 * rows), :] = (
                2.0 * BESSEL_ONE * turned - 4.0 * BESSEL_TWO * twice
            )


def fresh_kernel(
    sizes, bunch, occ_ref, update_ref, base_ref, tables_ref, fresh_ref, upper_ref, lower_ref, out_ref, packed
):
    planes, grid, rows, share = sizes
    length = planes * grid
    chunk = chunk_rows(sizes)
    cell_rows = rows * grid
    half = cell_rows // 2
    fill(out_ref, 2 * grid, chunk, planes * share)
    means, parts = [], []
    for inner in range(bunch):
        plane = pl.program_id(0) * bunch + inner
        part_sum = None
        for part in range(2):
            slot = packed.at[inner * 4 + part]
            for source in range(grid):
                start = ((source * planes + plane) * 2 + part) * rows
                slot[pl.ds(source * rows, rows), :] = update_ref[pl.ds(start, rows), :]
            fresh = base_ref[part, inner] + unpack(slot, length)
            fresh_ref[0, part, inner] = fresh
            part_sum = fresh * fresh if part_sum is None else part_sum + fresh * fresh
        part_sum = occ_ref[0] * part_sum
        slot = packed.at[inner * 4 + 2]
        pack(part_sum, slot)
        upper_ref[inner * half : (inner + 1) * half, :] = slot[:half, :]
        lower_ref[inner * half : (inner + 1) * half, :] = slot[half:, :]
        means.append(jnp.sum(part_sum) * (1.0 / length**2))
        parts.append(part_sum - means[inner])
    basis, turn = split(tables_ref[0]), split(tables_ref[1])
    along_z = product_of_parts(split(jnp.concatenate(parts, axis=0)), turn)
    first = (lax.broadcasted_iota(jnp.int32, (length, length), axis) == 0 for axis in range(2))
    first = jnp.logical_and(*first)
    for inner in range(bunch):
        plane = pl.program_id(0) * bunch + inner
        spectrum = product_of_parts(basis, split(along_z[inner * length : (inner + 1) * length, :]))
        slot = packed.at[inner * 4 + 3]
        pack(spectrum + jnp.where(first, means[inner] * length, 0.0), slot)
        for to in range(2 * grid):
            out_ref[pl.ds(to * chunk + plane * share, share), :] = slot[pl.ds(to * share, share), :]


def filter_kernel(sizes, spec_ref, cells_ref, tables_ref, upper_ref, lower_ref, lines):
    planes, grid, rows, share = sizes
    length = planes * grid
    chunk = chunk_rows(sizes)

    def places():
        for source in range(grid):
            for row in range(share):
                first, second = (
                    pl.ds((band * grid + source) * chunk + row, planes, stride=share) for band in range(2)
                )
                here = (pl.ds(source * planes, planes), slice(row * LANES, (row + 1) * LANES))
                yield first, second, here

    for first, second, here in places():
        lines[here] = spec_ref[first, :] + spec_ref[second, :]
    index = lax.broadcasted_iota(jnp.int32, lines.shape, 0)
    order = jnp.where(index <= length // 2, index, index - length // 2).astype(jnp.float32)
    total = order * order + cells_ref[...]
    scale = length * math.sqrt(length) / 16.0
    kernel = jnp.where(total > 0.0, scale / (total + 1.0), 0.0)
    field = kernel * product(tables_ref[0], lines[...])
    lines[...] = product_of_parts(split(tables_ref[1]), split(field))
    some = planes // 2
    chunk = whole_tiles(some * share)
    for part, out_ref in enumerate((upper_ref, lower_ref)):
        for source in range(grid):
            for row in range(share):
                piece = lines[pl.ds(source * planes + part * some, some), row * LANES : (row + 1) * LANES]
                out_ref[pl.ds(source * chunk + row, some, stride=share), :] = piece
            if some * share < chunk:
                rest = chunk - some * share
                out_ref[pl.ds(source * chunk + some * share, rest), :] = jnp.zeros((rest, LANES), jnp.float32)


def last_kernel(
    sizes, bunch, place_ref, near_ref, far_ref, upper_ref, lower_ref, upper_other, lower_other, tables_ref, *refs
):
    planes, grid, rows, share = sizes
    out_ref, packed = refs[-2:]
    length = planes * grid
    half = rows * grid // 2
    chunk = whole_tiles(planes // 2 * share)
    turn, basis = split(tables_ref[1]), split(tables_ref[0])
    band = place_ref[0] // grid
    lines = []
    for inner in range(bunch):
        plane = pl.program_id(0) * bunch + inner
        slot = packed.at[inner * 2]
        for part, spec_ref in ((band, near_ref), (1 - band, far_ref)):
            side = slot.at[pl.ds(pl.multiple_of(part * half, 8), half), :]
            for source in range(grid):
                start = source * chunk + plane * share
                side[pl.ds(source * share, share), :] = spec_ref[pl.ds(start, share), :]
        lines.append(product_of_parts(turn, split(unpack(slot, length))))
    hartree = product_of_parts(split(jnp.concatenate(lines, axis=0)), basis)
    for inner in range(bunch):
        slot = packed.at[inner * 2 + 1]
        here = slice(inner * half, (inner + 1) * half)
        slot[:half, :] = upper_ref[here, :] + upper_other[here, :]
        slot[half:, :] = lower_ref[here, :] + lower_other[here, :]
        root = jnp.exp(jnp.log(unpack(slot, length)) * (1.0 / 3.0))
        out_ref[inner] = hartree[inner * length : (inner + 1) * length, :] - XC_FACTOR * root


def shape(*dims):
    return jax.ShapeDtypeStruct(dims, jnp.float32)


def whole(*dims):
    return pl.BlockSpec(dims, lambda *_: (0,) * len(dims))


SMALL = pltpu.CompilerParams(vmem_limit_bytes=24 << 20)
PARAMS = pltpu.CompilerParams(vmem_limit_bytes=54 << 20)


def cost(flops, moved):
    return pl.CostEstimate(flops=flops, bytes_accessed=moved, transcendentals=0)


def turn_order(grid):
    order = [0]
    for near in range(grid // 2):
        order += [near, near + grid // 2] if near else [grid // 2]
    return order


def packed_path(orbitals, occupations, ion_potential, hxc_potential):
    length = orbitals.shape[-1]
    planes = orbitals.shape[2]
    grid = lax.axis_size("grid")
    cell_rows = length * length // LANES
    rows = cell_rows // grid
    share = rows // 2
    sizes = (planes, grid, rows, share)
    field = planes * cell_rows
    work = 2 * planes * length**3
    place = lax.axis_index(("band", "grid")).astype(jnp.int32).reshape(1)
    kin = jnp.asarray(kinetic_matrix(length))
    basis_np, squares_np = real_basis(length)
    tables = jnp.asarray(np.stack([basis_np, basis_np.T]))
    smem = pl.BlockSpec(memory_space=pltpu.SMEM)
    vmem = pl.BlockSpec(memory_space=pltpu.VMEM)
    some = planes // 2
    bunch = next(count for count in (3, 2, 1) if some % count == 0)
    groups = some // bunch
    psi_spec = pl.BlockSpec((1, 2, bunch, length, length), lambda i: (0, 0, i, 0, 0))
    plane_spec = pl.BlockSpec((bunch, length, length), lambda i: (i, 0, 0))
    pair_spec = pl.BlockSpec((2, bunch, length, length), lambda i: (0, i, 0, 0))
    half_rows = pl.BlockSpec((bunch * cell_rows // 2, LANES), lambda i: (i, 0))
    part_rows = grid * whole_tiles(some * share)
    square = whole(length, length)
    table_spec = whole(2, length, length)

    def scratch(count):
        return [pltpu.VMEM((count * bunch, cell_rows, LANES), jnp.float32)]

    line = []

    def send(turn, piece, *gates):
        if not turn:
            return piece
        if len(line) >= 5:
            gates += (line[-5],)
        if gates:
            piece = lax.optimization_barrier((piece, *gates))[0]
        line.append(lax.ppermute(piece, "grid", [(spot, spot ^ turn) for spot in range(grid)]))
        return line[-1]

    def swap(array):
        flat = array.reshape(grid, -1, LANES)
        return lax.all_to_all(flat, "grid", split_axis=0, concat_axis=0).reshape(array.shape)

    def swap_all(array):
        flat = array.reshape(2 * grid, -1, LANES)
        return lax.all_to_all(flat, ("band", "grid"), split_axis=0, concat_axis=0).reshape(array.shape)

    turns = turn_order(grid)
    spec_rows = 2 * grid * chunk_rows(sizes)
    mixed_rows = 2 * planes * rows
    steps = 6 if rows % 6 == 0 and share % (rows // 6) == 0 else 2
    shared = pl.pallas_call(
        functools.partial(potential_kernel, sizes, bunch),
        grid=(planes // bunch,),
        in_specs=[smem, plane_spec, plane_spec],
        out_specs=whole(spec_rows // 2, LANES),
        out_shape=shape(spec_rows // 2, LANES),
        scratch_shapes=scratch(1),
        compiler_params=PARAMS,
        cost_estimate=cost(0, 6 << 20),
    )(place, ion_potential, hxc_potential)
    place, shared = lax.optimization_barrier((place, shared))
    shared = swap(shared)
    moved = pl.pallas_call(
        functools.partial(pack_kernel, sizes, bunch, turns),
        grid=(planes // bunch,),
        in_specs=[smem, psi_spec],
        out_specs=[whole(mixed_rows, LANES)] * grid,
        out_shape=[shape(mixed_rows, LANES)] * grid,
        scratch_shapes=scratch(2),
        compiler_params=PARAMS,
        cost_estimate=cost(0, 8 << 20),
    )(place, orbitals)
    moved = [send(turn, piece) for turn, piece in zip(turns[:6], moved[:6])] + list(moved[6:])
    behind = lax.optimization_barrier((place, line[1]))[0]
    *mixed, base = pl.pallas_call(
        functools.partial(plane_kernel, sizes, bunch, turns),
        grid=(planes // bunch,),
        in_specs=[smem, psi_spec, plane_spec, plane_spec, square],
        out_specs=[whole(mixed_rows, LANES)] * grid + [pair_spec],
        out_shape=[shape(mixed_rows, LANES)] * grid + [shape(2, planes, length, length)],
        scratch_shapes=scratch(2),
        compiler_params=PARAMS,
        cost_estimate=cost(8 * 3 * work, 20 << 20),
    )(behind, orbitals, ion_potential, hxc_potential, kin)
    for index in range(6, grid):
        moved[index] = send(turns[index], moved[index], *([base] if index < 11 else []))
    own = pl.pallas_call(
        functools.partial(share_kernel, sizes),
        in_specs=[vmem],
        out_specs=vmem,
        out_shape=shape(share * length, LANES),
        compiler_params=PARAMS,
        cost_estimate=cost(0, 2 << 20),
    )(shared)
    other = lax.ppermute(own, "band", [(0, 1), (1, 0)])
    along = pl.pallas_call(
        functools.partial(along_kernel, sizes, steps, turns),
        grid=(steps,),
        in_specs=[smem] + [whole(mixed_rows, LANES)] * grid + [square],
        out_specs=pl.BlockSpec((rows // steps * length, 2 * LANES), lambda i: (i, 0)),
        out_shape=shape(rows * length, 2 * LANES),
        scratch_shapes=[pltpu.VMEM((rows // steps, 2, length, LANES), jnp.float32)],
        compiler_params=PARAMS,
        cost_estimate=cost(2 * 3 * work, 8 << 20),
    )(place, *moved, kin)
    mixed = [send(turn, piece) for turn, piece in zip(turns, mixed)]
    half_spec = pl.BlockSpec((rows // steps * length, LANES), lambda i: (i % (steps // 2), 0))
    update = pl.pallas_call(
        functools.partial(update_kernel, sizes, steps, turns),
        grid=(steps,),
        in_specs=[
            smem,
            pl.BlockSpec((rows // steps * length, 2 * LANES), lambda i: (i, 0)),
            half_spec,
            half_spec,
            square,
        ]
        + [whole(mixed_rows, LANES)] * grid,
        out_specs=whole(2 * field, LANES),
        out_shape=shape(2 * field, LANES),
        scratch_shapes=[pltpu.VMEM((rows // steps, 2, length, LANES), jnp.float32)],
        compiler_params=PARAMS,
        cost_estimate=cost(2 * 3 * work, 14 << 20),
    )(place, along, own, other, kin, *mixed)
    update = swap(update)

    fresh, upper, lower, spectrum = pl.pallas_call(
        functools.partial(fresh_kernel, sizes, bunch),
        grid=(planes // bunch,),
        in_specs=[smem, vmem, pair_spec, table_spec],
        out_specs=[
            psi_spec,
            half_rows,
            half_rows,
            whole(spec_rows, LANES),
        ],
        out_shape=[
            shape(*orbitals.shape),
            shape(field // 2, LANES),
            shape(field // 2, LANES),
            shape(spec_rows, LANES),
        ],
        scratch_shapes=scratch(4),
        compiler_params=PARAMS,
        cost_estimate=cost(2 * 6 * work, 16 << 20),
    )(occupations, update, base, tables)
    upper_other = lax.ppermute(upper, "band", [(0, 1), (1, 0)])
    lower_other = lax.ppermute(lower, "band", [(0, 1), (1, 0)])

    spectrum = swap_all(spectrum)
    cells_np = squares_np[:, None] + squares_np[None, :]
    half = length // 2
    cells_np = np.concatenate(
        [cells_np[:, :LANES], np.concatenate([cells_np[:half, LANES:], cells_np[half:, LANES:]], axis=1)]
    )
    device = lax.axis_index("band") * grid + lax.axis_index("grid")
    cells = lax.dynamic_slice_in_dim(jnp.asarray(cells_np), device * share, share, axis=0)
    first, second = pl.pallas_call(
        functools.partial(filter_kernel, sizes),
        in_specs=[vmem] * 3,
        out_specs=[vmem] * 2,
        out_shape=[shape(part_rows, LANES)] * 2,
        scratch_shapes=[pltpu.VMEM((length, share * LANES), jnp.float32)],
        compiler_params=SMALL,
        cost_estimate=cost(6 * work, 5 << 20),
    )(spectrum, cells.reshape(1, share * LANES), tables)

    def last_part(part, near, far, made):
        cells_spec = pl.BlockSpec((bunch * cell_rows // 2, LANES), lambda i: (i + part * groups, 0))
        return pl.pallas_call(
            functools.partial(last_kernel, sizes, bunch),
            grid=(groups,),
            in_specs=[smem, vmem, vmem]
            + [cells_spec] * 4
            + [table_spec]
            + [pl.BlockSpec(memory_space=pl.ANY)] * len(made),
            out_specs=pl.BlockSpec((bunch, length, length), lambda i: (i + part * groups, 0, 0)),
            out_shape=shape(planes, length, length),
            scratch_shapes=scratch(2),
            input_output_aliases={8: 0} if made else {},
            compiler_params=PARAMS,
            cost_estimate=cost(3 * work, 4 << 20),
        )(place, near, far, upper, lower, upper_other, lower_other, tables, *made)

    first, upper_other = lax.optimization_barrier((first, upper_other))
    near = swap(first)
    far = lax.ppermute(near, "band", [(0, 1), (1, 0)])
    second, lower_other = lax.optimization_barrier((second, lower_other))
    near_second = swap(second)
    far_second = lax.ppermute(near_second, "band", [(0, 1), (1, 0)])
    potential = last_part(0, near, far, [])
    potential = last_part(1, near_second, far_second, [potential])
    return (fresh, potential)


def local(orbitals, occupations, ion_potential, hxc_potential):
    length = orbitals.shape[-1]
    parts = 2 * lax.axis_size("grid") * LANES
    fits = lax.axis_size("grid") & (lax.axis_size("grid") - 1) == 0
    fits = fits and orbitals.shape[2] % 2 == 0 and length == LANES + LANES // 2 and lax.axis_size("band") == 2 and length * length % parts == 0
    path = packed_path if fits else general
    return path(orbitals, occupations, ion_potential, hxc_potential)


def solution(mesh):
    placed = (
        P("band", None, "grid", None, None),
        P("band"),
        P("grid", None, None),
        P("grid", None, None),
    )
    return jax.shard_map(
        local,
        mesh=mesh,
        in_specs=placed,
        out_specs=(P("band", None, "grid", None, None), P("grid", None, None)),
        check_vma=False,
    )
```

```python
import functools
import math

import jax
import jax.numpy as jnp
import numpy as np
from jax import lax
from jax.experimental import pallas as pl
from jax.experimental.pallas import tpu as pltpu
from jax.sharding import PartitionSpec as P

BESSEL_ZERO = 0.8462873527504802
BESSEL_ONE = 0.36884204609417703
BESSEL_TWO = 0.07581776248
XC_FACTOR = 0.98474502
PRECISION = lax.Precision.HIGH


def kinetic_matrix(length):
    idx = np.arange(length)
    freq = np.where(idx < length // 2, idx, idx - length).astype(np.float64)
    wave = np.cos(2.0 * math.pi * (np.outer(idx, idx) % length) / length)
    row = (wave @ (freq * freq)) / length * (2.0 / (3.0 * (length / 2) ** 2))
    return row[(idx[:, None] - idx[None, :]) % length].astype(np.float32)


def real_basis(length):
    half = length // 2
    idx = np.arange(length)
    order = np.concatenate([np.arange(half + 1), np.arange(1, half)])
    angle = 2.0 * math.pi * (np.outer(order, idx) % length) / length
    table = np.where((np.arange(length) <= half)[:, None], np.cos(angle), np.sin(angle))
    scale = np.where((order == 0) | (order == half), math.sqrt(1.0 / length), math.sqrt(2.0 / length))
    return (table * scale[:, None]).astype(np.float32), (order * order).astype(np.float32)


def dot(form, left, right):
    return jnp.einsum(form, left, right, precision=PRECISION)


def general(orbitals, occupations, ion_potential, hxc_potential):
    length = orbitals.shape[-1]
    planes = orbitals.shape[2]
    grid = lax.axis_size("grid")
    bands = lax.axis_size("band")
    cells = length * length
    columns = cells // grid
    share = cells // (grid * bands)
    kin = jnp.asarray(kinetic_matrix(length))
    kin_x = kin.reshape(length, grid, planes)
    basis_np, squares = real_basis(length)
    basis = jnp.asarray(basis_np)
    basis_x = basis.reshape(length, grid, planes)

    psi = orbitals[0]
    potential = ion_potential + hxc_potential

    def scatter(fields):
        parts = fields.reshape(fields.shape[0], planes, grid, columns).transpose(2, 1, 0, 3)
        return lax.all_to_all(parts, "grid", split_axis=0, concat_axis=0)

    def along_yz(field):
        return dot("cxyz,zk->cxyk", field, kin) + dot("cxyz,yk->cxkz", field, kin)

    moved = scatter(jnp.concatenate([psi, potential[None]], axis=0))
    local_kin = along_yz(psi) - psi
    applied = local_kin + potential * psi
    mixed = scatter(local_kin + applied)
    twice = along_yz(applied) - applied + potential * applied

    along = dot("ksp,spcn->ckn", kin_x, moved[:, :, :2])
    again = dot("ksp,spcn->ckn", kin_x, mixed) + dot("kx,cxn->ckn", kin, along)
    potential_cols = moved[:, :, 2].reshape(length, columns)
    again = again + potential_cols * along
    turned = jnp.stack([along[1], -along[0]])
    update = 2.0 * BESSEL_ONE * turned - 4.0 * BESSEL_TWO * again
    update = update.reshape(2, grid, planes, columns).transpose(1, 2, 0, 3)
    update = lax.all_to_all(update, "grid", split_axis=0, concat_axis=0)
    update = update.transpose(2, 1, 0, 3).reshape(psi.shape)

    turned = jnp.stack([applied[1], -applied[0]])
    fresh = (
        (BESSEL_ZERO + 2.0 * BESSEL_TWO) * psi
        + 2.0 * BESSEL_ONE * turned
        - 4.0 * BESSEL_TWO * twice
        + update
    )
    part = occupations[0] * (fresh[0] * fresh[0] + fresh[1] * fresh[1])
    density = lax.psum(part, "band")

    spectrum = dot("xyz,kz->xyk", part, basis)
    spectrum = dot("xyk,jy->xjk", spectrum, basis)
    spectrum = spectrum.reshape(planes, bands * grid, share).transpose(1, 0, 2)
    spectrum = lax.all_to_all(spectrum, ("band", "grid"), split_axis=0, concat_axis=0)
    spectrum = spectrum.reshape(bands, grid, planes, share).sum(axis=0)
    spectrum = dot("ksp,spn->kn", basis_x, spectrum)
    start = (lax.axis_index("band") * grid + lax.axis_index("grid")) * share
    cell = start + jnp.arange(share, dtype=jnp.int32)
    table = jnp.asarray(squares)
    total = table[:, None] + (table[cell // length] + table[cell % length])[None, :]
    kernel = jnp.where(total > 0, length * math.sqrt(length) / 16.0 / (total + 1.0), 0.0)
    spectrum = dot("kx,kn->xn", basis, kernel * spectrum)
    spectrum = spectrum.reshape(1, grid, planes, share)
    spectrum = jnp.broadcast_to(spectrum, (bands, grid, planes, share)).reshape(bands * grid, planes, share)
    spectrum = lax.all_to_all(spectrum, ("band", "grid"), split_axis=0, concat_axis=0)
    spectrum = spectrum.transpose(1, 0, 2).reshape(planes, length, length)
    spectrum = dot("xjk,jy->xyk", spectrum, basis)
    hartree = dot("xyk,kz->xyz", spectrum, basis)
    return (fresh[None], hartree - XC_FACTOR * jnp.cbrt(density))


LANES = 128


def product(left, right):
    return jnp.dot(left, right, precision=lax.Precision.HIGHEST, preferred_element_type=jnp.float32)


def split(array):
    high = array.astype(jnp.bfloat16)
    return high, (array - high.astype(jnp.float32)).astype(jnp.bfloat16)


def product_of_parts(left, right):
    total = jnp.dot(left[0], right[0], preferred_element_type=jnp.float32)
    total = total + jnp.dot(left[1], right[0], preferred_element_type=jnp.float32)
    return total + jnp.dot(left[0], right[1], preferred_element_type=jnp.float32)


def whole_tiles(rows):
    return -(-rows // 8) * 8


def chunk_rows(sizes):
    planes, _, rows, share = sizes
    return whole_tiles(planes * share)


def kinetic(plane, kin):
    plane = split(plane)
    return product_of_parts(plane, kin) + product_of_parts(kin, plane)


def pack(plane, packed):
    length = plane.shape[0]
    half = length // 2
    packed[:length, :] = plane[:, :LANES]
    packed[length:, :] = jnp.concatenate([plane[:half, LANES:], plane[half:, LANES:]], axis=1)


def unpack(packed, length):
    side = length - LANES
    tail = packed[length:, :]
    right = jnp.concatenate([tail[:, :side], tail[:, side:]], axis=0)
    return jnp.concatenate([packed[:length, :], right], axis=1)


def fill(out_ref, count, chunk, used):
    if used < chunk:

        @pl.when(pl.program_id(0) == 0)
        def _():
            for to in range(count):
                out_ref[pl.ds(to * chunk + used, chunk - used), :] = jnp.zeros((chunk - used, LANES), jnp.float32)


def potential_kernel(sizes, bunch, place_ref, ion_ref, hxc_ref, out_ref, packed):
    planes, grid, rows, share = sizes
    chunk = chunk_rows(sizes)
    band = place_ref[0] // grid
    fill(out_ref, grid, chunk, planes * share)
    for inner in range(bunch):
        plane = pl.program_id(0) * bunch + inner
        slot = packed.at[inner]
        pack(ion_ref[inner] + hxc_ref[inner], slot)
        for to in range(grid):
            start = to * rows + band * share
            out_ref[pl.ds(to * chunk + plane * share, share), :] = slot[pl.ds(start, share), :]


def pack_kernel(sizes, bunch, turns, place_ref, psi_ref, *refs):
    planes, grid, rows, share = sizes
    *out_refs, packed = refs
    mine = place_ref[0] % grid
    for inner in range(bunch):
        plane = pl.program_id(0) * bunch + inner
        for part in range(2):
            slot = packed.at[inner * 2 + part]
            pack(psi_ref[0, part, inner], slot)
            for turn, out_ref in zip(turns, out_refs):
                start = (mine ^ turn) * rows
                where = pl.ds(part * planes + plane, rows, stride=2 * planes)
                out_ref[where, :] = slot[pl.ds(start, rows), :]


def plane_kernel(sizes, bunch, turns, place_ref, psi_ref, ion_ref, hxc_ref, kin_ref, *refs):
    planes, grid, rows, share = sizes
    *out_refs, base_ref, packed = refs
    mine = place_ref[0] % grid
    kin = split(kin_ref[...])
    for inner in range(bunch):
        plane = pl.program_id(0) * bunch + inner
        potential = ion_ref[inner] + hxc_ref[inner]
        applied = []
        for part in range(2):
            field = psi_ref[0, part, inner]
            bare = kinetic(field, kin) - field
            applied.append(bare + potential * field)
            slot = packed.at[inner * 2 + part]
            pack(bare + applied[part], slot)
            for turn, out_ref in zip(turns, out_refs):
                start = (mine ^ turn) * rows
                where = pl.ds(part * planes + plane, rows, stride=2 * planes)
                out_ref[where, :] = slot[pl.ds(start, rows), :]
        for part in range(2):
            twice = kinetic(applied[part], kin) + (potential - 1.0) * applied[part]
            turned = applied[1] if part == 0 else -applied[0]
            base_ref[part, inner] = (
                (BESSEL_ZERO + 2.0 * BESSEL_TWO) * psi_ref[0, part, inner]
                + 2.0 * BESSEL_ONE * turned
                - 4.0 * BESSEL_TWO * twice
            )


def share_kernel(sizes, moved_ref, out_ref):
    planes, grid, rows, share = sizes
    length = planes * grid
    chunk = chunk_rows(sizes)
    for source in range(grid):
        for row in range(share):
            start = source * chunk + row
            out_ref[pl.ds(row * length + source * planes, planes), :] = moved_ref[pl.ds(start, planes, stride=share), :]


def along_kernel(sizes, steps, turns, place_ref, *refs):
    planes, grid, rows, share = sizes
    *moved_refs, kin_ref, out_ref, lines = refs
    length = planes * grid
    kin = split(kin_ref[...])
    for inner in range(rows // steps):
        slot = lines.at[inner]
        for turn, moved_ref in zip(turns, moved_refs):
            first = (place_ref[0] % grid ^ turn) * planes
            for part in range(2):
                start = (inner * 2 + part) * planes
                slot[part, pl.ds(first, planes), :] = moved_ref[start : start + planes, :]
        field = jnp.concatenate([slot[0], slot[1]], axis=1)
        out_ref[inner * length : (inner + 1) * length, :] = product_of_parts(kin, split(field))


def update_kernel(sizes, steps, turns, place_ref, along_ref, own_ref, other_ref, kin_ref, *refs):
    planes, grid, rows, share = sizes
    *mixed_refs, out_ref, lines = refs
    length = planes * grid
    kin = split(kin_ref[...])
    step = pl.program_id(0)
    mine_here = place_ref[0] // grid == step // (steps // 2)
    for inner in range(rows // steps):
        here = slice(inner * length, (inner + 1) * length)
        slot = lines.at[inner]
        for turn, mixed_ref in zip(turns, mixed_refs):
            first = (place_ref[0] % grid ^ turn) * planes
            for part in range(2):
                start = (inner * 2 + part) * planes
                slot[part, pl.ds(first, planes), :] = mixed_ref[start : start + planes, :]
        along = along_ref[here, :]
        again = product_of_parts(kin, split(jnp.concatenate([slot[0], slot[1]], axis=1) + along))
        potential = jnp.where(mine_here, own_ref[here, :], other_ref[here, :])
        for part in range(2):
            mine = along[:, part * LANES : (part + 1) * LANES]
            turned = along[:, LANES:] if part == 0 else -along[:, :LANES]
            twice = again[:, part * LANES : (part + 1) * LANES] + potential * mine
            slot[part] = 2.0 * BESSEL_ONE * turned - 4.0 * BESSEL_TWO * twice
            start = (inner * 2 + part) * planes
            for to in range(grid):
                out_ref[to, start : start + planes, :] = slot[part, to * planes : (to + 1) * planes, :]


def fresh_kernel(
    sizes, bunch, occ_ref, update_ref, base_ref, tables_ref, fresh_ref, upper_ref, lower_ref, out_ref, packed
):
    planes, grid, rows, share = sizes
    length = planes * grid
    chunk = chunk_rows(sizes)
    cell_rows = rows * grid
    half = cell_rows // 2
    fill(out_ref, 2 * grid, chunk, planes * share)
    means, parts = [], []
    for inner in range(bunch):
        plane = pl.program_id(0) * bunch + inner
        part_sum = None
        for part in range(2):
            slot = packed.at[inner * 4 + part]
            for source in range(grid):
                start = (source * rows * 2 + part) * planes + plane
                piece = update_ref[pl.ds(start, rows, stride=2 * planes), :]
                slot[pl.ds(source * rows, rows), :] = piece
            fresh = base_ref[part, inner] + unpack(slot, length)
            fresh_ref[0, part, inner] = fresh
            part_sum = fresh * fresh if part_sum is None else part_sum + fresh * fresh
        part_sum = occ_ref[0] * part_sum
        slot = packed.at[inner * 4 + 2]
        pack(part_sum, slot)
        upper_ref[inner * half : (inner + 1) * half, :] = slot[:half, :]
        lower_ref[inner * half : (inner + 1) * half, :] = slot[half:, :]
        means.append(jnp.sum(part_sum) * (1.0 / length**2))
        parts.append(part_sum - means[inner])
    basis, turn = split(tables_ref[0]), split(tables_ref[1])
    along_z = product_of_parts(split(jnp.concatenate(parts, axis=0)), turn)
    first = (lax.broadcasted_iota(jnp.int32, (length, length), axis) == 0 for axis in range(2))
    first = jnp.logical_and(*first)
    for inner in range(bunch):
        plane = pl.program_id(0) * bunch + inner
        spectrum = product_of_parts(basis, split(along_z[inner * length : (inner + 1) * length, :]))
        slot = packed.at[inner * 4 + 3]
        pack(spectrum + jnp.where(first, means[inner] * length, 0.0), slot)
        for to in range(2 * grid):
            out_ref[pl.ds(to * chunk + plane * share, share), :] = slot[pl.ds(to * share, share), :]


def filter_kernel(sizes, spec_ref, cells_ref, tables_ref, upper_ref, lower_ref, lines):
    planes, grid, rows, share = sizes
    length = planes * grid
    chunk = chunk_rows(sizes)

    def places():
        for source in range(grid):
            for row in range(share):
                first, second = (
                    pl.ds((band * grid + source) * chunk + row, planes, stride=share) for band in range(2)
                )
                here = (pl.ds(source * planes, planes), slice(row * LANES, (row + 1) * LANES))
                yield first, second, here

    for first, second, here in places():
        lines[here] = spec_ref[first, :] + spec_ref[second, :]
    index = lax.broadcasted_iota(jnp.int32, lines.shape, 0)
    order = jnp.where(index <= length // 2, index, index - length // 2).astype(jnp.float32)
    total = order * order + cells_ref[...]
    scale = length * math.sqrt(length) / 16.0
    kernel = jnp.where(total > 0.0, scale / (total + 1.0), 0.0)
    field = kernel * product(tables_ref[0], lines[...])
    lines[...] = product_of_parts(split(tables_ref[1]), split(field))
    some = planes // 2
    chunk = whole_tiles(some * share)
    for part, out_ref in enumerate((upper_ref, lower_ref)):
        for source in range(grid):
            for row in range(share):
                piece = lines[pl.ds(source * planes + part * some, some), row * LANES : (row + 1) * LANES]
                out_ref[pl.ds(source * chunk + row, some, stride=share), :] = piece
            if some * share < chunk:
                rest = chunk - some * share
                out_ref[pl.ds(source * chunk + some * share, rest), :] = jnp.zeros((rest, LANES), jnp.float32)


def last_kernel(
    sizes, bunch, place_ref, near_ref, far_ref, upper_ref, lower_ref, upper_other, lower_other, tables_ref, *refs
):
    planes, grid, rows, share = sizes
    out_ref, packed = refs[-2:]
    length = planes * grid
    half = rows * grid // 2
    chunk = whole_tiles(planes // 2 * share)
    turn, basis = split(tables_ref[1]), split(tables_ref[0])
    band = place_ref[0] // grid
    lines = []
    for inner in range(bunch):
        plane = pl.program_id(0) * bunch + inner
        slot = packed.at[inner * 2]
        for part, spec_ref in ((band, near_ref), (1 - band, far_ref)):
            side = slot.at[pl.ds(pl.multiple_of(part * half, 8), half), :]
            for source in range(grid):
                start = source * chunk + plane * share
                side[pl.ds(source * share, share), :] = spec_ref[pl.ds(start, share), :]
        lines.append(product_of_parts(turn, split(unpack(slot, length))))
    hartree = product_of_parts(split(jnp.concatenate(lines, axis=0)), basis)
    for inner in range(bunch):
        slot = packed.at[inner * 2 + 1]
        here = slice(inner * half, (inner + 1) * half)
        slot[:half, :] = upper_ref[here, :] + upper_other[here, :]
        slot[half:, :] = lower_ref[here, :] + lower_other[here, :]
        root = jnp.exp(jnp.log(unpack(slot, length)) * (1.0 / 3.0))
        out_ref[inner] = hartree[inner * length : (inner + 1) * length, :] - XC_FACTOR * root


def shape(*dims):
    return jax.ShapeDtypeStruct(dims, jnp.float32)


def whole(*dims):
    return pl.BlockSpec(dims, lambda *_: (0,) * len(dims))


SMALL = pltpu.CompilerParams(vmem_limit_bytes=24 << 20)
PARAMS = pltpu.CompilerParams(vmem_limit_bytes=54 << 20)


def cost(flops, moved):
    return pl.CostEstimate(flops=flops, bytes_accessed=moved, transcendentals=0)


def turn_order(grid):
    order = [0]
    for near in range(grid // 2):
        order += [near, near + grid // 2] if near else [grid // 2]
    return order


def packed_path(orbitals, occupations, ion_potential, hxc_potential):
    length = orbitals.shape[-1]
    planes = orbitals.shape[2]
    grid = lax.axis_size("grid")
    cell_rows = length * length // LANES
    rows = cell_rows // grid
    share = rows // 2
    sizes = (planes, grid, rows, share)
    field = planes * cell_rows
    work = 2 * planes * length**3
    place = lax.axis_index(("band", "grid")).astype(jnp.int32).reshape(1)
    kin = jnp.asarray(kinetic_matrix(length))
    basis_np, squares_np = real_basis(length)
    tables = jnp.asarray(np.stack([basis_np, basis_np.T]))
    smem = pl.BlockSpec(memory_space=pltpu.SMEM)
    vmem = pl.BlockSpec(memory_space=pltpu.VMEM)
    some = planes // 2
    bunch = next(count for count in (3, 2, 1) if some % count == 0)
    groups = some // bunch
    psi_spec = pl.BlockSpec((1, 2, bunch, length, length), lambda i: (0, 0, i, 0, 0))
    plane_spec = pl.BlockSpec((bunch, length, length), lambda i: (i, 0, 0))
    pair_spec = pl.BlockSpec((2, bunch, length, length), lambda i: (0, i, 0, 0))
    half_rows = pl.BlockSpec((bunch * cell_rows // 2, LANES), lambda i: (i, 0))
    part_rows = grid * whole_tiles(some * share)
    square = whole(length, length)
    table_spec = whole(2, length, length)

    def scratch(count):
        return [pltpu.VMEM((count * bunch, cell_rows, LANES), jnp.float32)]

    line = []

    def send(turn, piece, *gates):
        if not turn:
            return piece
        if len(line) >= 5:
            gates += (line[-5],)
        if gates:
            piece = lax.optimization_barrier((piece, *gates))[0]
        line.append(lax.ppermute(piece, "grid", [(spot, spot ^ turn) for spot in range(grid)]))
        return line[-1]

    def swap(array):
        flat = array.reshape(grid, -1, LANES)
        return lax.all_to_all(flat, "grid", split_axis=0, concat_axis=0).reshape(array.shape)

    def swap_all(array):
        flat = array.reshape(2 * grid, -1, LANES)
        return lax.all_to_all(flat, ("band", "grid"), split_axis=0, concat_axis=0).reshape(array.shape)

    turns = turn_order(grid)
    spec_rows = 2 * grid * chunk_rows(sizes)
    mixed_rows = 2 * planes * rows
    steps = 6 if rows % 6 == 0 and share % (rows // 6) == 0 else 2
    step_spec = pl.BlockSpec((mixed_rows // steps, LANES), lambda i: (i, 0))
    shared = pl.pallas_call(
        functools.partial(potential_kernel, sizes, bunch),
        grid=(planes // bunch,),
        in_specs=[smem, plane_spec, plane_spec],
        out_specs=whole(spec_rows // 2, LANES),
        out_shape=shape(spec_rows // 2, LANES),
        scratch_shapes=scratch(1),
        compiler_params=PARAMS,
        cost_estimate=cost(0, 6 << 20),
    )(place, ion_potential, hxc_potential)
    place, shared = lax.optimization_barrier((place, shared))
    shared = swap(shared)
    moved = pl.pallas_call(
        functools.partial(pack_kernel, sizes, bunch, turns),
        grid=(planes // bunch,),
        in_specs=[smem, psi_spec],
        out_specs=[whole(mixed_rows, LANES)] * grid,
        out_shape=[shape(mixed_rows, LANES)] * grid,
        scratch_shapes=scratch(2),
        compiler_params=PARAMS,
        cost_estimate=cost(0, 8 << 20),
    )(place, orbitals)
    moved = [send(turn, piece) for turn, piece in zip(turns[:6], moved[:6])] + list(moved[6:])
    behind = lax.optimization_barrier((place, line[1]))[0]
    *mixed, base = pl.pallas_call(
        functools.partial(plane_kernel, sizes, bunch, turns),
        grid=(planes // bunch,),
        in_specs=[smem, psi_spec, plane_spec, plane_spec, square],
        out_specs=[whole(mixed_rows, LANES)] * grid + [pair_spec],
        out_shape=[shape(mixed_rows, LANES)] * grid + [shape(2, planes, length, length)],
        scratch_shapes=scratch(2),
        compiler_params=PARAMS,
        cost_estimate=cost(8 * 3 * work, 20 << 20),
    )(behind, orbitals, ion_potential, hxc_potential, kin)
    for index in range(6, grid):
        moved[index] = send(turns[index], moved[index], *([base] if index < 11 else []))
    own = pl.pallas_call(
        functools.partial(share_kernel, sizes),
        in_specs=[vmem],
        out_specs=vmem,
        out_shape=shape(share * length, LANES),
        compiler_params=PARAMS,
        cost_estimate=cost(0, 2 << 20),
    )(shared)
    other = lax.ppermute(own, "band", [(0, 1), (1, 0)])
    along = pl.pallas_call(
        functools.partial(along_kernel, sizes, steps, turns),
        grid=(steps,),
        in_specs=[smem] + [step_spec] * grid + [square],
        out_specs=pl.BlockSpec((rows // steps * length, 2 * LANES), lambda i: (i, 0)),
        out_shape=shape(rows * length, 2 * LANES),
        scratch_shapes=[pltpu.VMEM((rows // steps, 2, length, LANES), jnp.float32)],
        compiler_params=PARAMS,
        cost_estimate=cost(2 * 3 * work, 8 << 20),
    )(place, *moved, kin)
    mixed = [send(turn, piece) for turn, piece in zip(turns, mixed)]
    half_spec = pl.BlockSpec((rows // steps * length, LANES), lambda i: (i % (steps // 2), 0))
    update = pl.pallas_call(
        functools.partial(update_kernel, sizes, steps, turns),
        grid=(steps,),
        in_specs=[
            smem,
            pl.BlockSpec((rows // steps * length, 2 * LANES), lambda i: (i, 0)),
            half_spec,
            half_spec,
            square,
        ]
        + [step_spec] * grid,
        out_specs=pl.BlockSpec((grid, mixed_rows // steps, LANES), lambda i: (0, i, 0)),
        out_shape=shape(grid, mixed_rows, LANES),
        scratch_shapes=[pltpu.VMEM((rows // steps, 2, length, LANES), jnp.float32)],
        compiler_params=PARAMS,
        cost_estimate=cost(2 * 3 * work, 14 << 20),
    )(place, along, own, other, kin, *mixed)
    update = swap(update).reshape(2 * field, LANES)

    fresh, upper, lower, spectrum = pl.pallas_call(
        functools.partial(fresh_kernel, sizes, bunch),
        grid=(planes // bunch,),
        in_specs=[smem, vmem, pair_spec, table_spec],
        out_specs=[
            psi_spec,
            half_rows,
            half_rows,
            whole(spec_rows, LANES),
        ],
        out_shape=[
            shape(*orbitals.shape),
            shape(field // 2, LANES),
            shape(field // 2, LANES),
            shape(spec_rows, LANES),
        ],
        scratch_shapes=scratch(4),
        compiler_params=PARAMS,
        cost_estimate=cost(2 * 6 * work, 16 << 20),
    )(occupations, update, base, tables)
    upper_other = lax.ppermute(upper, "band", [(0, 1), (1, 0)])
    lower_other = lax.ppermute(lower, "band", [(0, 1), (1, 0)])

    spectrum = swap_all(spectrum)
    cells_np = squares_np[:, None] + squares_np[None, :]
    half = length // 2
    cells_np = np.concatenate(
        [cells_np[:, :LANES], np.concatenate([cells_np[:half, LANES:], cells_np[half:, LANES:]], axis=1)]
    )
    device = lax.axis_index("band") * grid + lax.axis_index("grid")
    cells = lax.dynamic_slice_in_dim(jnp.asarray(cells_np), device * share, share, axis=0)
    first, second = pl.pallas_call(
        functools.partial(filter_kernel, sizes),
        in_specs=[vmem] * 3,
        out_specs=[vmem] * 2,
        out_shape=[shape(part_rows, LANES)] * 2,
        scratch_shapes=[pltpu.VMEM((length, share * LANES), jnp.float32)],
        compiler_params=SMALL,
        cost_estimate=cost(6 * work, 5 << 20),
    )(spectrum, cells.reshape(1, share * LANES), tables)

    def last_part(part, near, far, made):
        cells_spec = pl.BlockSpec((bunch * cell_rows // 2, LANES), lambda i: (i + part * groups, 0))
        return pl.pallas_call(
            functools.partial(last_kernel, sizes, bunch),
            grid=(groups,),
            in_specs=[smem, vmem, vmem]
            + [cells_spec] * 4
            + [table_spec]
            + [pl.BlockSpec(memory_space=pl.ANY)] * len(made),
            out_specs=pl.BlockSpec((bunch, length, length), lambda i: (i + part * groups, 0, 0)),
            out_shape=shape(planes, length, length),
            scratch_shapes=scratch(2),
            input_output_aliases={8: 0} if made else {},
            compiler_params=PARAMS,
            cost_estimate=cost(3 * work, 4 << 20),
        )(place, near, far, upper, lower, upper_other, lower_other, tables, *made)

    first, upper_other = lax.optimization_barrier((first, upper_other))
    near = swap(first)
    far = lax.ppermute(near, "band", [(0, 1), (1, 0)])
    second, lower_other = lax.optimization_barrier((second, lower_other))
    near_second = swap(second)
    far_second = lax.ppermute(near_second, "band", [(0, 1), (1, 0)])
    potential = last_part(0, near, far, [])
    potential = last_part(1, near_second, far_second, [potential])
    return (fresh, potential)


def local(orbitals, occupations, ion_potential, hxc_potential):
    length = orbitals.shape[-1]
    parts = 2 * lax.axis_size("grid") * LANES
    fits = lax.axis_size("grid") & (lax.axis_size("grid") - 1) == 0
    fits = fits and orbitals.shape[2] % 2 == 0 and length == LANES + LANES // 2 and lax.axis_size("band") == 2 and length * length % parts == 0
    path = packed_path if fits else general
    return path(orbitals, occupations, ion_potential, hxc_potential)


def solution(mesh):
    placed = (
        P("band", None, "grid", None, None),
        P("band"),
        P("grid", None, None),
        P("grid", None, None),
    )
    return jax.shard_map(
        local,
        mesh=mesh,
        in_specs=placed,
        out_specs=(P("band", None, "grid", None, None), P("grid", None, None)),
        check_vma=False,
    )
```

```python
import functools
import math

import jax
import jax.numpy as jnp
import numpy as np
from jax import lax
from jax.experimental import pallas as pl
from jax.experimental.pallas import tpu as pltpu
from jax.sharding import PartitionSpec as P

BESSEL_ZERO = 0.8462873527504802
BESSEL_ONE = 0.36884204609417703
BESSEL_TWO = 0.07581776248
XC_FACTOR = 0.98474502
PRECISION = lax.Precision.HIGH


def kinetic_matrix(length):
    idx = np.arange(length)
    freq = np.where(idx < length // 2, idx, idx - length).astype(np.float64)
    wave = np.cos(2.0 * math.pi * (np.outer(idx, idx) % length) / length)
    row = (wave @ (freq * freq)) / length * (2.0 / (3.0 * (length / 2) ** 2))
    return row[(idx[:, None] - idx[None, :]) % length].astype(np.float32)


def real_basis(length):
    half = length // 2
    idx = np.arange(length)
    order = np.concatenate([np.arange(half + 1), np.arange(1, half)])
    angle = 2.0 * math.pi * (np.outer(order, idx) % length) / length
    table = np.where((np.arange(length) <= half)[:, None], np.cos(angle), np.sin(angle))
    scale = np.where((order == 0) | (order == half), math.sqrt(1.0 / length), math.sqrt(2.0 / length))
    return (table * scale[:, None]).astype(np.float32), (order * order).astype(np.float32)


def dot(form, left, right):
    return jnp.einsum(form, left, right, precision=PRECISION)


def general(orbitals, occupations, ion_potential, hxc_potential):
    length = orbitals.shape[-1]
    planes = orbitals.shape[2]
    grid = lax.axis_size("grid")
    bands = lax.axis_size("band")
    cells = length * length
    columns = cells // grid
    share = cells // (grid * bands)
    kin = jnp.asarray(kinetic_matrix(length))
    kin_x = kin.reshape(length, grid, planes)
    basis_np, squares = real_basis(length)
    basis = jnp.asarray(basis_np)
    basis_x = basis.reshape(length, grid, planes)

    psi = orbitals[0]
    potential = ion_potential + hxc_potential

    def scatter(fields):
        parts = fields.reshape(fields.shape[0], planes, grid, columns).transpose(2, 1, 0, 3)
        return lax.all_to_all(parts, "grid", split_axis=0, concat_axis=0)

    def along_yz(field):
        return dot("cxyz,zk->cxyk", field, kin) + dot("cxyz,yk->cxkz", field, kin)

    moved = scatter(jnp.concatenate([psi, potential[None]], axis=0))
    local_kin = along_yz(psi) - psi
    applied = local_kin + potential * psi
    mixed = scatter(local_kin + applied)
    twice = along_yz(applied) - applied + potential * applied

    along = dot("ksp,spcn->ckn", kin_x, moved[:, :, :2])
    again = dot("ksp,spcn->ckn", kin_x, mixed) + dot("kx,cxn->ckn", kin, along)
    potential_cols = moved[:, :, 2].reshape(length, columns)
    again = again + potential_cols * along
    turned = jnp.stack([along[1], -along[0]])
    update = 2.0 * BESSEL_ONE * turned - 4.0 * BESSEL_TWO * again
    update = update.reshape(2, grid, planes, columns).transpose(1, 2, 0, 3)
    update = lax.all_to_all(update, "grid", split_axis=0, concat_axis=0)
    update = update.transpose(2, 1, 0, 3).reshape(psi.shape)

    turned = jnp.stack([applied[1], -applied[0]])
    fresh = (
        (BESSEL_ZERO + 2.0 * BESSEL_TWO) * psi
        + 2.0 * BESSEL_ONE * turned
        - 4.0 * BESSEL_TWO * twice
        + update
    )
    part = occupations[0] * (fresh[0] * fresh[0] + fresh[1] * fresh[1])
    density = lax.psum(part, "band")

    spectrum = dot("xyz,kz->xyk", part, basis)
    spectrum = dot("xyk,jy->xjk", spectrum, basis)
    spectrum = spectrum.reshape(planes, bands * grid, share).transpose(1, 0, 2)
    spectrum = lax.all_to_all(spectrum, ("band", "grid"), split_axis=0, concat_axis=0)
    spectrum = spectrum.reshape(bands, grid, planes, share).sum(axis=0)
    spectrum = dot("ksp,spn->kn", basis_x, spectrum)
    start = (lax.axis_index("band") * grid + lax.axis_index("grid")) * share
    cell = start + jnp.arange(share, dtype=jnp.int32)
    table = jnp.asarray(squares)
    total = table[:, None] + (table[cell // length] + table[cell % length])[None, :]
    kernel = jnp.where(total > 0, length * math.sqrt(length) / 16.0 / (total + 1.0), 0.0)
    spectrum = dot("kx,kn->xn", basis, kernel * spectrum)
    spectrum = spectrum.reshape(1, grid, planes, share)
    spectrum = jnp.broadcast_to(spectrum, (bands, grid, planes, share)).reshape(bands * grid, planes, share)
    spectrum = lax.all_to_all(spectrum, ("band", "grid"), split_axis=0, concat_axis=0)
    spectrum = spectrum.transpose(1, 0, 2).reshape(planes, length, length)
    spectrum = dot("xjk,jy->xyk", spectrum, basis)
    hartree = dot("xyk,kz->xyz", spectrum, basis)
    return (fresh[None], hartree - XC_FACTOR * jnp.cbrt(density))


LANES = 128


def product(left, right):
    return jnp.dot(left, right, precision=lax.Precision.HIGHEST, preferred_element_type=jnp.float32)


def split(array):
    high = array.astype(jnp.bfloat16)
    return high, (array - high.astype(jnp.float32)).astype(jnp.bfloat16)


def product_of_parts(left, right):
    total = jnp.dot(left[0], right[0], preferred_element_type=jnp.float32)
    total = total + jnp.dot(left[1], right[0], preferred_element_type=jnp.float32)
    return total + jnp.dot(left[0], right[1], preferred_element_type=jnp.float32)


def whole_tiles(rows):
    return -(-rows // 8) * 8


def chunk_rows(sizes):
    planes, _, rows, share = sizes
    return whole_tiles(planes * share)


def kinetic(plane, kin):
    plane = split(plane)
    return product_of_parts(plane, kin) + product_of_parts(kin, plane)


def pack(plane, packed):
    length = plane.shape[0]
    half = length // 2
    packed[:length, :] = plane[:, :LANES]
    packed[length:, :] = jnp.concatenate([plane[:half, LANES:], plane[half:, LANES:]], axis=1)


def unpack(packed, length):
    side = length - LANES
    tail = packed[length:, :]
    right = jnp.concatenate([tail[:, :side], tail[:, side:]], axis=0)
    return jnp.concatenate([packed[:length, :], right], axis=1)


def fill(out_ref, count, chunk, used):
    if used < chunk:

        @pl.when(pl.program_id(0) == 0)
        def _():
            for to in range(count):
                out_ref[pl.ds(to * chunk + used, chunk - used), :] = jnp.zeros((chunk - used, LANES), jnp.float32)


def potential_kernel(sizes, bunch, place_ref, ion_ref, hxc_ref, out_ref, packed):
    planes, grid, rows, share = sizes
    chunk = chunk_rows(sizes)
    band = place_ref[0] // grid
    fill(out_ref, grid, chunk, planes * share)
    for inner in range(bunch):
        plane = pl.program_id(0) * bunch + inner
        slot = packed.at[inner]
        pack(ion_ref[inner] + hxc_ref[inner], slot)
        for to in range(grid):
            start = to * rows + band * share
            out_ref[pl.ds(to * chunk + plane * share, share), :] = slot[pl.ds(start, share), :]


def pack_kernel(sizes, bunch, turns, place_ref, psi_ref, *refs):
    planes, grid, rows, share = sizes
    *out_refs, packed = refs
    mine = place_ref[0] % grid
    for inner in range(bunch):
        plane = pl.program_id(0) * bunch + inner
        for part in range(2):
            slot = packed.at[inner * 2 + part]
            pack(psi_ref[0, part, inner], slot)
            for turn, out_ref in zip(turns, out_refs):
                start = (mine ^ turn) * rows
                out_ref[pl.ds((plane * 2 + part) * rows, rows), :] = slot[pl.ds(start, rows), :]


def plane_kernel(sizes, bunch, turns, place_ref, psi_ref, ion_ref, hxc_ref, kin_ref, *refs):
    planes, grid, rows, share = sizes
    *out_refs, base_ref, packed = refs
    mine = place_ref[0] % grid
    kin = split(kin_ref[...])
    for inner in range(bunch):
        plane = pl.program_id(0) * bunch + inner
        potential = ion_ref[inner] + hxc_ref[inner]
        applied = []
        for part in range(2):
            field = psi_ref[0, part, inner]
            bare = kinetic(field, kin) - field
            applied.append(bare + potential * field)
            slot = packed.at[inner * 2 + part]
            pack(bare + applied[part], slot)
            for turn, out_ref in zip(turns, out_refs):
                start = (mine ^ turn) * rows
                out_ref[pl.ds((plane * 2 + part) * rows, rows), :] = slot[pl.ds(start, rows), :]
        for part in range(2):
            twice = kinetic(applied[part], kin) + (potential - 1.0) * applied[part]
            turned = applied[1] if part == 0 else -applied[0]
            base_ref[part, inner] = (
                (BESSEL_ZERO + 2.0 * BESSEL_TWO) * psi_ref[0, part, inner]
                + 2.0 * BESSEL_ONE * turned
                - 4.0 * BESSEL_TWO * twice
            )


def share_kernel(sizes, place_ref, moved_ref, out_ref):
    planes, grid, rows, share = sizes
    length = planes * grid
    chunk = chunk_rows(sizes)
    for source in range(grid):
        for row in range(share):
            start = source * chunk + row
            first = row * length + (place_ref[0] % grid ^ source) * planes
            out_ref[pl.ds(first, planes), :] = moved_ref[pl.ds(start, planes, stride=share), :]


def along_kernel(sizes, steps, turns, *refs):
    planes, grid, rows, share = sizes
    *moved_refs, kin_ref, out_ref, lines = refs
    length = planes * grid
    kin = split(kin_ref[...])
    for inner in range(rows // steps):
        row = pl.program_id(0) * (rows // steps) + inner
        slot = lines.at[inner]
        for turn, moved_ref in zip(turns, moved_refs):
            here = slice(turn * planes, (turn + 1) * planes)
            for part in range(2):
                slot[part, here, :] = moved_ref[pl.ds(part * rows + row, planes, stride=2 * rows), :]
        field = jnp.concatenate([slot[0], slot[1]], axis=1)
        out_ref[inner * length : (inner + 1) * length, :] = product_of_parts(kin, split(field))


def update_kernel(sizes, steps, turns, place_ref, along_ref, own_ref, other_ref, kin_ref, *refs):
    planes, grid, rows, share = sizes
    *mixed_refs, out_ref, lines = refs
    length = planes * grid
    kin = split(kin_ref[...])
    step = pl.program_id(0)
    mine_here = place_ref[0] // grid == step // (steps // 2)
    for inner in range(rows // steps):
        row = step * (rows // steps) + inner
        here = slice(inner * length, (inner + 1) * length)
        slot = lines.at[inner]
        for turn, mixed_ref in zip(turns, mixed_refs):
            rest = slice(turn * planes, (turn + 1) * planes)
            for part in range(2):
                slot[part, rest, :] = mixed_ref[pl.ds(part * rows + row, planes, stride=2 * rows), :]
        along = along_ref[here, :]
        again = product_of_parts(kin, split(jnp.concatenate([slot[0], slot[1]], axis=1) + along))
        potential = jnp.where(mine_here, own_ref[here, :], other_ref[here, :])
        for part in range(2):
            mine = along[:, part * LANES : (part + 1) * LANES]
            turned = along[:, LANES:] if part == 0 else -along[:, :LANES]
            twice = again[:, part * LANES : (part + 1) * LANES] + potential * mine
            slot[part] = 2.0 * BESSEL_ONE * turned - 4.0 * BESSEL_TWO * twice
            for turn in range(grid):
                start = (place_ref[0] % grid ^ turn) * planes * 2 * rows + part * rows + row
                piece = slot[part, turn * planes : (turn + 1) * planes, :]
                out_ref[pl.ds(start, planes, stride=2 * rows), :] = piece


def fresh_kernel(
    sizes, bunch, occ_ref, update_ref, base_ref, tables_ref, fresh_ref, upper_ref, lower_ref, out_ref, packed
):
    planes, grid, rows, share = sizes
    length = planes * grid
    chunk = chunk_rows(sizes)
    cell_rows = rows * grid
    half = cell_rows // 2
    fill(out_ref, 2 * grid, chunk, planes * share)
    means, parts = [], []
    for inner in range(bunch):
        plane = pl.program_id(0) * bunch + inner
        part_sum = None
        for part in range(2):
            slot = packed.at[inner * 4 + part]
            for source in range(grid):
                start = ((source * planes + plane) * 2 + part) * rows
                slot[pl.ds(source * rows, rows), :] = update_ref[pl.ds(start, rows), :]
            fresh = base_ref[part, inner] + unpack(slot, length)
            fresh_ref[0, part, inner] = fresh
            part_sum = fresh * fresh if part_sum is None else part_sum + fresh * fresh
        part_sum = occ_ref[0] * part_sum
        slot = packed.at[inner * 4 + 2]
        pack(part_sum, slot)
        upper_ref[inner * half : (inner + 1) * half, :] = slot[:half, :]
        lower_ref[inner * half : (inner + 1) * half, :] = slot[half:, :]
        means.append(jnp.sum(part_sum) * (1.0 / length**2))
        parts.append(part_sum - means[inner])
    basis, turn = split(tables_ref[0]), split(tables_ref[1])
    along_z = product_of_parts(split(jnp.concatenate(parts, axis=0)), turn)
    first = (lax.broadcasted_iota(jnp.int32, (length, length), axis) == 0 for axis in range(2))
    first = jnp.logical_and(*first)
    for inner in range(bunch):
        plane = pl.program_id(0) * bunch + inner
        spectrum = product_of_parts(basis, split(along_z[inner * length : (inner + 1) * length, :]))
        slot = packed.at[inner * 4 + 3]
        pack(spectrum + jnp.where(first, means[inner] * length, 0.0), slot)
        for to in range(2 * grid):
            out_ref[pl.ds(to * chunk + plane * share, share), :] = slot[pl.ds(to * share, share), :]


def filter_kernel(sizes, spec_ref, cells_ref, tables_ref, upper_ref, lower_ref, lines):
    planes, grid, rows, share = sizes
    length = planes * grid
    chunk = chunk_rows(sizes)

    def places():
        for source in range(grid):
            for row in range(share):
                first, second = (
                    pl.ds((band * grid + source) * chunk + row, planes, stride=share) for band in range(2)
                )
                here = (pl.ds(source * planes, planes), slice(row * LANES, (row + 1) * LANES))
                yield first, second, here

    for first, second, here in places():
        lines[here] = spec_ref[first, :] + spec_ref[second, :]
    index = lax.broadcasted_iota(jnp.int32, lines.shape, 0)
    order = jnp.where(index <= length // 2, index, index - length // 2).astype(jnp.float32)
    total = order * order + cells_ref[...]
    scale = length * math.sqrt(length) / 16.0
    kernel = jnp.where(total > 0.0, scale / (total + 1.0), 0.0)
    field = kernel * product(tables_ref[0], lines[...])
    lines[...] = product_of_parts(split(tables_ref[1]), split(field))
    some = planes // 2
    chunk = whole_tiles(some * share)
    for part, out_ref in enumerate((upper_ref, lower_ref)):
        for source in range(grid):
            for row in range(share):
                piece = lines[pl.ds(source * planes + part * some, some), row * LANES : (row + 1) * LANES]
                out_ref[pl.ds(source * chunk + row, some, stride=share), :] = piece
            if some * share < chunk:
                rest = chunk - some * share
                out_ref[pl.ds(source * chunk + some * share, rest), :] = jnp.zeros((rest, LANES), jnp.float32)


def last_kernel(
    sizes, bunch, place_ref, near_ref, far_ref, upper_ref, lower_ref, upper_other, lower_other, tables_ref, *refs
):
    planes, grid, rows, share = sizes
    out_ref, packed = refs[-2:]
    length = planes * grid
    half = rows * grid // 2
    chunk = whole_tiles(planes // 2 * share)
    turn, basis = split(tables_ref[1]), split(tables_ref[0])
    band = place_ref[0] // grid
    lines = []
    for inner in range(bunch):
        plane = pl.program_id(0) * bunch + inner
        slot = packed.at[inner * 2]
        for part, spec_ref in ((band, near_ref), (1 - band, far_ref)):
            side = slot.at[pl.ds(pl.multiple_of(part * half, 8), half), :]
            for source in range(grid):
                start = source * chunk + plane * share
                side[pl.ds(source * share, share), :] = spec_ref[pl.ds(start, share), :]
        lines.append(product_of_parts(turn, split(unpack(slot, length))))
    hartree = product_of_parts(split(jnp.concatenate(lines, axis=0)), basis)
    for inner in range(bunch):
        slot = packed.at[inner * 2 + 1]
        here = slice(inner * half, (inner + 1) * half)
        slot[:half, :] = upper_ref[here, :] + upper_other[here, :]
        slot[half:, :] = lower_ref[here, :] + lower_other[here, :]
        root = jnp.exp(jnp.log(unpack(slot, length)) * (1.0 / 3.0))
        out_ref[inner] = hartree[inner * length : (inner + 1) * length, :] - XC_FACTOR * root


def shape(*dims):
    return jax.ShapeDtypeStruct(dims, jnp.float32)


def whole(*dims):
    return pl.BlockSpec(dims, lambda *_: (0,) * len(dims))


SMALL = pltpu.CompilerParams(vmem_limit_bytes=24 << 20)
PARAMS = pltpu.CompilerParams(vmem_limit_bytes=54 << 20)


def cost(flops, moved):
    return pl.CostEstimate(flops=flops, bytes_accessed=moved, transcendentals=0)


def turn_order(grid):
    order = [0]
    for near in range(grid // 2):
        order += [near, near + grid // 2] if near else [grid // 2]
    return order


def packed_path(orbitals, occupations, ion_potential, hxc_potential):
    length = orbitals.shape[-1]
    planes = orbitals.shape[2]
    grid = lax.axis_size("grid")
    cell_rows = length * length // LANES
    rows = cell_rows // grid
    share = rows // 2
    sizes = (planes, grid, rows, share)
    field = planes * cell_rows
    work = 2 * planes * length**3
    place = lax.axis_index(("band", "grid")).astype(jnp.int32).reshape(1)
    kin_np = kinetic_matrix(length)
    kin = jnp.asarray(kin_np)
    blocks = kin_np.reshape(grid, planes, grid, planes)
    orders = [[spot ^ turn for turn in range(grid)] for spot in range(grid)]
    turned = np.stack([blocks[order][:, :, order].reshape(length, length) for order in orders])
    turned_kin = lax.dynamic_index_in_dim(jnp.asarray(turned), lax.axis_index("grid"), keepdims=False)
    basis_np, squares_np = real_basis(length)
    tables = jnp.asarray(np.stack([basis_np, basis_np.T]))
    smem = pl.BlockSpec(memory_space=pltpu.SMEM)
    vmem = pl.BlockSpec(memory_space=pltpu.VMEM)
    some = planes // 2
    bunch = next(count for count in (3, 2, 1) if some % count == 0)
    groups = some // bunch
    psi_spec = pl.BlockSpec((1, 2, bunch, length, length), lambda i: (0, 0, i, 0, 0))
    plane_spec = pl.BlockSpec((bunch, length, length), lambda i: (i, 0, 0))
    pair_spec = pl.BlockSpec((2, bunch, length, length), lambda i: (0, i, 0, 0))
    half_rows = pl.BlockSpec((bunch * cell_rows // 2, LANES), lambda i: (i, 0))
    part_rows = grid * whole_tiles(some * share)
    square = whole(length, length)
    table_spec = whole(2, length, length)

    def scratch(count):
        return [pltpu.VMEM((count * bunch, cell_rows, LANES), jnp.float32)]

    def send(turn, piece):
        if not turn:
            return piece
        return lax.ppermute(piece, "grid", [(spot, spot ^ turn) for spot in range(grid)])

    def hold(pieces, gates):
        late = lax.optimization_barrier((list(pieces[6:]), gates))[0]
        return list(pieces[:6]) + list(late)

    def swap(array):
        flat = array.reshape(grid, -1, LANES)
        return lax.all_to_all(flat, "grid", split_axis=0, concat_axis=0).reshape(array.shape)

    def swap_all(array):
        flat = array.reshape(2 * grid, -1, LANES)
        return lax.all_to_all(flat, ("band", "grid"), split_axis=0, concat_axis=0).reshape(array.shape)

    turns = turn_order(grid)
    first_turns = [0] * grid
    for rank, name in enumerate(sorted(range(grid - 1), key=str)):
        first_turns[name + 1] = turns[rank + 1]
    spec_rows = 2 * grid * chunk_rows(sizes)
    mixed_rows = 2 * planes * rows
    steps = 6 if rows % 6 == 0 and share % (rows // 6) == 0 else 2
    shared = pl.pallas_call(
        functools.partial(potential_kernel, sizes, bunch),
        grid=(planes // bunch,),
        in_specs=[smem, plane_spec, plane_spec],
        out_specs=whole(spec_rows // 2, LANES),
        out_shape=shape(spec_rows // 2, LANES),
        scratch_shapes=scratch(1),
        compiler_params=PARAMS,
        cost_estimate=cost(0, 6 << 20),
    )(place, ion_potential, hxc_potential)
    place, shared = lax.optimization_barrier((place, shared))
    shared = swap(shared)
    moved = pl.pallas_call(
        functools.partial(pack_kernel, sizes, bunch, first_turns),
        grid=(planes // bunch,),
        in_specs=[smem, psi_spec],
        out_specs=[whole(mixed_rows, LANES)] * grid,
        out_shape=[shape(mixed_rows, LANES)] * grid,
        scratch_shapes=scratch(2),
        compiler_params=PARAMS,
        cost_estimate=cost(0, 8 << 20),
    )(place, orbitals)
    *mixed, base = pl.pallas_call(
        functools.partial(plane_kernel, sizes, bunch, turns),
        grid=(planes // bunch,),
        in_specs=[smem, psi_spec, plane_spec, plane_spec, square],
        out_specs=[whole(mixed_rows, LANES)] * grid + [pair_spec],
        out_shape=[shape(mixed_rows, LANES)] * grid + [shape(2, planes, length, length)],
        scratch_shapes=scratch(2),
        compiler_params=PARAMS,
        cost_estimate=cost(8 * 3 * work, 20 << 20),
    )(place, orbitals, ion_potential, hxc_potential, kin)
    moved = [send(turn, piece) for turn, piece in zip(first_turns, moved)]
    own = pl.pallas_call(
        functools.partial(share_kernel, sizes),
        in_specs=[smem, vmem],
        out_specs=vmem,
        out_shape=shape(share * length, LANES),
        compiler_params=PARAMS,
        cost_estimate=cost(0, 2 << 20),
    )(place, shared)
    other = lax.ppermute(own, "band", [(0, 1), (1, 0)])
    along = pl.pallas_call(
        functools.partial(along_kernel, sizes, steps, first_turns),
        grid=(steps,),
        in_specs=[whole(mixed_rows, LANES)] * grid + [square],
        out_specs=pl.BlockSpec((rows // steps * length, 2 * LANES), lambda i: (i, 0)),
        out_shape=shape(rows * length, 2 * LANES),
        scratch_shapes=[pltpu.VMEM((rows // steps, 2, length, LANES), jnp.float32)],
        compiler_params=PARAMS,
        cost_estimate=cost(2 * 3 * work, 8 << 20),
    )(*moved, turned_kin)
    mixed = [send(turn, piece) for turn, piece in zip(turns, mixed)]
    half_spec = pl.BlockSpec((rows // steps * length, LANES), lambda i: (i % (steps // 2), 0))
    update = pl.pallas_call(
        functools.partial(update_kernel, sizes, steps, turns),
        grid=(steps,),
        in_specs=[
            smem,
            pl.BlockSpec((rows // steps * length, 2 * LANES), lambda i: (i, 0)),
            half_spec,
            half_spec,
            square,
        ]
        + [whole(mixed_rows, LANES)] * grid,
        out_specs=whole(2 * field, LANES),
        out_shape=shape(2 * field, LANES),
        scratch_shapes=[pltpu.VMEM((rows // steps, 2, length, LANES), jnp.float32)],
        compiler_params=PARAMS,
        cost_estimate=cost(2 * 3 * work, 14 << 20),
    )(place, along, own, other, turned_kin, *mixed)
    update = swap(update)

    fresh, upper, lower, spectrum = pl.pallas_call(
        functools.partial(fresh_kernel, sizes, bunch),
        grid=(planes // bunch,),
        in_specs=[smem, vmem, pair_spec, table_spec],
        out_specs=[
            psi_spec,
            half_rows,
            half_rows,
            whole(spec_rows, LANES),
        ],
        out_shape=[
            shape(*orbitals.shape),
            shape(field // 2, LANES),
            shape(field // 2, LANES),
            shape(spec_rows, LANES),
        ],
        scratch_shapes=scratch(4),
        compiler_params=PARAMS,
        cost_estimate=cost(2 * 6 * work, 16 << 20),
    )(occupations, update, base, tables)
    upper_other = lax.ppermute(upper, "band", [(0, 1), (1, 0)])
    lower_other = lax.ppermute(lower, "band", [(0, 1), (1, 0)])

    spectrum = swap_all(spectrum)
    cells_np = squares_np[:, None] + squares_np[None, :]
    half = length // 2
    cells_np = np.concatenate(
        [cells_np[:, :LANES], np.concatenate([cells_np[:half, LANES:], cells_np[half:, LANES:]], axis=1)]
    )
    device = lax.axis_index("band") * grid + lax.axis_index("grid")
    cells = lax.dynamic_slice_in_dim(jnp.asarray(cells_np), device * share, share, axis=0)
    first, second = pl.pallas_call(
        functools.partial(filter_kernel, sizes),
        in_specs=[vmem] * 3,
        out_specs=[vmem] * 2,
        out_shape=[shape(part_rows, LANES)] * 2,
        scratch_shapes=[pltpu.VMEM((length, share * LANES), jnp.float32)],
        compiler_params=SMALL,
        cost_estimate=cost(6 * work, 5 << 20),
    )(spectrum, cells.reshape(1, share * LANES), tables)

    def last_part(part, near, far, made):
        cells_spec = pl.BlockSpec((bunch * cell_rows // 2, LANES), lambda i: (i + part * groups, 0))
        return pl.pallas_call(
            functools.partial(last_kernel, sizes, bunch),
            grid=(groups,),
            in_specs=[smem, vmem, vmem]
            + [cells_spec] * 4
            + [table_spec]
            + [pl.BlockSpec(memory_space=pl.ANY)] * len(made),
            out_specs=pl.BlockSpec((bunch, length, length), lambda i: (i + part * groups, 0, 0)),
            out_shape=shape(planes, length, length),
            scratch_shapes=scratch(2),
            input_output_aliases={8: 0} if made else {},
            compiler_params=PARAMS,
            cost_estimate=cost(3 * work, 4 << 20),
        )(place, near, far, upper, lower, upper_other, lower_other, tables, *made)

    first, upper_other = lax.optimization_barrier((first, upper_other))
    near = swap(first)
    far = lax.ppermute(near, "band", [(0, 1), (1, 0)])
    second, lower_other = lax.optimization_barrier((second, lower_other))
    near_second = swap(second)
    far_second = lax.ppermute(near_second, "band", [(0, 1), (1, 0)])
    potential = last_part(0, near, far, [])
    potential = last_part(1, near_second, far_second, [potential])
    return (fresh, potential)


def local(orbitals, occupations, ion_potential, hxc_potential):
    length = orbitals.shape[-1]
    parts = 2 * lax.axis_size("grid") * LANES
    fits = lax.axis_size("grid") & (lax.axis_size("grid") - 1) == 0
    fits = fits and orbitals.shape[2] % 2 == 0 and length == LANES + LANES // 2 and lax.axis_size("band") == 2 and length * length % parts == 0
    path = packed_path if fits else general
    return path(orbitals, occupations, ion_potential, hxc_potential)


def solution(mesh):
    placed = (
        P("band", None, "grid", None, None),
        P("band"),
        P("grid", None, None),
        P("grid", None, None),
    )
    return jax.shard_map(
        local,
        mesh=mesh,
        in_specs=placed,
        out_specs=(P("band", None, "grid", None, None), P("grid", None, None)),
        check_vma=False,
    )
```

```python
import functools
import math

import jax
import jax.numpy as jnp
import numpy as np
from jax import lax
from jax.experimental import pallas as pl
from jax.experimental.pallas import tpu as pltpu
from jax.sharding import PartitionSpec as P

BESSEL_ZERO = 0.8462873527504802
BESSEL_ONE = 0.36884204609417703
BESSEL_TWO = 0.07581776248
XC_FACTOR = 0.98474502
PRECISION = lax.Precision.HIGH


def kinetic_matrix(length):
    idx = np.arange(length)
    freq = np.where(idx < length // 2, idx, idx - length).astype(np.float64)
    wave = np.cos(2.0 * math.pi * (np.outer(idx, idx) % length) / length)
    row = (wave @ (freq * freq)) / length * (2.0 / (3.0 * (length / 2) ** 2))
    return row[(idx[:, None] - idx[None, :]) % length].astype(np.float32)


def real_basis(length):
    half = length // 2
    idx = np.arange(length)
    order = np.concatenate([np.arange(half + 1), np.arange(1, half)])
    angle = 2.0 * math.pi * (np.outer(order, idx) % length) / length
    table = np.where((np.arange(length) <= half)[:, None], np.cos(angle), np.sin(angle))
    scale = np.where((order == 0) | (order == half), math.sqrt(1.0 / length), math.sqrt(2.0 / length))
    return (table * scale[:, None]).astype(np.float32), (order * order).astype(np.float32)


def dot(form, left, right):
    return jnp.einsum(form, left, right, precision=PRECISION)


def general(orbitals, occupations, ion_potential, hxc_potential):
    length = orbitals.shape[-1]
    planes = orbitals.shape[2]
    grid = lax.axis_size("grid")
    bands = lax.axis_size("band")
    cells = length * length
    columns = cells // grid
    share = cells // (grid * bands)
    kin = jnp.asarray(kinetic_matrix(length))
    kin_x = kin.reshape(length, grid, planes)
    basis_np, squares = real_basis(length)
    basis = jnp.asarray(basis_np)
    basis_x = basis.reshape(length, grid, planes)

    psi = orbitals[0]
    potential = ion_potential + hxc_potential

    def scatter(fields):
        parts = fields.reshape(fields.shape[0], planes, grid, columns).transpose(2, 1, 0, 3)
        return lax.all_to_all(parts, "grid", split_axis=0, concat_axis=0)

    def along_yz(field):
        return dot("cxyz,zk->cxyk", field, kin) + dot("cxyz,yk->cxkz", field, kin)

    moved = scatter(jnp.concatenate([psi, potential[None]], axis=0))
    local_kin = along_yz(psi) - psi
    applied = local_kin + potential * psi
    mixed = scatter(local_kin + applied)
    twice = along_yz(applied) - applied + potential * applied

    along = dot("ksp,spcn->ckn", kin_x, moved[:, :, :2])
    again = dot("ksp,spcn->ckn", kin_x, mixed) + dot("kx,cxn->ckn", kin, along)
    potential_cols = moved[:, :, 2].reshape(length, columns)
    again = again + potential_cols * along
    turned = jnp.stack([along[1], -along[0]])
    update = 2.0 * BESSEL_ONE * turned - 4.0 * BESSEL_TWO * again
    update = update.reshape(2, grid, planes, columns).transpose(1, 2, 0, 3)
    update = lax.all_to_all(update, "grid", split_axis=0, concat_axis=0)
    update = update.transpose(2, 1, 0, 3).reshape(psi.shape)

    turned = jnp.stack([applied[1], -applied[0]])
    fresh = (
        (BESSEL_ZERO + 2.0 * BESSEL_TWO) * psi
        + 2.0 * BESSEL_ONE * turned
        - 4.0 * BESSEL_TWO * twice
        + update
    )
    part = occupations[0] * (fresh[0] * fresh[0] + fresh[1] * fresh[1])
    density = lax.psum(part, "band")

    spectrum = dot("xyz,kz->xyk", part, basis)
    spectrum = dot("xyk,jy->xjk", spectrum, basis)
    spectrum = spectrum.reshape(planes, bands * grid, share).transpose(1, 0, 2)
    spectrum = lax.all_to_all(spectrum, ("band", "grid"), split_axis=0, concat_axis=0)
    spectrum = spectrum.reshape(bands, grid, planes, share).sum(axis=0)
    spectrum = dot("ksp,spn->kn", basis_x, spectrum)
    start = (lax.axis_index("band") * grid + lax.axis_index("grid")) * share
    cell = start + jnp.arange(share, dtype=jnp.int32)
    table = jnp.asarray(squares)
    total = table[:, None] + (table[cell // length] + table[cell % length])[None, :]
    kernel = jnp.where(total > 0, length * math.sqrt(length) / 16.0 / (total + 1.0), 0.0)
    spectrum = dot("kx,kn->xn", basis, kernel * spectrum)
    spectrum = spectrum.reshape(1, grid, planes, share)
    spectrum = jnp.broadcast_to(spectrum, (bands, grid, planes, share)).reshape(bands * grid, planes, share)
    spectrum = lax.all_to_all(spectrum, ("band", "grid"), split_axis=0, concat_axis=0)
    spectrum = spectrum.transpose(1, 0, 2).reshape(planes, length, length)
    spectrum = dot("xjk,jy->xyk", spectrum, basis)
    hartree = dot("xyk,kz->xyz", spectrum, basis)
    return (fresh[None], hartree - XC_FACTOR * jnp.cbrt(density))


LANES = 128


def product(left, right):
    return jnp.dot(left, right, precision=lax.Precision.HIGHEST, preferred_element_type=jnp.float32)


def split(array):
    high = array.astype(jnp.bfloat16)
    return high, (array - high.astype(jnp.float32)).astype(jnp.bfloat16)


def product_of_parts(left, right):
    total = jnp.dot(left[0], right[0], preferred_element_type=jnp.float32)
    total = total + jnp.dot(left[1], right[0], preferred_element_type=jnp.float32)
    return total + jnp.dot(left[0], right[1], preferred_element_type=jnp.float32)


def whole_tiles(rows):
    return -(-rows // 8) * 8


def chunk_rows(sizes):
    planes, _, rows, share = sizes
    return whole_tiles(planes * share)


def kinetic(plane, kin):
    plane = split(plane)
    return product_of_parts(plane, kin) + product_of_parts(kin, plane)


def pack(plane, packed):
    length = plane.shape[0]
    half = length // 2
    packed[:length, :] = plane[:, :LANES]
    packed[length:, :] = jnp.concatenate([plane[:half, LANES:], plane[half:, LANES:]], axis=1)


def unpack(packed, length):
    side = length - LANES
    tail = packed[length:, :]
    right = jnp.concatenate([tail[:, :side], tail[:, side:]], axis=0)
    return jnp.concatenate([packed[:length, :], right], axis=1)


def fill(out_ref, count, chunk, used):
    if used < chunk:

        @pl.when(pl.program_id(0) == 0)
        def _():
            for to in range(count):
                out_ref[pl.ds(to * chunk + used, chunk - used), :] = jnp.zeros((chunk - used, LANES), jnp.float32)


def potential_kernel(sizes, bunch, place_ref, ion_ref, hxc_ref, out_ref, packed):
    planes, grid, rows, share = sizes
    chunk = chunk_rows(sizes)
    band = place_ref[0] // grid
    fill(out_ref, grid, chunk, planes * share)
    for inner in range(bunch):
        plane = pl.program_id(0) * bunch + inner
        slot = packed.at[inner]
        pack(ion_ref[inner] + hxc_ref[inner], slot)
        for to in range(grid):
            start = to * rows + band * share
            out_ref[pl.ds(to * chunk + plane * share, share), :] = slot[pl.ds(start, share), :]


def pack_kernel(sizes, bunch, turns, place_ref, psi_ref, *refs):
    planes, grid, rows, share = sizes
    *out_refs, packed = refs
    mine = place_ref[0] % grid
    for inner in range(bunch):
        plane = pl.program_id(0) * bunch + inner
        for part in range(2):
            slot = packed.at[inner * 2 + part]
            pack(psi_ref[0, part, inner], slot)
            for turn, out_ref in zip(turns, out_refs):
                start = (mine ^ turn) * rows
                out_ref[pl.ds((plane * 2 + part) * rows, rows), :] = slot[pl.ds(start, rows), :]


def plane_kernel(sizes, bunch, turns, place_ref, psi_ref, ion_ref, hxc_ref, kin_ref, *refs):
    planes, grid, rows, share = sizes
    *out_refs, base_ref, packed = refs
    mine = place_ref[0] % grid
    kin = split(kin_ref[...])
    for inner in range(bunch):
        plane = pl.program_id(0) * bunch + inner
        potential = ion_ref[inner] + hxc_ref[inner]
        applied = []
        for part in range(2):
            field = psi_ref[0, part, inner]
            bare = kinetic(field, kin) - field
            applied.append(bare + potential * field)
            slot = packed.at[inner * 2 + part]
            pack(bare + applied[part], slot)
            for turn, out_ref in zip(turns, out_refs):
                start = (mine ^ turn) * rows
                out_ref[pl.ds((plane * 2 + part) * rows, rows), :] = slot[pl.ds(start, rows), :]
        for part in range(2):
            twice = kinetic(applied[part], kin) + (potential - 1.0) * applied[part]
            turned = applied[1] if part == 0 else -applied[0]
            base_ref[part, inner] = (
                (BESSEL_ZERO + 2.0 * BESSEL_TWO) * psi_ref[0, part, inner]
                + 2.0 * BESSEL_ONE * turned
                - 4.0 * BESSEL_TWO * twice
            )


def share_kernel(sizes, moved_ref, out_ref):
    planes, grid, rows, share = sizes
    length = planes * grid
    chunk = chunk_rows(sizes)
    for source in range(grid):
        for row in range(share):
            start = source * chunk + row
            out_ref[pl.ds(row * length + source * planes, planes), :] = moved_ref[pl.ds(start, planes, stride=share), :]


def along_kernel(sizes, steps, turns, place_ref, *refs):
    planes, grid, rows, share = sizes
    moved_refs, (own_ref, other_ref, kin_ref, out_ref, lines) = refs[:grid], refs[grid:]
    length = planes * grid
    kin = split(kin_ref[...])
    step = pl.program_id(0)
    mine_here = place_ref[0] // grid == step // (steps // 2)
    for inner in range(rows // steps):
        row = step * (rows // steps) + inner
        slot = lines.at[inner]
        for turn, moved_ref in zip(turns, moved_refs):
            first = (place_ref[0] % grid ^ turn) * planes
            for part in range(2):
                slot[part, pl.ds(first, planes), :] = moved_ref[pl.ds(part * rows + row, planes, stride=2 * rows), :]
        along = product_of_parts(kin, split(jnp.concatenate([slot[0], slot[1]], axis=1)))
        again = product_of_parts(kin, split(along))
        here = slice(inner * length, (inner + 1) * length)
        potential = jnp.where(mine_here, own_ref[here, :], other_ref[here, :])
        for part in range(2):
            lanes = slice(part * LANES, (part + 1) * LANES)
            turned = along[:, LANES:] if part == 0 else -along[:, :LANES]
            twice = again[:, lanes] + potential * along[:, lanes]
            out_ref[here, lanes] = 2.0 * BESSEL_ONE * turned - 4.0 * BESSEL_TWO * twice


def update_kernel(sizes, steps, turns, place_ref, along_ref, kin_ref, *refs):
    planes, grid, rows, share = sizes
    *mixed_refs, out_ref, lines = refs
    length = planes * grid
    kin = split(-4.0 * BESSEL_TWO * kin_ref[...])
    step = pl.program_id(0)
    for inner in range(rows // steps):
        row = step * (rows // steps) + inner
        slot = lines.at[inner]
        for turn, mixed_ref in zip(turns, mixed_refs):
            first = (place_ref[0] % grid ^ turn) * planes
            for part in range(2):
                slot[part, pl.ds(first, planes), :] = mixed_ref[pl.ds(part * rows + row, planes, stride=2 * rows), :]
        mixed = product_of_parts(kin, split(jnp.concatenate([slot[0], slot[1]], axis=1)))
        update = along_ref[inner * length : (inner + 1) * length, :] + mixed
        for part in range(2):
            where = pl.ds(part * rows + row, length, stride=2 * rows)
            out_ref[where, :] = update[:, part * LANES : (part + 1) * LANES]


def fresh_kernel(
    sizes, bunch, occ_ref, update_ref, base_ref, tables_ref, fresh_ref, upper_ref, lower_ref, out_ref, packed
):
    planes, grid, rows, share = sizes
    length = planes * grid
    chunk = chunk_rows(sizes)
    cell_rows = rows * grid
    half = cell_rows // 2
    fill(out_ref, 2 * grid, chunk, planes * share)
    means, parts = [], []
    for inner in range(bunch):
        plane = pl.program_id(0) * bunch + inner
        part_sum = None
        for part in range(2):
            slot = packed.at[inner * 4 + part]
            for source in range(grid):
                start = ((source * planes + plane) * 2 + part) * rows
                slot[pl.ds(source * rows, rows), :] = update_ref[pl.ds(start, rows), :]
            fresh = base_ref[part, inner] + unpack(slot, length)
            fresh_ref[0, part, inner] = fresh
            part_sum = fresh * fresh if part_sum is None else part_sum + fresh * fresh
        part_sum = occ_ref[0] * part_sum
        slot = packed.at[inner * 4 + 2]
        pack(part_sum, slot)
        upper_ref[inner * half : (inner + 1) * half, :] = slot[:half, :]
        lower_ref[inner * half : (inner + 1) * half, :] = slot[half:, :]
        means.append(jnp.sum(part_sum) * (1.0 / length**2))
        parts.append(part_sum - means[inner])
    basis, turn = split(tables_ref[0]), split(tables_ref[1])
    along_z = product_of_parts(split(jnp.concatenate(parts, axis=0)), turn)
    first = (lax.broadcasted_iota(jnp.int32, (length, length), axis) == 0 for axis in range(2))
    first = jnp.logical_and(*first)
    for inner in range(bunch):
        plane = pl.program_id(0) * bunch + inner
        spectrum = product_of_parts(basis, split(along_z[inner * length : (inner + 1) * length, :]))
        slot = packed.at[inner * 4 + 3]
        pack(spectrum + jnp.where(first, means[inner] * length, 0.0), slot)
        for to in range(2 * grid):
            out_ref[pl.ds(to * chunk + plane * share, share), :] = slot[pl.ds(to * share, share), :]


def filter_kernel(sizes, spec_ref, cells_ref, tables_ref, upper_ref, lower_ref, lines):
    planes, grid, rows, share = sizes
    length = planes * grid
    chunk = chunk_rows(sizes)

    def places():
        for source in range(grid):
            for row in range(share):
                first, second = (
                    pl.ds((band * grid + source) * chunk + row, planes, stride=share) for band in range(2)
                )
                here = (pl.ds(source * planes, planes), slice(row * LANES, (row + 1) * LANES))
                yield first, second, here

    for first, second, here in places():
        lines[here] = spec_ref[first, :] + spec_ref[second, :]
    index = lax.broadcasted_iota(jnp.int32, lines.shape, 0)
    order = jnp.where(index <= length // 2, index, index - length // 2).astype(jnp.float32)
    total = order * order + cells_ref[...]
    scale = length * math.sqrt(length) / 16.0
    kernel = jnp.where(total > 0.0, scale / (total + 1.0), 0.0)
    field = kernel * product(tables_ref[0], lines[...])
    lines[...] = product_of_parts(split(tables_ref[1]), split(field))
    some = planes // 2
    chunk = whole_tiles(some * share)
    for part, out_ref in enumerate((upper_ref, lower_ref)):
        for source in range(grid):
            for row in range(share):
                piece = lines[pl.ds(source * planes + part * some, some), row * LANES : (row + 1) * LANES]
                out_ref[pl.ds(source * chunk + row, some, stride=share), :] = piece
            if some * share < chunk:
                rest = chunk - some * share
                out_ref[pl.ds(source * chunk + some * share, rest), :] = jnp.zeros((rest, LANES), jnp.float32)


def last_kernel(
    sizes, bunch, place_ref, near_ref, far_ref, upper_ref, lower_ref, upper_other, lower_other, tables_ref, *refs
):
    planes, grid, rows, share = sizes
    out_ref, packed = refs[-2:]
    length = planes * grid
    half = rows * grid // 2
    chunk = whole_tiles(planes // 2 * share)
    turn, basis = split(tables_ref[1]), split(tables_ref[0])
    band = place_ref[0] // grid
    lines = []
    for inner in range(bunch):
        plane = pl.program_id(0) * bunch + inner
        slot = packed.at[inner * 2]
        for part, spec_ref in ((band, near_ref), (1 - band, far_ref)):
            side = slot.at[pl.ds(pl.multiple_of(part * half, 8), half), :]
            for source in range(grid):
                start = source * chunk + plane * share
                side[pl.ds(source * share, share), :] = spec_ref[pl.ds(start, share), :]
        lines.append(product_of_parts(turn, split(unpack(slot, length))))
    hartree = product_of_parts(split(jnp.concatenate(lines, axis=0)), basis)
    for inner in range(bunch):
        slot = packed.at[inner * 2 + 1]
        here = slice(inner * half, (inner + 1) * half)
        slot[:half, :] = upper_ref[here, :] + upper_other[here, :]
        slot[half:, :] = lower_ref[here, :] + lower_other[here, :]
        root = jnp.exp(jnp.log(unpack(slot, length)) * (1.0 / 3.0))
        out_ref[inner] = hartree[inner * length : (inner + 1) * length, :] - XC_FACTOR * root


def shape(*dims):
    return jax.ShapeDtypeStruct(dims, jnp.float32)


def whole(*dims):
    return pl.BlockSpec(dims, lambda *_: (0,) * len(dims))


SMALL = pltpu.CompilerParams(vmem_limit_bytes=24 << 20)
PARAMS = pltpu.CompilerParams(vmem_limit_bytes=54 << 20)


def cost(flops, moved):
    return pl.CostEstimate(flops=flops, bytes_accessed=moved, transcendentals=0)


def turn_order(grid):
    order = [0]
    for near in range(grid // 2):
        order += [near, near + grid // 2] if near else [grid // 2]
    return order


def packed_path(orbitals, occupations, ion_potential, hxc_potential):
    length = orbitals.shape[-1]
    planes = orbitals.shape[2]
    grid = lax.axis_size("grid")
    cell_rows = length * length // LANES
    rows = cell_rows // grid
    share = rows // 2
    sizes = (planes, grid, rows, share)
    field = planes * cell_rows
    work = 2 * planes * length**3
    place = lax.axis_index(("band", "grid")).astype(jnp.int32).reshape(1)
    kin = jnp.asarray(kinetic_matrix(length))
    basis_np, squares_np = real_basis(length)
    tables = jnp.asarray(np.stack([basis_np, basis_np.T]))
    smem = pl.BlockSpec(memory_space=pltpu.SMEM)
    vmem = pl.BlockSpec(memory_space=pltpu.VMEM)
    some = planes // 2
    bunch = next(count for count in (3, 2, 1) if some % count == 0)
    groups = some // bunch
    psi_spec = pl.BlockSpec((1, 2, bunch, length, length), lambda i: (0, 0, i, 0, 0))
    plane_spec = pl.BlockSpec((bunch, length, length), lambda i: (i, 0, 0))
    pair_spec = pl.BlockSpec((2, bunch, length, length), lambda i: (0, i, 0, 0))
    half_rows = pl.BlockSpec((bunch * cell_rows // 2, LANES), lambda i: (i, 0))
    part_rows = grid * whole_tiles(some * share)
    square = whole(length, length)
    table_spec = whole(2, length, length)

    def scratch(count):
        return [pltpu.VMEM((count * bunch, cell_rows, LANES), jnp.float32)]

    line = []

    def send(turn, piece, *gates):
        if not turn:
            return piece
        if len(line) >= 5:
            gates += (line[-5],)
        if gates:
            piece = lax.optimization_barrier((piece, *gates))[0]
        line.append(lax.ppermute(piece, "grid", [(spot, spot ^ turn) for spot in range(grid)]))
        return line[-1]

    def swap(array):
        flat = array.reshape(grid, -1, LANES)
        return lax.all_to_all(flat, "grid", split_axis=0, concat_axis=0).reshape(array.shape)

    def swap_all(array):
        flat = array.reshape(2 * grid, -1, LANES)
        return lax.all_to_all(flat, ("band", "grid"), split_axis=0, concat_axis=0).reshape(array.shape)

    turns = turn_order(grid)
    spec_rows = 2 * grid * chunk_rows(sizes)
    mixed_rows = 2 * planes * rows
    steps = 6 if rows % 6 == 0 and share % (rows // 6) == 0 else 2
    moved = pl.pallas_call(
        functools.partial(pack_kernel, sizes, bunch, turns),
        grid=(planes // bunch,),
        in_specs=[smem, psi_spec],
        out_specs=[whole(mixed_rows, LANES)] * grid,
        out_shape=[shape(mixed_rows, LANES)] * grid,
        scratch_shapes=scratch(2),
        compiler_params=PARAMS,
        cost_estimate=cost(0, 8 << 20),
    )(place, orbitals)
    moved = [send(turn, piece) for turn, piece in zip(turns[:6], moved[:6])] + list(moved[6:])
    behind = lax.optimization_barrier((place, line[1]))[0]
    shared = pl.pallas_call(
        functools.partial(potential_kernel, sizes, bunch),
        grid=(planes // bunch,),
        in_specs=[smem, plane_spec, plane_spec],
        out_specs=whole(spec_rows // 2, LANES),
        out_shape=shape(spec_rows // 2, LANES),
        scratch_shapes=scratch(1),
        compiler_params=PARAMS,
        cost_estimate=cost(0, 6 << 20),
    )(behind, ion_potential, hxc_potential)
    shared = swap(shared)
    *mixed, base = pl.pallas_call(
        functools.partial(plane_kernel, sizes, bunch, turns),
        grid=(planes // bunch,),
        in_specs=[smem, psi_spec, plane_spec, plane_spec, square],
        out_specs=[whole(mixed_rows, LANES)] * grid + [pair_spec],
        out_shape=[shape(mixed_rows, LANES)] * grid + [shape(2, planes, length, length)],
        scratch_shapes=scratch(2),
        compiler_params=PARAMS,
        cost_estimate=cost(8 * 3 * work, 20 << 20),
    )(behind, orbitals, ion_potential, hxc_potential, kin)
    for index in range(6, grid):
        moved[index] = send(turns[index], moved[index], *([base] if index < 11 else []))
    own = pl.pallas_call(
        functools.partial(share_kernel, sizes),
        in_specs=[vmem],
        out_specs=vmem,
        out_shape=shape(share * length, LANES),
        compiler_params=PARAMS,
        cost_estimate=cost(0, 2 << 20),
    )(shared)
    other = lax.ppermute(own, "band", [(0, 1), (1, 0)])
    half_spec = pl.BlockSpec((rows // steps * length, LANES), lambda i: (i % (steps // 2), 0))
    along = pl.pallas_call(
        functools.partial(along_kernel, sizes, steps, turns),
        grid=(steps,),
        in_specs=[smem] + [whole(mixed_rows, LANES)] * grid + [half_spec, half_spec, square],
        out_specs=pl.BlockSpec((rows // steps * length, 2 * LANES), lambda i: (i, 0)),
        out_shape=shape(rows * length, 2 * LANES),
        scratch_shapes=[pltpu.VMEM((rows // steps, 2, length, LANES), jnp.float32)],
        compiler_params=PARAMS,
        cost_estimate=cost(4 * 3 * work, 10 << 20),
    )(place, *moved, own, other, kin)
    mixed = [send(turn, piece) for turn, piece in zip(turns, mixed)]
    update = pl.pallas_call(
        functools.partial(update_kernel, sizes, steps, turns),
        grid=(steps,),
        in_specs=[
            smem,
            pl.BlockSpec((rows // steps * length, 2 * LANES), lambda i: (i, 0)),
            square,
        ]
        + [whole(mixed_rows, LANES)] * grid,
        out_specs=whole(2 * field, LANES),
        out_shape=shape(2 * field, LANES),
        scratch_shapes=[pltpu.VMEM((rows // steps, 2, length, LANES), jnp.float32)],
        compiler_params=PARAMS,
        cost_estimate=cost(2 * 3 * work, 14 << 20),
    )(place, along, kin, *mixed)
    update = swap(update)

    fresh, upper, lower, spectrum = pl.pallas_call(
        functools.partial(fresh_kernel, sizes, bunch),
        grid=(planes // bunch,),
        in_specs=[smem, vmem, pair_spec, table_spec],
        out_specs=[
            psi_spec,
            half_rows,
            half_rows,
            whole(spec_rows, LANES),
        ],
        out_shape=[
            shape(*orbitals.shape),
            shape(field // 2, LANES),
            shape(field // 2, LANES),
            shape(spec_rows, LANES),
        ],
        scratch_shapes=scratch(4),
        compiler_params=PARAMS,
        cost_estimate=cost(2 * 6 * work, 16 << 20),
    )(occupations, update, base, tables)
    upper_other = lax.ppermute(upper, "band", [(0, 1), (1, 0)])
    lower_other = lax.ppermute(lower, "band", [(0, 1), (1, 0)])

    spectrum = swap_all(spectrum)
    cells_np = squares_np[:, None] + squares_np[None, :]
    half = length // 2
    cells_np = np.concatenate(
        [cells_np[:, :LANES], np.concatenate([cells_np[:half, LANES:], cells_np[half:, LANES:]], axis=1)]
    )
    device = lax.axis_index("band") * grid + lax.axis_index("grid")
    cells = lax.dynamic_slice_in_dim(jnp.asarray(cells_np), device * share, share, axis=0)
    first, second = pl.pallas_call(
        functools.partial(filter_kernel, sizes),
        in_specs=[vmem] * 3,
        out_specs=[vmem] * 2,
        out_shape=[shape(part_rows, LANES)] * 2,
        scratch_shapes=[pltpu.VMEM((length, share * LANES), jnp.float32)],
        compiler_params=SMALL,
        cost_estimate=cost(6 * work, 5 << 20),
    )(spectrum, cells.reshape(1, share * LANES), tables)

    def last_part(part, near, far, made):
        cells_spec = pl.BlockSpec((bunch * cell_rows // 2, LANES), lambda i: (i + part * groups, 0))
        return pl.pallas_call(
            functools.partial(last_kernel, sizes, bunch),
            grid=(groups,),
            in_specs=[smem, vmem, vmem]
            + [cells_spec] * 4
            + [table_spec]
            + [pl.BlockSpec(memory_space=pl.ANY)] * len(made),
            out_specs=pl.BlockSpec((bunch, length, length), lambda i: (i + part * groups, 0, 0)),
            out_shape=shape(planes, length, length),
            scratch_shapes=scratch(2),
            input_output_aliases={8: 0} if made else {},
            compiler_params=PARAMS,
            cost_estimate=cost(3 * work, 4 << 20),
        )(place, near, far, upper, lower, upper_other, lower_other, tables, *made)

    first, upper_other = lax.optimization_barrier((first, upper_other))
    near = swap(first)
    far = lax.ppermute(near, "band", [(0, 1), (1, 0)])
    second, lower_other = lax.optimization_barrier((second, lower_other))
    near_second = swap(second)
    far_second = lax.ppermute(near_second, "band", [(0, 1), (1, 0)])
    potential = last_part(0, near, far, [])
    potential = last_part(1, near_second, far_second, [potential])
    return (fresh, potential)


def local(orbitals, occupations, ion_potential, hxc_potential):
    length = orbitals.shape[-1]
    parts = 2 * lax.axis_size("grid") * LANES
    fits = lax.axis_size("grid") & (lax.axis_size("grid") - 1) == 0
    fits = fits and orbitals.shape[2] % 2 == 0 and length == LANES + LANES // 2 and lax.axis_size("band") == 2 and length * length % parts == 0
    path = packed_path if fits else general
    return path(orbitals, occupations, ion_potential, hxc_potential)


def solution(mesh):
    placed = (
        P("band", None, "grid", None, None),
        P("band"),
        P("grid", None, None),
        P("grid", None, None),
    )
    return jax.shard_map(
        local,
        mesh=mesh,
        in_specs=placed,
        out_specs=(P("band", None, "grid", None, None), P("grid", None, None)),
        check_vma=False,
    )
```

```python
import functools
import math

import jax
import jax.numpy as jnp
import numpy as np
from jax import lax
from jax.experimental import pallas as pl
from jax.experimental.pallas import tpu as pltpu
from jax.sharding import PartitionSpec as P

BESSEL_ZERO = 0.8462873527504802
BESSEL_ONE = 0.36884204609417703
BESSEL_TWO = 0.07581776248
XC_FACTOR = 0.98474502
PRECISION = lax.Precision.HIGH


def kinetic_matrix(length):
    idx = np.arange(length)
    freq = np.where(idx < length // 2, idx, idx - length).astype(np.float64)
    wave = np.cos(2.0 * math.pi * (np.outer(idx, idx) % length) / length)
    row = (wave @ (freq * freq)) / length * (2.0 / (3.0 * (length / 2) ** 2))
    return row[(idx[:, None] - idx[None, :]) % length].astype(np.float32)


def real_basis(length):
    half = length // 2
    idx = np.arange(length)
    order = np.concatenate([np.arange(half + 1), np.arange(1, half)])
    angle = 2.0 * math.pi * (np.outer(order, idx) % length) / length
    table = np.where((np.arange(length) <= half)[:, None], np.cos(angle), np.sin(angle))
    scale = np.where((order == 0) | (order == half), math.sqrt(1.0 / length), math.sqrt(2.0 / length))
    return (table * scale[:, None]).astype(np.float32), (order * order).astype(np.float32)


def dot(form, left, right):
    return jnp.einsum(form, left, right, precision=PRECISION)


def general(orbitals, occupations, ion_potential, hxc_potential):
    length = orbitals.shape[-1]
    planes = orbitals.shape[2]
    grid = lax.axis_size("grid")
    bands = lax.axis_size("band")
    cells = length * length
    columns = cells // grid
    share = cells // (grid * bands)
    kin = jnp.asarray(kinetic_matrix(length))
    kin_x = kin.reshape(length, grid, planes)
    basis_np, squares = real_basis(length)
    basis = jnp.asarray(basis_np)
    basis_x = basis.reshape(length, grid, planes)

    psi = orbitals[0]
    potential = ion_potential + hxc_potential

    def scatter(fields):
        parts = fields.reshape(fields.shape[0], planes, grid, columns).transpose(2, 1, 0, 3)
        return lax.all_to_all(parts, "grid", split_axis=0, concat_axis=0)

    def along_yz(field):
        return dot("cxyz,zk->cxyk", field, kin) + dot("cxyz,yk->cxkz", field, kin)

    moved = scatter(jnp.concatenate([psi, potential[None]], axis=0))
    local_kin = along_yz(psi) - psi
    applied = local_kin + potential * psi
    mixed = scatter(local_kin + applied)
    twice = along_yz(applied) - applied + potential * applied

    along = dot("ksp,spcn->ckn", kin_x, moved[:, :, :2])
    again = dot("ksp,spcn->ckn", kin_x, mixed) + dot("kx,cxn->ckn", kin, along)
    potential_cols = moved[:, :, 2].reshape(length, columns)
    again = again + potential_cols * along
    turned = jnp.stack([along[1], -along[0]])
    update = 2.0 * BESSEL_ONE * turned - 4.0 * BESSEL_TWO * again
    update = update.reshape(2, grid, planes, columns).transpose(1, 2, 0, 3)
    update = lax.all_to_all(update, "grid", split_axis=0, concat_axis=0)
    update = update.transpose(2, 1, 0, 3).reshape(psi.shape)

    turned = jnp.stack([applied[1], -applied[0]])
    fresh = (
        (BESSEL_ZERO + 2.0 * BESSEL_TWO) * psi
        + 2.0 * BESSEL_ONE * turned
        - 4.0 * BESSEL_TWO * twice
        + update
    )
    part = occupations[0] * (fresh[0] * fresh[0] + fresh[1] * fresh[1])
    density = lax.psum(part, "band")

    spectrum = dot("xyz,kz->xyk", part, basis)
    spectrum = dot("xyk,jy->xjk", spectrum, basis)
    spectrum = spectrum.reshape(planes, bands * grid, share).transpose(1, 0, 2)
    spectrum = lax.all_to_all(spectrum, ("band", "grid"), split_axis=0, concat_axis=0)
    spectrum = spectrum.reshape(bands, grid, planes, share).sum(axis=0)
    spectrum = dot("ksp,spn->kn", basis_x, spectrum)
    start = (lax.axis_index("band") * grid + lax.axis_index("grid")) * share
    cell = start + jnp.arange(share, dtype=jnp.int32)
    table = jnp.asarray(squares)
    total = table[:, None] + (table[cell // length] + table[cell % length])[None, :]
    kernel = jnp.where(total > 0, length * math.sqrt(length) / 16.0 / (total + 1.0), 0.0)
    spectrum = dot("kx,kn->xn", basis, kernel * spectrum)
    spectrum = spectrum.reshape(1, grid, planes, share)
    spectrum = jnp.broadcast_to(spectrum, (bands, grid, planes, share)).reshape(bands * grid, planes, share)
    spectrum = lax.all_to_all(spectrum, ("band", "grid"), split_axis=0, concat_axis=0)
    spectrum = spectrum.transpose(1, 0, 2).reshape(planes, length, length)
    spectrum = dot("xjk,jy->xyk", spectrum, basis)
    hartree = dot("xyk,kz->xyz", spectrum, basis)
    return (fresh[None], hartree - XC_FACTOR * jnp.cbrt(density))


LANES = 128


def product(left, right):
    return jnp.dot(left, right, precision=lax.Precision.HIGHEST, preferred_element_type=jnp.float32)


def split(array):
    high = array.astype(jnp.bfloat16)
    return high, (array - high.astype(jnp.float32)).astype(jnp.bfloat16)


def product_of_parts(left, right):
    total = jnp.dot(left[0], right[0], preferred_element_type=jnp.float32)
    total = total + jnp.dot(left[1], right[0], preferred_element_type=jnp.float32)
    return total + jnp.dot(left[0], right[1], preferred_element_type=jnp.float32)


def whole_tiles(rows):
    return -(-rows // 8) * 8


def chunk_rows(sizes):
    planes, _, rows, share = sizes
    return whole_tiles(planes * share)


def kinetic(plane, kin):
    plane = split(plane)
    return product_of_parts(plane, kin) + product_of_parts(kin, plane)


def pack(plane, packed):
    length = plane.shape[0]
    half = length // 2
    packed[:length, :] = plane[:, :LANES]
    packed[length:, :] = jnp.concatenate([plane[:half, LANES:], plane[half:, LANES:]], axis=1)


def unpack(packed, length):
    side = length - LANES
    tail = packed[length:, :]
    right = jnp.concatenate([tail[:, :side], tail[:, side:]], axis=0)
    return jnp.concatenate([packed[:length, :], right], axis=1)


def fill(out_ref, count, chunk, used):
    if used < chunk:

        @pl.when(pl.program_id(0) == 0)
        def _():
            for to in range(count):
                out_ref[pl.ds(to * chunk + used, chunk - used), :] = jnp.zeros((chunk - used, LANES), jnp.float32)


def move(to_ref, to, from_ref, start, count, step=1):
    if count < 8:
        to_ref[pl.ds(to, count), :] = from_ref[pl.ds(start, count, stride=step), :]
        return
    for first in [*range(0, count - 7, 8)] + ([count - 8] if count % 8 else []):
        to_ref[pl.ds(to + first, 8), :] = from_ref[pl.ds(start + first * step, 8, stride=step), :]


def potential_kernel(sizes, bunch, place_ref, ion_ref, hxc_ref, out_ref, packed):
    planes, grid, rows, share = sizes
    chunk = chunk_rows(sizes)
    band = place_ref[0] // grid
    fill(out_ref, grid, chunk, planes * share)
    for inner in range(bunch):
        plane = pl.program_id(0) * bunch + inner
        slot = packed.at[inner]
        pack(ion_ref[inner] + hxc_ref[inner], slot)
        for to in range(grid):
            start = to * rows + band * share
            move(out_ref, to * chunk + plane * share, slot, start, share)


def pack_kernel(sizes, bunch, turns, place_ref, psi_ref, *refs):
    planes, grid, rows, share = sizes
    *out_refs, packed = refs
    mine = place_ref[0] % grid
    for inner in range(bunch):
        plane = pl.program_id(0) * bunch + inner
        for part in range(2):
            slot = packed.at[inner * 2 + part]
            pack(psi_ref[0, part, inner], slot)
            for turn, out_ref in zip(turns, out_refs):
                start = (mine ^ turn) * rows
                move(out_ref, (plane * 2 + part) * rows, slot, start, rows)


def plane_kernel(sizes, bunch, turns, place_ref, psi_ref, ion_ref, hxc_ref, kin_ref, *refs):
    planes, grid, rows, share = sizes
    *out_refs, base_ref, packed = refs
    mine = place_ref[0] % grid
    kin = split(kin_ref[...])
    for inner in range(bunch):
        plane = pl.program_id(0) * bunch + inner
        potential = ion_ref[inner] + hxc_ref[inner]
        applied = []
        for part in range(2):
            field = psi_ref[0, part, inner]
            bare = kinetic(field, kin) - field
            applied.append(bare + potential * field)
            slot = packed.at[inner * 2 + part]
            pack(bare + applied[part], slot)
            for turn, out_ref in zip(turns, out_refs):
                start = (mine ^ turn) * rows
                move(out_ref, (plane * 2 + part) * rows, slot, start, rows)
        for part in range(2):
            twice = kinetic(applied[part], kin) + (potential - 1.0) * applied[part]
            turned = applied[1] if part == 0 else -applied[0]
            base_ref[part, inner] = (
                (BESSEL_ZERO + 2.0 * BESSEL_TWO) * psi_ref[0, part, inner]
                + 2.0 * BESSEL_ONE * turned
                - 4.0 * BESSEL_TWO * twice
            )


def share_kernel(sizes, moved_ref, out_ref):
    planes, grid, rows, share = sizes
    length = planes * grid
    chunk = chunk_rows(sizes)
    for source in range(grid):
        for row in range(share):
            start = source * chunk + row
            move(out_ref, row * length + source * planes, moved_ref, start, planes, share)


def along_kernel(sizes, steps, turns, place_ref, *refs):
    planes, grid, rows, share = sizes
    moved_refs, (own_ref, other_ref, kin_ref, out_ref, lines) = refs[:grid], refs[grid:]
    length = planes * grid
    kin = split(kin_ref[...])
    step = pl.program_id(0)
    mine_here = place_ref[0] // grid == step // (steps // 2)
    for inner in range(rows // steps):
        row = step * (rows // steps) + inner
        slot = lines.at[inner]
        for turn, moved_ref in zip(turns, moved_refs):
            first = (place_ref[0] % grid ^ turn) * planes
            for part in range(2):
                move(slot.at[part], first, moved_ref, part * rows + row, planes, 2 * rows)
        along = product_of_parts(kin, split(jnp.concatenate([slot[0], slot[1]], axis=1)))
        again = product_of_parts(kin, split(along))
        here = slice(inner * length, (inner + 1) * length)
        potential = jnp.where(mine_here, own_ref[here, :], other_ref[here, :])
        for part in range(2):
            lanes = slice(part * LANES, (part + 1) * LANES)
            turned = along[:, LANES:] if part == 0 else -along[:, :LANES]
            twice = again[:, lanes] + potential * along[:, lanes]
            out_ref[here, lanes] = 2.0 * BESSEL_ONE * turned - 4.0 * BESSEL_TWO * twice


def update_kernel(sizes, steps, turns, place_ref, along_ref, kin_ref, *refs):
    planes, grid, rows, share = sizes
    *mixed_refs, out_ref, lines = refs
    length = planes * grid
    kin = split(-4.0 * BESSEL_TWO * kin_ref[...])
    step = pl.program_id(0)
    for inner in range(rows // steps):
        row = step * (rows // steps) + inner
        slot = lines.at[inner]
        for turn, mixed_ref in zip(turns, mixed_refs):
            first = (place_ref[0] % grid ^ turn) * planes
            for part in range(2):
                move(slot.at[part], first, mixed_ref, part * rows + row, planes, 2 * rows)
        mixed = product_of_parts(kin, split(jnp.concatenate([slot[0], slot[1]], axis=1)))
        update = along_ref[inner * length : (inner + 1) * length, :] + mixed
        for part in range(2):
            where = pl.ds(part * rows + row, length, stride=2 * rows)
            out_ref[where, :] = update[:, part * LANES : (part + 1) * LANES]


def fresh_kernel(
    sizes, bunch, occ_ref, update_ref, base_ref, tables_ref, fresh_ref, upper_ref, lower_ref, out_ref, packed
):
    planes, grid, rows, share = sizes
    length = planes * grid
    chunk = chunk_rows(sizes)
    cell_rows = rows * grid
    half = cell_rows // 2
    fill(out_ref, 2 * grid, chunk, planes * share)
    means, parts = [], []
    for inner in range(bunch):
        plane = pl.program_id(0) * bunch + inner
        part_sum = None
        for part in range(2):
            slot = packed.at[inner * 4 + part]
            for source in range(grid):
                start = ((source * planes + plane) * 2 + part) * rows
                move(slot, source * rows, update_ref, start, rows)
            fresh = base_ref[part, inner] + unpack(slot, length)
            fresh_ref[0, part, inner] = fresh
            part_sum = fresh * fresh if part_sum is None else part_sum + fresh * fresh
        part_sum = occ_ref[0] * part_sum
        slot = packed.at[inner * 4 + 2]
        pack(part_sum, slot)
        upper_ref[inner * half : (inner + 1) * half, :] = slot[:half, :]
        lower_ref[inner * half : (inner + 1) * half, :] = slot[half:, :]
        means.append(jnp.sum(part_sum) * (1.0 / length**2))
        parts.append(part_sum - means[inner])
    basis, turn = split(tables_ref[0]), split(tables_ref[1])
    along_z = product_of_parts(split(jnp.concatenate(parts, axis=0)), turn)
    first = (lax.broadcasted_iota(jnp.int32, (length, length), axis) == 0 for axis in range(2))
    first = jnp.logical_and(*first)
    for inner in range(bunch):
        plane = pl.program_id(0) * bunch + inner
        spectrum = product_of_parts(basis, split(along_z[inner * length : (inner + 1) * length, :]))
        slot = packed.at[inner * 4 + 3]
        pack(spectrum + jnp.where(first, means[inner] * length, 0.0), slot)
        for to in range(2 * grid):
            move(out_ref, to * chunk + plane * share, slot, to * share, share)


def filter_kernel(sizes, spec_ref, cells_ref, tables_ref, upper_ref, lower_ref, lines):
    planes, grid, rows, share = sizes
    length = planes * grid
    chunk = chunk_rows(sizes)

    def places():
        for source in range(grid):
            for row in range(share):
                first, second = (
                    pl.ds((band * grid + source) * chunk + row, planes, stride=share) for band in range(2)
                )
                here = (pl.ds(source * planes, planes), slice(row * LANES, (row + 1) * LANES))
                yield first, second, here

    for first, second, here in places():
        lines[here] = spec_ref[first, :] + spec_ref[second, :]
    index = lax.broadcasted_iota(jnp.int32, lines.shape, 0)
    order = jnp.where(index <= length // 2, index, index - length // 2).astype(jnp.float32)
    total = order * order + cells_ref[...]
    scale = length * math.sqrt(length) / 16.0
    kernel = jnp.where(total > 0.0, scale / (total + 1.0), 0.0)
    field = kernel * product(tables_ref[0], lines[...])
    lines[...] = product_of_parts(split(tables_ref[1]), split(field))
    some = planes // 2
    chunk = whole_tiles(some * share)
    for part, out_ref in enumerate((upper_ref, lower_ref)):
        for source in range(grid):
            for row in range(share):
                piece = lines[pl.ds(source * planes + part * some, some), row * LANES : (row + 1) * LANES]
                out_ref[pl.ds(source * chunk + row, some, stride=share), :] = piece
            if some * share < chunk:
                rest = chunk - some * share
                out_ref[pl.ds(source * chunk + some * share, rest), :] = jnp.zeros((rest, LANES), jnp.float32)


def last_kernel(
    sizes, bunch, place_ref, near_ref, far_ref, upper_ref, lower_ref, upper_other, lower_other, tables_ref, *refs
):
    planes, grid, rows, share = sizes
    out_ref, packed = refs[-2:]
    length = planes * grid
    half = rows * grid // 2
    chunk = whole_tiles(planes // 2 * share)
    turn, basis = split(tables_ref[1]), split(tables_ref[0])
    band = place_ref[0] // grid
    lines = []
    for inner in range(bunch):
        plane = pl.program_id(0) * bunch + inner
        slot = packed.at[inner * 2]
        for part, spec_ref in ((band, near_ref), (1 - band, far_ref)):
            side = slot.at[pl.ds(pl.multiple_of(part * half, 8), half), :]
            for source in range(grid):
                start = source * chunk + plane * share
                move(side, source * share, spec_ref, start, share)
        lines.append(product_of_parts(turn, split(unpack(slot, length))))
    hartree = product_of_parts(split(jnp.concatenate(lines, axis=0)), basis)
    for inner in range(bunch):
        slot = packed.at[inner * 2 + 1]
        here = slice(inner * half, (inner + 1) * half)
        slot[:half, :] = upper_ref[here, :] + upper_other[here, :]
        slot[half:, :] = lower_ref[here, :] + lower_other[here, :]
        root = jnp.exp(jnp.log(unpack(slot, length)) * (1.0 / 3.0))
        out_ref[inner] = hartree[inner * length : (inner + 1) * length, :] - XC_FACTOR * root


def shape(*dims):
    return jax.ShapeDtypeStruct(dims, jnp.float32)


def whole(*dims):
    return pl.BlockSpec(dims, lambda *_: (0,) * len(dims))


SMALL = pltpu.CompilerParams(vmem_limit_bytes=24 << 20)
PARAMS = pltpu.CompilerParams(vmem_limit_bytes=54 << 20)


def cost(flops, moved):
    return pl.CostEstimate(flops=flops, bytes_accessed=moved, transcendentals=0)


def turn_order(grid):
    order = [0]
    for near in range(grid // 2):
        order += [near, near + grid // 2] if near else [grid // 2]
    return order


def packed_path(orbitals, occupations, ion_potential, hxc_potential):
    length = orbitals.shape[-1]
    planes = orbitals.shape[2]
    grid = lax.axis_size("grid")
    cell_rows = length * length // LANES
    rows = cell_rows // grid
    share = rows // 2
    sizes = (planes, grid, rows, share)
    field = planes * cell_rows
    work = 2 * planes * length**3
    place = lax.axis_index(("band", "grid")).astype(jnp.int32).reshape(1)
    kin = jnp.asarray(kinetic_matrix(length))
    basis_np, squares_np = real_basis(length)
    tables = jnp.asarray(np.stack([basis_np, basis_np.T]))
    smem = pl.BlockSpec(memory_space=pltpu.SMEM)
    vmem = pl.BlockSpec(memory_space=pltpu.VMEM)
    some = planes // 2
    bunch = next(count for count in (3, 2, 1) if some % count == 0)
    groups = some // bunch
    psi_spec = pl.BlockSpec((1, 2, bunch, length, length), lambda i: (0, 0, i, 0, 0))
    plane_spec = pl.BlockSpec((bunch, length, length), lambda i: (i, 0, 0))
    pair_spec = pl.BlockSpec((2, bunch, length, length), lambda i: (0, i, 0, 0))
    half_rows = pl.BlockSpec((bunch * cell_rows // 2, LANES), lambda i: (i, 0))
    part_rows = grid * whole_tiles(some * share)
    square = whole(length, length)
    table_spec = whole(2, length, length)

    def scratch(count):
        return [pltpu.VMEM((count * bunch, cell_rows, LANES), jnp.float32)]

    line = []

    def send(turn, piece, *gates):
        if not turn:
            return piece
        if len(line) >= 5:
            gates += (line[-5],)
        if gates:
            piece = lax.optimization_barrier((piece, *gates))[0]
        line.append(lax.ppermute(piece, "grid", [(spot, spot ^ turn) for spot in range(grid)]))
        return line[-1]

    def swap(array):
        flat = array.reshape(grid, -1, LANES)
        return lax.all_to_all(flat, "grid", split_axis=0, concat_axis=0).reshape(array.shape)

    def swap_all(array):
        flat = array.reshape(2 * grid, -1, LANES)
        return lax.all_to_all(flat, ("band", "grid"), split_axis=0, concat_axis=0).reshape(array.shape)

    turns = turn_order(grid)
    spec_rows = 2 * grid * chunk_rows(sizes)
    mixed_rows = 2 * planes * rows
    steps = 6 if rows % 6 == 0 and share % (rows // 6) == 0 else 2
    shared = pl.pallas_call(
        functools.partial(potential_kernel, sizes, bunch),
        grid=(planes // bunch,),
        in_specs=[smem, plane_spec, plane_spec],
        out_specs=whole(spec_rows // 2, LANES),
        out_shape=shape(spec_rows // 2, LANES),
        scratch_shapes=scratch(1),
        compiler_params=PARAMS,
        cost_estimate=cost(0, 6 << 20),
    )(place, ion_potential, hxc_potential)
    place, shared = lax.optimization_barrier((place, shared))
    shared = swap(shared)
    moved = pl.pallas_call(
        functools.partial(pack_kernel, sizes, bunch, turns),
        grid=(planes // bunch,),
        in_specs=[smem, psi_spec],
        out_specs=[whole(mixed_rows, LANES)] * grid,
        out_shape=[shape(mixed_rows, LANES)] * grid,
        scratch_shapes=scratch(2),
        compiler_params=PARAMS,
        cost_estimate=cost(0, 8 << 20),
    )(place, orbitals)
    moved = [send(turn, piece) for turn, piece in zip(turns[:6], moved[:6])] + list(moved[6:])
    behind = lax.optimization_barrier((place, line[1]))[0]
    *mixed, base = pl.pallas_call(
        functools.partial(plane_kernel, sizes, bunch, turns),
        grid=(planes // bunch,),
        in_specs=[smem, psi_spec, plane_spec, plane_spec, square],
        out_specs=[whole(mixed_rows, LANES)] * grid + [pair_spec],
        out_shape=[shape(mixed_rows, LANES)] * grid + [shape(2, planes, length, length)],
        scratch_shapes=scratch(2),
        compiler_params=PARAMS,
        cost_estimate=cost(8 * 3 * work, 20 << 20),
    )(behind, orbitals, ion_potential, hxc_potential, kin)
    for index in range(6, grid):
        moved[index] = send(turns[index], moved[index], *([base] if index < 11 else []))
    own = pl.pallas_call(
        functools.partial(share_kernel, sizes),
        in_specs=[vmem],
        out_specs=vmem,
        out_shape=shape(share * length, LANES),
        compiler_params=PARAMS,
        cost_estimate=cost(0, 2 << 20),
    )(shared)
    other = lax.ppermute(own, "band", [(0, 1), (1, 0)])
    half_spec = pl.BlockSpec((rows // steps * length, LANES), lambda i: (i % (steps // 2), 0))
    along = pl.pallas_call(
        functools.partial(along_kernel, sizes, steps, turns),
        grid=(steps,),
        in_specs=[smem] + [whole(mixed_rows, LANES)] * grid + [half_spec, half_spec, square],
        out_specs=pl.BlockSpec((rows // steps * length, 2 * LANES), lambda i: (i, 0)),
        out_shape=shape(rows * length, 2 * LANES),
        scratch_shapes=[pltpu.VMEM((rows // steps, 2, length, LANES), jnp.float32)],
        compiler_params=PARAMS,
        cost_estimate=cost(4 * 3 * work, 10 << 20),
    )(place, *moved, own, other, kin)
    mixed = [send(turn, piece) for turn, piece in zip(turns, mixed)]
    update = pl.pallas_call(
        functools.partial(update_kernel, sizes, steps, turns),
        grid=(steps,),
        in_specs=[
            smem,
            pl.BlockSpec((rows // steps * length, 2 * LANES), lambda i: (i, 0)),
            square,
        ]
        + [whole(mixed_rows, LANES)] * grid,
        out_specs=whole(2 * field, LANES),
        out_shape=shape(2 * field, LANES),
        scratch_shapes=[pltpu.VMEM((rows // steps, 2, length, LANES), jnp.float32)],
        compiler_params=PARAMS,
        cost_estimate=cost(2 * 3 * work, 14 << 20),
    )(place, along, kin, *mixed)
    update = swap(update)

    fresh, upper, lower, spectrum = pl.pallas_call(
        functools.partial(fresh_kernel, sizes, bunch),
        grid=(planes // bunch,),
        in_specs=[smem, vmem, pair_spec, table_spec],
        out_specs=[
            psi_spec,
            half_rows,
            half_rows,
            whole(spec_rows, LANES),
        ],
        out_shape=[
            shape(*orbitals.shape),
            shape(field // 2, LANES),
            shape(field // 2, LANES),
            shape(spec_rows, LANES),
        ],
        scratch_shapes=scratch(4),
        compiler_params=PARAMS,
        cost_estimate=cost(2 * 6 * work, 16 << 20),
    )(occupations, update, base, tables)
    upper_other = lax.ppermute(upper, "band", [(0, 1), (1, 0)])
    lower_other = lax.ppermute(lower, "band", [(0, 1), (1, 0)])

    spectrum = swap_all(spectrum)
    cells_np = squares_np[:, None] + squares_np[None, :]
    half = length // 2
    cells_np = np.concatenate(
        [cells_np[:, :LANES], np.concatenate([cells_np[:half, LANES:], cells_np[half:, LANES:]], axis=1)]
    )
    device = lax.axis_index("band") * grid + lax.axis_index("grid")
    cells = lax.dynamic_slice_in_dim(jnp.asarray(cells_np), device * share, share, axis=0)
    first, second = pl.pallas_call(
        functools.partial(filter_kernel, sizes),
        in_specs=[vmem] * 3,
        out_specs=[vmem] * 2,
        out_shape=[shape(part_rows, LANES)] * 2,
        scratch_shapes=[pltpu.VMEM((length, share * LANES), jnp.float32)],
        compiler_params=SMALL,
        cost_estimate=cost(6 * work, 5 << 20),
    )(spectrum, cells.reshape(1, share * LANES), tables)

    def last_part(part, near, far, made):
        cells_spec = pl.BlockSpec((bunch * cell_rows // 2, LANES), lambda i: (i + part * groups, 0))
        return pl.pallas_call(
            functools.partial(last_kernel, sizes, bunch),
            grid=(groups,),
            in_specs=[smem, vmem, vmem]
            + [cells_spec] * 4
            + [table_spec]
            + [pl.BlockSpec(memory_space=pl.ANY)] * len(made),
            out_specs=pl.BlockSpec((bunch, length, length), lambda i: (i + part * groups, 0, 0)),
            out_shape=shape(planes, length, length),
            scratch_shapes=scratch(2),
            input_output_aliases={8: 0} if made else {},
            compiler_params=PARAMS,
            cost_estimate=cost(3 * work, 4 << 20),
        )(place, near, far, upper, lower, upper_other, lower_other, tables, *made)

    first, upper_other = lax.optimization_barrier((first, upper_other))
    near = swap(first)
    far = lax.ppermute(near, "band", [(0, 1), (1, 0)])
    second, lower_other = lax.optimization_barrier((second, lower_other))
    near_second = swap(second)
    far_second = lax.ppermute(near_second, "band", [(0, 1), (1, 0)])
    potential = last_part(0, near, far, [])
    potential = last_part(1, near_second, far_second, [potential])
    return (fresh, potential)


def local(orbitals, occupations, ion_potential, hxc_potential):
    length = orbitals.shape[-1]
    parts = 2 * lax.axis_size("grid") * LANES
    fits = lax.axis_size("grid") & (lax.axis_size("grid") - 1) == 0
    fits = fits and orbitals.shape[2] % 2 == 0 and length == LANES + LANES // 2 and lax.axis_size("band") == 2 and length * length % parts == 0
    path = packed_path if fits else general
    return path(orbitals, occupations, ion_potential, hxc_potential)


def solution(mesh):
    placed = (
        P("band", None, "grid", None, None),
        P("band"),
        P("grid", None, None),
        P("grid", None, None),
    )
    return jax.shard_map(
        local,
        mesh=mesh,
        in_specs=placed,
        out_specs=(P("band", None, "grid", None, None), P("grid", None, None)),
        check_vma=False,
    )
```

```python
import functools
import math

import jax
import jax.numpy as jnp
import numpy as np
from jax import lax
from jax.experimental import pallas as pl
from jax.experimental.pallas import tpu as pltpu
from jax.sharding import PartitionSpec as P

BESSEL_ZERO = 0.8462873527504802
BESSEL_ONE = 0.36884204609417703
BESSEL_TWO = 0.07581776248
XC_FACTOR = 0.98474502
PRECISION = lax.Precision.HIGH


def kinetic_matrix(length):
    idx = np.arange(length)
    freq = np.where(idx < length // 2, idx, idx - length).astype(np.float64)
    wave = np.cos(2.0 * math.pi * (np.outer(idx, idx) % length) / length)
    row = (wave @ (freq * freq)) / length * (2.0 / (3.0 * (length / 2) ** 2))
    return row[(idx[:, None] - idx[None, :]) % length].astype(np.float32)


def real_basis(length):
    half = length // 2
    idx = np.arange(length)
    order = np.concatenate([np.arange(half + 1), np.arange(1, half)])
    angle = 2.0 * math.pi * (np.outer(order, idx) % length) / length
    table = np.where((np.arange(length) <= half)[:, None], np.cos(angle), np.sin(angle))
    scale = np.where((order == 0) | (order == half), math.sqrt(1.0 / length), math.sqrt(2.0 / length))
    return (table * scale[:, None]).astype(np.float32), (order * order).astype(np.float32)


def dot(form, left, right):
    return jnp.einsum(form, left, right, precision=PRECISION)


def general(orbitals, occupations, ion_potential, hxc_potential):
    length = orbitals.shape[-1]
    planes = orbitals.shape[2]
    grid = lax.axis_size("grid")
    bands = lax.axis_size("band")
    cells = length * length
    columns = cells // grid
    share = cells // (grid * bands)
    kin = jnp.asarray(kinetic_matrix(length))
    kin_x = kin.reshape(length, grid, planes)
    basis_np, squares = real_basis(length)
    basis = jnp.asarray(basis_np)
    basis_x = basis.reshape(length, grid, planes)

    psi = orbitals[0]
    potential = ion_potential + hxc_potential

    def scatter(fields):
        parts = fields.reshape(fields.shape[0], planes, grid, columns).transpose(2, 1, 0, 3)
        return lax.all_to_all(parts, "grid", split_axis=0, concat_axis=0)

    def along_yz(field):
        return dot("cxyz,zk->cxyk", field, kin) + dot("cxyz,yk->cxkz", field, kin)

    moved = scatter(jnp.concatenate([psi, potential[None]], axis=0))
    local_kin = along_yz(psi) - psi
    applied = local_kin + potential * psi
    mixed = scatter(local_kin + applied)
    twice = along_yz(applied) - applied + potential * applied

    along = dot("ksp,spcn->ckn", kin_x, moved[:, :, :2])
    again = dot("ksp,spcn->ckn", kin_x, mixed) + dot("kx,cxn->ckn", kin, along)
    potential_cols = moved[:, :, 2].reshape(length, columns)
    again = again + potential_cols * along
    turned = jnp.stack([along[1], -along[0]])
    update = 2.0 * BESSEL_ONE * turned - 4.0 * BESSEL_TWO * again
    update = update.reshape(2, grid, planes, columns).transpose(1, 2, 0, 3)
    update = lax.all_to_all(update, "grid", split_axis=0, concat_axis=0)
    update = update.transpose(2, 1, 0, 3).reshape(psi.shape)

    turned = jnp.stack([applied[1], -applied[0]])
    fresh = (
        (BESSEL_ZERO + 2.0 * BESSEL_TWO) * psi
        + 2.0 * BESSEL_ONE * turned
        - 4.0 * BESSEL_TWO * twice
        + update
    )
    part = occupations[0] * (fresh[0] * fresh[0] + fresh[1] * fresh[1])
    density = lax.psum(part, "band")

    spectrum = dot("xyz,kz->xyk", part, basis)
    spectrum = dot("xyk,jy->xjk", spectrum, basis)
    spectrum = spectrum.reshape(planes, bands * grid, share).transpose(1, 0, 2)
    spectrum = lax.all_to_all(spectrum, ("band", "grid"), split_axis=0, concat_axis=0)
    spectrum = spectrum.reshape(bands, grid, planes, share).sum(axis=0)
    spectrum = dot("ksp,spn->kn", basis_x, spectrum)
    start = (lax.axis_index("band") * grid + lax.axis_index("grid")) * share
    cell = start + jnp.arange(share, dtype=jnp.int32)
    table = jnp.asarray(squares)
    total = table[:, None] + (table[cell // length] + table[cell % length])[None, :]
    kernel = jnp.where(total > 0, length * math.sqrt(length) / 16.0 / (total + 1.0), 0.0)
    spectrum = dot("kx,kn->xn", basis, kernel * spectrum)
    spectrum = spectrum.reshape(1, grid, planes, share)
    spectrum = jnp.broadcast_to(spectrum, (bands, grid, planes, share)).reshape(bands * grid, planes, share)
    spectrum = lax.all_to_all(spectrum, ("band", "grid"), split_axis=0, concat_axis=0)
    spectrum = spectrum.transpose(1, 0, 2).reshape(planes, length, length)
    spectrum = dot("xjk,jy->xyk", spectrum, basis)
    hartree = dot("xyk,kz->xyz", spectrum, basis)
    return (fresh[None], hartree - XC_FACTOR * jnp.cbrt(density))


LANES = 128


def product(left, right):
    return jnp.dot(left, right, precision=lax.Precision.HIGHEST, preferred_element_type=jnp.float32)


def split(array):
    high = array.astype(jnp.bfloat16)
    return high, (array - high.astype(jnp.float32)).astype(jnp.bfloat16)


def product_of_parts(left, right):
    total = jnp.dot(left[0], right[0], preferred_element_type=jnp.float32)
    total = total + jnp.dot(left[1], right[0], preferred_element_type=jnp.float32)
    return total + jnp.dot(left[0], right[1], preferred_element_type=jnp.float32)


def whole_tiles(rows):
    return -(-rows // 8) * 8


def chunk_rows(sizes):
    planes, _, rows, share = sizes
    return whole_tiles(planes * share)


def kinetic(plane, kin):
    plane = split(plane)
    return product_of_parts(plane, kin) + product_of_parts(kin, plane)


def pack(plane, packed):
    length = plane.shape[0]
    half = length // 2
    packed[:length, :] = plane[:, :LANES]
    packed[length:, :] = jnp.concatenate([plane[:half, LANES:], plane[half:, LANES:]], axis=1)


def unpack(packed, length):
    side = length - LANES
    tail = packed[length:, :]
    right = jnp.concatenate([tail[:, :side], tail[:, side:]], axis=0)
    return jnp.concatenate([packed[:length, :], right], axis=1)


def fill(out_ref, count, chunk, used):
    if used < chunk:

        @pl.when(pl.program_id(0) == 0)
        def _():
            for to in range(count):
                out_ref[pl.ds(to * chunk + used, chunk - used), :] = jnp.zeros((chunk - used, LANES), jnp.float32)


def move(to_ref, to, from_ref, start, count, step=1):
    if count < 8:
        to_ref[pl.ds(to, count), :] = from_ref[pl.ds(start, count, stride=step), :]
        return
    for first in [*range(0, count - 7, 8)] + ([count - 8] if count % 8 else []):
        to_ref[pl.ds(to + first, 8), :] = from_ref[pl.ds(start + first * step, 8, stride=step), :]


def potential_kernel(sizes, bunch, place_ref, ion_ref, hxc_ref, out_ref, packed):
    planes, grid, rows, share = sizes
    chunk = chunk_rows(sizes)
    band = place_ref[0] // grid
    fill(out_ref, grid, chunk, planes * share)
    for inner in range(bunch):
        plane = pl.program_id(0) * bunch + inner
        slot = packed.at[inner]
        pack(ion_ref[inner] + hxc_ref[inner], slot)
        for to in range(grid):
            start = to * rows + band * share
            move(out_ref, to * chunk + plane * share, slot, start, share)


def pack_kernel(sizes, bunch, turns, place_ref, psi_ref, *refs):
    planes, grid, rows, share = sizes
    *out_refs, packed = refs
    mine = place_ref[0] % grid
    for inner in range(bunch):
        plane = pl.program_id(0) * bunch + inner
        for part in range(2):
            slot = packed.at[inner * 2 + part]
            pack(psi_ref[0, part, inner], slot)
            for turn, out_ref in zip(turns, out_refs):
                start = (mine ^ turn) * rows
                move(out_ref, (plane * 2 + part) * rows, slot, start, rows)


def plane_kernel(sizes, bunch, turns, place_ref, psi_ref, ion_ref, hxc_ref, kin_ref, *refs):
    planes, grid, rows, share = sizes
    *out_refs, base_ref, packed = refs
    mine = place_ref[0] % grid
    kin = split(kin_ref[...])
    for inner in range(bunch):
        plane = pl.program_id(0) * bunch + inner
        potential = ion_ref[inner] + hxc_ref[inner]
        applied = []
        for part in range(2):
            field = psi_ref[0, part, inner]
            bare = kinetic(field, kin) - field
            applied.append(bare + potential * field)
            slot = packed.at[inner * 2 + part]
            pack(bare + applied[part], slot)
            for turn, out_ref in zip(turns, out_refs):
                start = (mine ^ turn) * rows
                move(out_ref, (plane * 2 + part) * rows, slot, start, rows)
        for part in range(2):
            twice = kinetic(applied[part], kin) + (potential - 1.0) * applied[part]
            turned = applied[1] if part == 0 else -applied[0]
            base_ref[part, inner] = (
                (BESSEL_ZERO + 2.0 * BESSEL_TWO) * psi_ref[0, part, inner]
                + 2.0 * BESSEL_ONE * turned
                - 4.0 * BESSEL_TWO * twice
            )


def share_kernel(sizes, moved_ref, out_ref):
    planes, grid, rows, share = sizes
    length = planes * grid
    chunk = chunk_rows(sizes)
    for source in range(grid):
        for row in range(share):
            start = source * chunk + row
            move(out_ref, row * length + source * planes, moved_ref, start, planes, share)


def along_kernel(sizes, steps, turns, place_ref, *refs):
    planes, grid, rows, share = sizes
    *moved_refs, kin_ref, out_ref, lines = refs
    length = planes * grid
    kin = split(kin_ref[...])
    for inner in range(rows // steps):
        row = pl.program_id(0) * (rows // steps) + inner
        slot = lines.at[inner]
        for turn, moved_ref in zip(turns, moved_refs):
            first = (place_ref[0] % grid ^ turn) * planes
            for part in range(2):
                move(slot.at[part], first, moved_ref, part * rows + row, planes, 2 * rows)
        field = jnp.concatenate([slot[0], slot[1]], axis=1)
        out_ref[inner * length : (inner + 1) * length, :] = product_of_parts(kin, split(field))


def update_kernel(sizes, steps, turns, place_ref, along_ref, own_ref, other_ref, kin_ref, *refs):
    planes, grid, rows, share = sizes
    *mixed_refs, out_ref, lines = refs
    length = planes * grid
    kin = split(kin_ref[...])
    step = pl.program_id(0)
    mine_here = place_ref[0] // grid == step // (steps // 2)
    for inner in range(rows // steps):
        row = step * (rows // steps) + inner
        here = slice(inner * length, (inner + 1) * length)
        slot = lines.at[inner]
        for turn, mixed_ref in zip(turns, mixed_refs):
            first = (place_ref[0] % grid ^ turn) * planes
            for part in range(2):
                move(slot.at[part], first, mixed_ref, part * rows + row, planes, 2 * rows)
        along = along_ref[here, :]
        again = product_of_parts(kin, split(jnp.concatenate([slot[0], slot[1]], axis=1) + along))
        potential = jnp.where(mine_here, own_ref[here, :], other_ref[here, :])
        for part in range(2):
            mine = along[:, part * LANES : (part + 1) * LANES]
            turned = along[:, LANES:] if part == 0 else -along[:, :LANES]
            twice = again[:, part * LANES : (part + 1) * LANES] + potential * mine
            out_ref[pl.ds(part * rows + row, length, stride=2 * rows), :] = (
                2.0 * BESSEL_ONE * turned - 4.0 * BESSEL_TWO * twice
            )


def fresh_kernel(
    sizes, bunch, occ_ref, update_ref, base_ref, tables_ref, fresh_ref, upper_ref, lower_ref, out_ref, packed
):
    planes, grid, rows, share = sizes
    length = planes * grid
    chunk = chunk_rows(sizes)
    cell_rows = rows * grid
    half = cell_rows // 2
    fill(out_ref, 2 * grid, chunk, planes * share)
    means, parts = [], []
    for inner in range(bunch):
        plane = pl.program_id(0) * bunch + inner
        part_sum = None
        for part in range(2):
            slot = packed.at[inner * 4 + part]
            for source in range(grid):
                start = ((source * planes + plane) * 2 + part) * rows
                move(slot, source * rows, update_ref, start, rows)
            fresh = base_ref[part, inner] + unpack(slot, length)
            fresh_ref[0, part, inner] = fresh
            part_sum = fresh * fresh if part_sum is None else part_sum + fresh * fresh
        part_sum = occ_ref[0] * part_sum
        slot = packed.at[inner * 4 + 2]
        pack(part_sum, slot)
        upper_ref[inner * half : (inner + 1) * half, :] = slot[:half, :]
        lower_ref[inner * half : (inner + 1) * half, :] = slot[half:, :]
        means.append(jnp.sum(part_sum) * (1.0 / length**2))
        parts.append(part_sum - means[inner])
    basis, turn = split(tables_ref[0]), split(tables_ref[1])
    along_z = product_of_parts(split(jnp.concatenate(parts, axis=0)), turn)
    first = (lax.broadcasted_iota(jnp.int32, (length, length), axis) == 0 for axis in range(2))
    first = jnp.logical_and(*first)
    for inner in range(bunch):
        plane = pl.program_id(0) * bunch + inner
        spectrum = product_of_parts(basis, split(along_z[inner * length : (inner + 1) * length, :]))
        slot = packed.at[inner * 4 + 3]
        pack(spectrum + jnp.where(first, means[inner] * length, 0.0), slot)
        for to in range(2 * grid):
            move(out_ref, to * chunk + plane * share, slot, to * share, share)


def filter_kernel(sizes, spec_ref, cells_ref, tables_ref, upper_ref, lower_ref, lines):
    planes, grid, rows, share = sizes
    length = planes * grid
    chunk = chunk_rows(sizes)

    def places():
        for source in range(grid):
            for row in range(share):
                first, second = (
                    pl.ds((band * grid + source) * chunk + row, planes, stride=share) for band in range(2)
                )
                here = (pl.ds(source * planes, planes), slice(row * LANES, (row + 1) * LANES))
                yield first, second, here

    for first, second, here in places():
        lines[here] = spec_ref[first, :] + spec_ref[second, :]
    index = lax.broadcasted_iota(jnp.int32, lines.shape, 0)
    order = jnp.where(index <= length // 2, index, index - length // 2).astype(jnp.float32)
    total = order * order + cells_ref[...]
    scale = length * math.sqrt(length) / 16.0
    kernel = jnp.where(total > 0.0, scale / (total + 1.0), 0.0)
    field = kernel * product(tables_ref[0], lines[...])
    lines[...] = product_of_parts(split(tables_ref[1]), split(field))
    some = planes // 2
    chunk = whole_tiles(some * share)
    for part, out_ref in enumerate((upper_ref, lower_ref)):
        for source in range(grid):
            for row in range(share):
                piece = lines[pl.ds(source * planes + part * some, some), row * LANES : (row + 1) * LANES]
                out_ref[pl.ds(source * chunk + row, some, stride=share), :] = piece
            if some * share < chunk:
                rest = chunk - some * share
                out_ref[pl.ds(source * chunk + some * share, rest), :] = jnp.zeros((rest, LANES), jnp.float32)


def last_kernel(
    sizes, bunch, place_ref, near_ref, far_ref, upper_ref, lower_ref, upper_other, lower_other, tables_ref, *refs
):
    planes, grid, rows, share = sizes
    out_ref, packed = refs[-2:]
    length = planes * grid
    half = rows * grid // 2
    chunk = whole_tiles(planes // 2 * share)
    turn, basis = split(tables_ref[1]), split(tables_ref[0])
    band = place_ref[0] // grid
    lines = []
    for inner in range(bunch):
        plane = pl.program_id(0) * bunch + inner
        slot = packed.at[inner * 2]
        for part, spec_ref in ((band, near_ref), (1 - band, far_ref)):
            side = slot.at[pl.ds(pl.multiple_of(part * half, 8), half), :]
            for source in range(grid):
                start = source * chunk + plane * share
                move(side, source * share, spec_ref, start, share)
        lines.append(product_of_parts(turn, split(unpack(slot, length))))
    hartree = product_of_parts(split(jnp.concatenate(lines, axis=0)), basis)
    for inner in range(bunch):
        slot = packed.at[inner * 2 + 1]
        here = slice(inner * half, (inner + 1) * half)
        slot[:half, :] = upper_ref[here, :] + upper_other[here, :]
        slot[half:, :] = lower_ref[here, :] + lower_other[here, :]
        root = jnp.exp(jnp.log(unpack(slot, length)) * (1.0 / 3.0))
        out_ref[inner] = hartree[inner * length : (inner + 1) * length, :] - XC_FACTOR * root


def shape(*dims):
    return jax.ShapeDtypeStruct(dims, jnp.float32)


def whole(*dims):
    return pl.BlockSpec(dims, lambda *_: (0,) * len(dims))


SMALL = pltpu.CompilerParams(vmem_limit_bytes=24 << 20)
PARAMS = pltpu.CompilerParams(vmem_limit_bytes=54 << 20)


def cost(flops, moved):
    return pl.CostEstimate(flops=flops, bytes_accessed=moved, transcendentals=0)


def turn_order(grid):
    order = [0]
    for near in range(grid // 2):
        order += [near, near + grid // 2] if near else [grid // 2]
    return order


def packed_path(orbitals, occupations, ion_potential, hxc_potential):
    length = orbitals.shape[-1]
    planes = orbitals.shape[2]
    grid = lax.axis_size("grid")
    cell_rows = length * length // LANES
    rows = cell_rows // grid
    share = rows // 2
    sizes = (planes, grid, rows, share)
    field = planes * cell_rows
    work = 2 * planes * length**3
    place = lax.axis_index(("band", "grid")).astype(jnp.int32).reshape(1)
    kin = jnp.asarray(kinetic_matrix(length))
    basis_np, squares_np = real_basis(length)
    tables = jnp.asarray(np.stack([basis_np, basis_np.T]))
    smem = pl.BlockSpec(memory_space=pltpu.SMEM)
    vmem = pl.BlockSpec(memory_space=pltpu.VMEM)
    some = planes // 2
    bunch = next(count for count in (3, 2, 1) if some % count == 0)
    groups = some // bunch
    psi_spec = pl.BlockSpec((1, 2, bunch, length, length), lambda i: (0, 0, i, 0, 0))
    plane_spec = pl.BlockSpec((bunch, length, length), lambda i: (i, 0, 0))
    pair_spec = pl.BlockSpec((2, bunch, length, length), lambda i: (0, i, 0, 0))
    half_rows = pl.BlockSpec((bunch * cell_rows // 2, LANES), lambda i: (i, 0))
    part_rows = grid * whole_tiles(some * share)
    square = whole(length, length)
    table_spec = whole(2, length, length)

    def scratch(count):
        return [pltpu.VMEM((count * bunch, cell_rows, LANES), jnp.float32)]

    line = []

    def send(turn, piece, *gates):
        if not turn:
            return piece
        if len(line) >= 5:
            gates += (line[-5],)
        if gates:
            piece = lax.optimization_barrier((piece, *gates))[0]
        line.append(lax.ppermute(piece, "grid", [(spot, spot ^ turn) for spot in range(grid)]))
        return line[-1]

    def swap(array):
        flat = array.reshape(grid, -1, LANES)
        return lax.all_to_all(flat, "grid", split_axis=0, concat_axis=0).reshape(array.shape)

    def swap_all(array):
        flat = array.reshape(2 * grid, -1, LANES)
        return lax.all_to_all(flat, ("band", "grid"), split_axis=0, concat_axis=0).reshape(array.shape)

    turns = turn_order(grid)
    spec_rows = 2 * grid * chunk_rows(sizes)
    mixed_rows = 2 * planes * rows
    steps = 6 if rows % 6 == 0 and share % (rows // 6) == 0 else 2
    shared = pl.pallas_call(
        functools.partial(potential_kernel, sizes, bunch),
        grid=(planes // bunch,),
        in_specs=[smem, plane_spec, plane_spec],
        out_specs=whole(spec_rows // 2, LANES),
        out_shape=shape(spec_rows // 2, LANES),
        scratch_shapes=scratch(1),
        compiler_params=PARAMS,
        cost_estimate=cost(0, 6 << 20),
    )(place, ion_potential, hxc_potential)
    place, shared = lax.optimization_barrier((place, shared))
    shared = swap(shared)
    moved = pl.pallas_call(
        functools.partial(pack_kernel, sizes, bunch, turns),
        grid=(planes // bunch,),
        in_specs=[smem, psi_spec],
        out_specs=[whole(mixed_rows, LANES)] * grid,
        out_shape=[shape(mixed_rows, LANES)] * grid,
        scratch_shapes=scratch(2),
        compiler_params=PARAMS,
        cost_estimate=cost(0, 8 << 20),
    )(place, orbitals)
    moved = [send(turn, piece) for turn, piece in zip(turns[:6], moved[:6])] + list(moved[6:])
    behind = lax.optimization_barrier((place, line[1]))[0]
    *mixed, base = pl.pallas_call(
        functools.partial(plane_kernel, sizes, bunch, turns),
        grid=(planes // bunch,),
        in_specs=[smem, psi_spec, plane_spec, plane_spec, square],
        out_specs=[whole(mixed_rows, LANES)] * grid + [pair_spec],
        out_shape=[shape(mixed_rows, LANES)] * grid + [shape(2, planes, length, length)],
        scratch_shapes=scratch(2),
        compiler_params=PARAMS,
        cost_estimate=cost(8 * 3 * work, 20 << 20),
    )(behind, orbitals, ion_potential, hxc_potential, kin)
    for index in range(6, grid):
        moved[index] = send(turns[index], moved[index], *([base] if index < 11 else []))
    own = pl.pallas_call(
        functools.partial(share_kernel, sizes),
        in_specs=[vmem],
        out_specs=vmem,
        out_shape=shape(share * length, LANES),
        compiler_params=PARAMS,
        cost_estimate=cost(0, 2 << 20),
    )(shared)
    other = lax.ppermute(own, "band", [(0, 1), (1, 0)])
    along = pl.pallas_call(
        functools.partial(along_kernel, sizes, steps, turns),
        grid=(steps,),
        in_specs=[smem] + [whole(mixed_rows, LANES)] * grid + [square],
        out_specs=pl.BlockSpec((rows // steps * length, 2 * LANES), lambda i: (i, 0)),
        out_shape=shape(rows * length, 2 * LANES),
        scratch_shapes=[pltpu.VMEM((rows // steps, 2, length, LANES), jnp.float32)],
        compiler_params=PARAMS,
        cost_estimate=cost(2 * 3 * work, 8 << 20),
    )(place, *moved, kin)
    mixed = [send(turn, piece) for turn, piece in zip(turns, mixed)]
    half_spec = pl.BlockSpec((rows // steps * length, LANES), lambda i: (i % (steps // 2), 0))
    update = pl.pallas_call(
        functools.partial(update_kernel, sizes, steps, turns),
        grid=(steps,),
        in_specs=[
            smem,
            pl.BlockSpec((rows // steps * length, 2 * LANES), lambda i: (i, 0)),
            half_spec,
            half_spec,
            square,
        ]
        + [whole(mixed_rows, LANES)] * grid,
        out_specs=whole(2 * field, LANES),
        out_shape=shape(2 * field, LANES),
        scratch_shapes=[pltpu.VMEM((rows // steps, 2, length, LANES), jnp.float32)],
        compiler_params=PARAMS,
        cost_estimate=cost(2 * 3 * work, 14 << 20),
    )(place, along, own, other, kin, *mixed)
    update = swap(update)

    fresh, upper, lower, spectrum = pl.pallas_call(
        functools.partial(fresh_kernel, sizes, bunch),
        grid=(planes // bunch,),
        in_specs=[smem, vmem, pair_spec, table_spec],
        out_specs=[
            psi_spec,
            half_rows,
            half_rows,
            whole(spec_rows, LANES),
        ],
        out_shape=[
            shape(*orbitals.shape),
            shape(field // 2, LANES),
            shape(field // 2, LANES),
            shape(spec_rows, LANES),
        ],
        scratch_shapes=scratch(4),
        compiler_params=PARAMS,
        cost_estimate=cost(2 * 6 * work, 16 << 20),
    )(occupations, update, base, tables)
    upper_other = lax.ppermute(upper, "band", [(0, 1), (1, 0)])
    lower_other = lax.ppermute(lower, "band", [(0, 1), (1, 0)])

    spectrum = swap_all(spectrum)
    cells_np = squares_np[:, None] + squares_np[None, :]
    half = length // 2
    cells_np = np.concatenate(
        [cells_np[:, :LANES], np.concatenate([cells_np[:half, LANES:], cells_np[half:, LANES:]], axis=1)]
    )
    device = lax.axis_index("band") * grid + lax.axis_index("grid")
    cells = lax.dynamic_slice_in_dim(jnp.asarray(cells_np), device * share, share, axis=0)
    first, second = pl.pallas_call(
        functools.partial(filter_kernel, sizes),
        in_specs=[vmem] * 3,
        out_specs=[vmem] * 2,
        out_shape=[shape(part_rows, LANES)] * 2,
        scratch_shapes=[pltpu.VMEM((length, share * LANES), jnp.float32)],
        compiler_params=SMALL,
        cost_estimate=cost(6 * work, 5 << 20),
    )(spectrum, cells.reshape(1, share * LANES), tables)

    def last_part(part, near, far, made):
        cells_spec = pl.BlockSpec((bunch * cell_rows // 2, LANES), lambda i: (i + part * groups, 0))
        return pl.pallas_call(
            functools.partial(last_kernel, sizes, bunch),
            grid=(groups,),
            in_specs=[smem, vmem, vmem]
            + [cells_spec] * 4
            + [table_spec]
            + [pl.BlockSpec(memory_space=pl.ANY)] * len(made),
            out_specs=pl.BlockSpec((bunch, length, length), lambda i: (i + part * groups, 0, 0)),
            out_shape=shape(planes, length, length),
            scratch_shapes=scratch(2),
            input_output_aliases={8: 0} if made else {},
            compiler_params=PARAMS,
            cost_estimate=cost(3 * work, 4 << 20),
        )(place, near, far, upper, lower, upper_other, lower_other, tables, *made)

    first, upper_other = lax.optimization_barrier((first, upper_other))
    near = swap(first)
    far = lax.ppermute(near, "band", [(0, 1), (1, 0)])
    second, lower_other = lax.optimization_barrier((second, lower_other))
    near_second = swap(second)
    far_second = lax.ppermute(near_second, "band", [(0, 1), (1, 0)])
    potential = last_part(0, near, far, [])
    potential = last_part(1, near_second, far_second, [potential])
    return (fresh, potential)


def local(orbitals, occupations, ion_potential, hxc_potential):
    length = orbitals.shape[-1]
    parts = 2 * lax.axis_size("grid") * LANES
    fits = lax.axis_size("grid") & (lax.axis_size("grid") - 1) == 0
    fits = fits and orbitals.shape[2] % 2 == 0 and length == LANES + LANES // 2 and lax.axis_size("band") == 2 and length * length % parts == 0
    path = packed_path if fits else general
    return path(orbitals, occupations, ion_potential, hxc_potential)


def solution(mesh):
    placed = (
        P("band", None, "grid", None, None),
        P("band"),
        P("grid", None, None),
        P("grid", None, None),
    )
    return jax.shard_map(
        local,
        mesh=mesh,
        in_specs=placed,
        out_specs=(P("band", None, "grid", None, None), P("grid", None, None)),
        check_vma=False,
    )
```

```python
import functools
import math

import jax
import jax.numpy as jnp
import numpy as np
from jax import lax
from jax.experimental import pallas as pl
from jax.experimental.pallas import tpu as pltpu
from jax.sharding import PartitionSpec as P

BESSEL_ZERO = 0.8462873527504802
BESSEL_ONE = 0.36884204609417703
BESSEL_TWO = 0.07581776248
XC_FACTOR = 0.98474502
PRECISION = lax.Precision.HIGH


def kinetic_matrix(length):
    idx = np.arange(length)
    freq = np.where(idx < length // 2, idx, idx - length).astype(np.float64)
    wave = np.cos(2.0 * math.pi * (np.outer(idx, idx) % length) / length)
    row = (wave @ (freq * freq)) / length * (2.0 / (3.0 * (length / 2) ** 2))
    return row[(idx[:, None] - idx[None, :]) % length].astype(np.float32)


def real_basis(length):
    half = length // 2
    idx = np.arange(length)
    order = np.concatenate([np.arange(half + 1), np.arange(1, half)])
    angle = 2.0 * math.pi * (np.outer(order, idx) % length) / length
    table = np.where((np.arange(length) <= half)[:, None], np.cos(angle), np.sin(angle))
    scale = np.where((order == 0) | (order == half), math.sqrt(1.0 / length), math.sqrt(2.0 / length))
    return (table * scale[:, None]).astype(np.float32), (order * order).astype(np.float32)


def dot(form, left, right):
    return jnp.einsum(form, left, right, precision=PRECISION)


def general(orbitals, occupations, ion_potential, hxc_potential):
    length = orbitals.shape[-1]
    planes = orbitals.shape[2]
    grid = lax.axis_size("grid")
    bands = lax.axis_size("band")
    cells = length * length
    columns = cells // grid
    share = cells // (grid * bands)
    kin = jnp.asarray(kinetic_matrix(length))
    kin_x = kin.reshape(length, grid, planes)
    basis_np, squares = real_basis(length)
    basis = jnp.asarray(basis_np)
    basis_x = basis.reshape(length, grid, planes)

    psi = orbitals[0]
    potential = ion_potential + hxc_potential

    def scatter(fields):
        parts = fields.reshape(fields.shape[0], planes, grid, columns).transpose(2, 1, 0, 3)
        return lax.all_to_all(parts, "grid", split_axis=0, concat_axis=0)

    def along_yz(field):
        return dot("cxyz,zk->cxyk", field, kin) + dot("cxyz,yk->cxkz", field, kin)

    moved = scatter(jnp.concatenate([psi, potential[None]], axis=0))
    local_kin = along_yz(psi) - psi
    applied = local_kin + potential * psi
    mixed = scatter(local_kin + applied)
    twice = along_yz(applied) - applied + potential * applied

    along = dot("ksp,spcn->ckn", kin_x, moved[:, :, :2])
    again = dot("ksp,spcn->ckn", kin_x, mixed) + dot("kx,cxn->ckn", kin, along)
    potential_cols = moved[:, :, 2].reshape(length, columns)
    again = again + potential_cols * along
    turned = jnp.stack([along[1], -along[0]])
    update = 2.0 * BESSEL_ONE * turned - 4.0 * BESSEL_TWO * again
    update = update.reshape(2, grid, planes, columns).transpose(1, 2, 0, 3)
    update = lax.all_to_all(update, "grid", split_axis=0, concat_axis=0)
    update = update.transpose(2, 1, 0, 3).reshape(psi.shape)

    turned = jnp.stack([applied[1], -applied[0]])
    fresh = (
        (BESSEL_ZERO + 2.0 * BESSEL_TWO) * psi
        + 2.0 * BESSEL_ONE * turned
        - 4.0 * BESSEL_TWO * twice
        + update
    )
    part = occupations[0] * (fresh[0] * fresh[0] + fresh[1] * fresh[1])
    density = lax.psum(part, "band")

    spectrum = dot("xyz,kz->xyk", part, basis)
    spectrum = dot("xyk,jy->xjk", spectrum, basis)
    spectrum = spectrum.reshape(planes, bands * grid, share).transpose(1, 0, 2)
    spectrum = lax.all_to_all(spectrum, ("band", "grid"), split_axis=0, concat_axis=0)
    spectrum = spectrum.reshape(bands, grid, planes, share).sum(axis=0)
    spectrum = dot("ksp,spn->kn", basis_x, spectrum)
    start = (lax.axis_index("band") * grid + lax.axis_index("grid")) * share
    cell = start + jnp.arange(share, dtype=jnp.int32)
    table = jnp.asarray(squares)
    total = table[:, None] + (table[cell // length] + table[cell % length])[None, :]
    kernel = jnp.where(total > 0, length * math.sqrt(length) / 16.0 / (total + 1.0), 0.0)
    spectrum = dot("kx,kn->xn", basis, kernel * spectrum)
    spectrum = spectrum.reshape(1, grid, planes, share)
    spectrum = jnp.broadcast_to(spectrum, (bands, grid, planes, share)).reshape(bands * grid, planes, share)
    spectrum = lax.all_to_all(spectrum, ("band", "grid"), split_axis=0, concat_axis=0)
    spectrum = spectrum.transpose(1, 0, 2).reshape(planes, length, length)
    spectrum = dot("xjk,jy->xyk", spectrum, basis)
    hartree = dot("xyk,kz->xyz", spectrum, basis)
    return (fresh[None], hartree - XC_FACTOR * jnp.cbrt(density))


LANES = 128


def product(left, right):
    return jnp.dot(left, right, precision=lax.Precision.HIGHEST, preferred_element_type=jnp.float32)


def split(array):
    high = array.astype(jnp.bfloat16)
    return high, (array - high.astype(jnp.float32)).astype(jnp.bfloat16)


def product_of_parts(left, right):
    total = jnp.dot(left[0], right[0], preferred_element_type=jnp.float32)
    total = total + jnp.dot(left[1], right[0], preferred_element_type=jnp.float32)
    return total + jnp.dot(left[0], right[1], preferred_element_type=jnp.float32)


def whole_tiles(rows):
    return -(-rows // 8) * 8


def chunk_rows(sizes):
    planes, _, rows, share = sizes
    return whole_tiles(planes * share)


def kinetic(plane, kin):
    plane = split(plane)
    return product_of_parts(plane, kin) + product_of_parts(kin, plane)


def pack(plane, packed):
    length = plane.shape[0]
    half = length // 2
    packed[:length, :] = plane[:, :LANES]
    packed[length:, :] = jnp.concatenate([plane[:half, LANES:], plane[half:, LANES:]], axis=1)


def unpack(packed, length):
    side = length - LANES
    tail = packed[length:, :]
    right = jnp.concatenate([tail[:, :side], tail[:, side:]], axis=0)
    return jnp.concatenate([packed[:length, :], right], axis=1)


def fill(out_ref, count, chunk, used):
    if used < chunk:

        @pl.when(pl.program_id(0) == 0)
        def _():
            for to in range(count):
                out_ref[pl.ds(to * chunk + used, chunk - used), :] = jnp.zeros((chunk - used, LANES), jnp.float32)


def move(to_ref, to, from_ref, start, count, step=1):
    if count < 8:
        to_ref[pl.ds(to, count), :] = from_ref[pl.ds(start, count, stride=step), :]
        return
    for first in [*range(0, count - 7, 8)] + ([count - 8] if count % 8 else []):
        to_ref[pl.ds(to + first, 8), :] = from_ref[pl.ds(start + first * step, 8, stride=step), :]


def potential_kernel(sizes, bunch, place_ref, ion_ref, hxc_ref, out_ref, packed):
    planes, grid, rows, share = sizes
    chunk = chunk_rows(sizes)
    band = place_ref[0] // grid
    fill(out_ref, grid, chunk, planes * share)
    for inner in range(bunch):
        plane = pl.program_id(0) * bunch + inner
        slot = packed.at[inner]
        pack(ion_ref[inner] + hxc_ref[inner], slot)
        for to in range(grid):
            start = to * rows + band * share
            move(out_ref, to * chunk + plane * share, slot, start, share)


def pack_kernel(sizes, bunch, turns, place_ref, psi_ref, *refs):
    planes, grid, rows, share = sizes
    *out_refs, packed = refs
    mine = place_ref[0] % grid
    for inner in range(bunch):
        plane = pl.program_id(0) * bunch + inner
        for part in range(2):
            slot = packed.at[inner * 2 + part]
            pack(psi_ref[0, part, inner], slot)
            for turn, out_ref in zip(turns, out_refs):
                start = (mine ^ turn) * rows
                move(out_ref, (plane * 2 + part) * rows, slot, start, rows)


def plane_kernel(sizes, bunch, turns, place_ref, psi_ref, ion_ref, hxc_ref, kin_ref, *refs):
    planes, grid, rows, share = sizes
    *out_refs, base_ref, packed = refs
    mine = place_ref[0] % grid
    kin = split(kin_ref[...])
    for inner in range(bunch):
        plane = pl.program_id(0) * bunch + inner
        potential = ion_ref[inner] + hxc_ref[inner]
        applied = []
        for part in range(2):
            field = psi_ref[0, part, inner]
            bare = kinetic(field, kin) - field
            applied.append(bare + potential * field)
            slot = packed.at[inner * 2 + part]
            pack(bare + applied[part], slot)
            for turn, out_ref in zip(turns, out_refs):
                start = (mine ^ turn) * rows
                move(out_ref, (plane * 2 + part) * rows, slot, start, rows)
        for part in range(2):
            twice = kinetic(applied[part], kin) + (potential - 1.0) * applied[part]
            turned = applied[1] if part == 0 else -applied[0]
            base_ref[part, inner] = (
                (BESSEL_ZERO + 2.0 * BESSEL_TWO) * psi_ref[0, part, inner]
                + 2.0 * BESSEL_ONE * turned
                - 4.0 * BESSEL_TWO * twice
            )


def share_kernel(sizes, moved_ref, out_ref):
    planes, grid, rows, share = sizes
    length = planes * grid
    chunk = chunk_rows(sizes)
    for source in range(grid):
        for row in range(share):
            start = source * chunk + row
            move(out_ref, row * length + source * planes, moved_ref, start, planes, share)


def along_kernel(sizes, steps, turns, place_ref, *refs):
    planes, grid, rows, share = sizes
    *moved_refs, kin_ref, out_ref, lines = refs
    length = planes * grid
    kin = split(kin_ref[...])
    for inner in range(rows // steps):
        row = pl.program_id(0) * (rows // steps) + inner
        slot = lines.at[inner]
        for turn, moved_ref in zip(turns, moved_refs):
            first = (place_ref[0] % grid ^ turn) * planes
            for part in range(2):
                move(slot.at[part], first, moved_ref, part * rows + row, planes, 2 * rows)
        field = jnp.concatenate([slot[0], slot[1]], axis=1)
        out_ref[inner * length : (inner + 1) * length, :] = product_of_parts(kin, split(field))


def update_kernel(sizes, steps, turns, place_ref, along_ref, own_ref, other_ref, kin_ref, *refs):
    planes, grid, rows, share = sizes
    *mixed_refs, out_ref, lines = refs
    length = planes * grid
    kin = split(kin_ref[...])
    step = pl.program_id(0)
    mine_here = place_ref[0] // grid == step // (steps // 2)
    for inner in range(rows // steps):
        row = step * (rows // steps) + inner
        here = slice(inner * length, (inner + 1) * length)
        slot = lines.at[inner]
        for turn, mixed_ref in zip(turns, mixed_refs):
            first = (place_ref[0] % grid ^ turn) * planes
            for part in range(2):
                move(slot.at[part], first, mixed_ref, part * rows + row, planes, 2 * rows)
        along = along_ref[here, :]
        again = product_of_parts(kin, split(jnp.concatenate([slot[0], slot[1]], axis=1) + along))
        potential = jnp.where(mine_here, own_ref[here, :], other_ref[here, :])
        for part in range(2):
            mine = along[:, part * LANES : (part + 1) * LANES]
            turned = along[:, LANES:] if part == 0 else -along[:, :LANES]
            twice = again[:, part * LANES : (part + 1) * LANES] + potential * mine
            out_ref[pl.ds(part * rows + row, length, stride=2 * rows), :] = (
                2.0 * BESSEL_ONE * turned - 4.0 * BESSEL_TWO * twice
            )


def fresh_kernel(
    sizes, bunch, occ_ref, update_ref, base_ref, tables_ref, fresh_ref, upper_ref, lower_ref, out_ref, packed
):
    planes, grid, rows, share = sizes
    length = planes * grid
    chunk = chunk_rows(sizes)
    cell_rows = rows * grid
    half = cell_rows // 2
    fill(out_ref, 2 * grid, chunk, planes * share)
    means, parts = [], []
    for inner in range(bunch):
        plane = pl.program_id(0) * bunch + inner
        part_sum = None
        for part in range(2):
            slot = packed.at[inner * 4 + part]
            for source in range(grid):
                start = ((source * planes + plane) * 2 + part) * rows
                move(slot, source * rows, update_ref, start, rows)
            fresh = base_ref[part, inner] + unpack(slot, length)
            fresh_ref[0, part, inner] = fresh
            part_sum = fresh * fresh if part_sum is None else part_sum + fresh * fresh
        part_sum = occ_ref[0] * part_sum
        slot = packed.at[inner * 4 + 2]
        pack(part_sum, slot)
        upper_ref[inner * half : (inner + 1) * half, :] = slot[:half, :]
        lower_ref[inner * half : (inner + 1) * half, :] = slot[half:, :]
        means.append(jnp.sum(part_sum) * (1.0 / length**2))
        parts.append(part_sum - means[inner])
    basis, turn = split(tables_ref[0]), split(tables_ref[1])
    along_z = product_of_parts(split(jnp.concatenate(parts, axis=0)), turn)
    first = (lax.broadcasted_iota(jnp.int32, (length, length), axis) == 0 for axis in range(2))
    first = jnp.logical_and(*first)
    for inner in range(bunch):
        plane = pl.program_id(0) * bunch + inner
        spectrum = product_of_parts(basis, split(along_z[inner * length : (inner + 1) * length, :]))
        slot = packed.at[inner * 4 + 3]
        pack(spectrum + jnp.where(first, means[inner] * length, 0.0), slot)
        for to in range(2 * grid):
            move(out_ref, to * chunk + plane * share, slot, to * share, share)


def filter_kernel(sizes, spec_ref, cells_ref, tables_ref, upper_ref, lower_ref, lines):
    planes, grid, rows, share = sizes
    length = planes * grid
    chunk = chunk_rows(sizes)

    def places():
        for source in range(grid):
            for row in range(share):
                first, second = (
                    pl.ds((band * grid + source) * chunk + row, planes, stride=share) for band in range(2)
                )
                here = (pl.ds(source * planes, planes), slice(row * LANES, (row + 1) * LANES))
                yield first, second, here

    for first, second, here in places():
        lines[here] = spec_ref[first, :] + spec_ref[second, :]
    index = lax.broadcasted_iota(jnp.int32, lines.shape, 0)
    order = jnp.where(index <= length // 2, index, index - length // 2).astype(jnp.float32)
    total = order * order + cells_ref[...]
    scale = length * math.sqrt(length) / 16.0
    kernel = jnp.where(total > 0.0, scale / (total + 1.0), 0.0)
    field = kernel * product(tables_ref[0], lines[...])
    lines[...] = product_of_parts(split(tables_ref[1]), split(field))
    some = planes // 2
    chunk = whole_tiles(some * share)
    for part, out_ref in enumerate((upper_ref, lower_ref)):
        for source in range(grid):
            for row in range(share):
                piece = lines[pl.ds(source * planes + part * some, some), row * LANES : (row + 1) * LANES]
                out_ref[pl.ds(source * chunk + row, some, stride=share), :] = piece
            if some * share < chunk:
                rest = chunk - some * share
                out_ref[pl.ds(source * chunk + some * share, rest), :] = jnp.zeros((rest, LANES), jnp.float32)


def last_kernel(
    sizes, bunch, place_ref, near_ref, far_ref, upper_ref, lower_ref, upper_other, lower_other, tables_ref, *refs
):
    planes, grid, rows, share = sizes
    out_ref, packed = refs[-2:]
    length = planes * grid
    half = rows * grid // 2
    chunk = whole_tiles(planes // 2 * share)
    turn, basis = split(tables_ref[1]), split(tables_ref[0])
    band = place_ref[0] // grid
    lines = []
    for inner in range(bunch):
        plane = pl.program_id(0) * bunch + inner
        slot = packed.at[inner * 2]
        for part, spec_ref in ((band, near_ref), (1 - band, far_ref)):
            side = slot.at[pl.ds(pl.multiple_of(part * half, 8), half), :]
            for source in range(grid):
                start = source * chunk + plane * share
                move(side, source * share, spec_ref, start, share)
        lines.append(product_of_parts(turn, split(unpack(slot, length))))
    hartree = product_of_parts(split(jnp.concatenate(lines, axis=0)), basis)
    for inner in range(bunch):
        slot = packed.at[inner * 2 + 1]
        here = slice(inner * half, (inner + 1) * half)
        slot[:half, :] = upper_ref[here, :] + upper_other[here, :]
        slot[half:, :] = lower_ref[here, :] + lower_other[here, :]
        root = jnp.exp(jnp.log(unpack(slot, length)) * (1.0 / 3.0))
        out_ref[inner] = hartree[inner * length : (inner + 1) * length, :] - XC_FACTOR * root


def shape(*dims):
    return jax.ShapeDtypeStruct(dims, jnp.float32)


def whole(*dims):
    return pl.BlockSpec(dims, lambda *_: (0,) * len(dims))


SMALL = pltpu.CompilerParams(vmem_limit_bytes=24 << 20)
PARAMS = pltpu.CompilerParams(vmem_limit_bytes=54 << 20)


def cost(flops, moved):
    return pl.CostEstimate(flops=flops, bytes_accessed=moved, transcendentals=0)


def turn_order(grid):
    order = [0]
    for near in range(grid // 2):
        order += [near, near + grid // 2] if near else [grid // 2]
    return order


def packed_path(orbitals, occupations, ion_potential, hxc_potential):
    length = orbitals.shape[-1]
    planes = orbitals.shape[2]
    grid = lax.axis_size("grid")
    cell_rows = length * length // LANES
    rows = cell_rows // grid
    share = rows // 2
    sizes = (planes, grid, rows, share)
    field = planes * cell_rows
    work = 2 * planes * length**3
    place = lax.axis_index(("band", "grid")).astype(jnp.int32).reshape(1)
    kin = jnp.asarray(kinetic_matrix(length))
    basis_np, squares_np = real_basis(length)
    tables = jnp.asarray(np.stack([basis_np, basis_np.T]))
    smem = pl.BlockSpec(memory_space=pltpu.SMEM)
    vmem = pl.BlockSpec(memory_space=pltpu.VMEM)
    some = planes // 2
    bunch = next(count for count in (3, 2, 1) if some % count == 0)
    groups = some // bunch
    psi_spec = pl.BlockSpec((1, 2, bunch, length, length), lambda i: (0, 0, i, 0, 0))
    plane_spec = pl.BlockSpec((bunch, length, length), lambda i: (i, 0, 0))
    pair_spec = pl.BlockSpec((2, bunch, length, length), lambda i: (0, i, 0, 0))
    half_rows = pl.BlockSpec((bunch * cell_rows // 2, LANES), lambda i: (i, 0))
    part_rows = grid * whole_tiles(some * share)
    square = whole(length, length)
    table_spec = whole(2, length, length)

    def scratch(count):
        return [pltpu.VMEM((count * bunch, cell_rows, LANES), jnp.float32)]

    line = []

    def send(turn, piece, *gates):
        if not turn:
            return piece
        if len(line) >= 5:
            gates += (line[-5],)
        if gates:
            piece = lax.optimization_barrier((piece, *gates))[0]
        line.append(lax.ppermute(piece, "grid", [(spot, spot ^ turn) for spot in range(grid)]))
        return line[-1]

    def swap(array):
        flat = array.reshape(grid, -1, LANES)
        return lax.all_to_all(flat, "grid", split_axis=0, concat_axis=0).reshape(array.shape)

    def swap_all(array):
        flat = array.reshape(2 * grid, -1, LANES)
        return lax.all_to_all(flat, ("band", "grid"), split_axis=0, concat_axis=0).reshape(array.shape)

    turns = turn_order(grid)
    spec_rows = 2 * grid * chunk_rows(sizes)
    mixed_rows = 2 * planes * rows
    steps = 6 if rows % 6 == 0 and share % (rows // 6) == 0 else 2
    shared = pl.pallas_call(
        functools.partial(potential_kernel, sizes, bunch),
        grid=(planes // bunch,),
        in_specs=[smem, plane_spec, plane_spec],
        out_specs=whole(spec_rows // 2, LANES),
        out_shape=shape(spec_rows // 2, LANES),
        scratch_shapes=scratch(1),
        compiler_params=PARAMS,
        cost_estimate=cost(0, 6 << 20),
    )(place, ion_potential, hxc_potential)
    place, shared = lax.optimization_barrier((place, shared))
    shared = swap(shared)
    moved = pl.pallas_call(
        functools.partial(pack_kernel, sizes, bunch, turns),
        grid=(planes // bunch,),
        in_specs=[smem, psi_spec],
        out_specs=[whole(mixed_rows, LANES)] * grid,
        out_shape=[shape(mixed_rows, LANES)] * grid,
        scratch_shapes=scratch(2),
        compiler_params=PARAMS,
        cost_estimate=cost(0, 8 << 20),
    )(place, orbitals)
    moved = [send(turn, piece) for turn, piece in zip(turns[:6], moved[:6])] + list(moved[6:])
    behind = lax.optimization_barrier((place, line[1]))[0]
    *mixed, base = pl.pallas_call(
        functools.partial(plane_kernel, sizes, bunch, turns),
        grid=(planes // bunch,),
        in_specs=[smem, psi_spec, plane_spec, plane_spec, square],
        out_specs=[whole(mixed_rows, LANES)] * grid + [pair_spec],
        out_shape=[shape(mixed_rows, LANES)] * grid + [shape(2, planes, length, length)],
        scratch_shapes=scratch(2),
        compiler_params=PARAMS,
        cost_estimate=cost(8 * 3 * work, 20 << 20),
    )(behind, orbitals, ion_potential, hxc_potential, kin)
    for index in range(6, grid):
        moved[index] = send(turns[index], moved[index], *([base] if index < 11 else []))
    own = pl.pallas_call(
        functools.partial(share_kernel, sizes),
        in_specs=[vmem],
        out_specs=vmem,
        out_shape=shape(share * length, LANES),
        compiler_params=PARAMS,
        cost_estimate=cost(0, 2 << 20),
    )(shared)
    other = lax.ppermute(own, "band", [(0, 1), (1, 0)])
    along = pl.pallas_call(
        functools.partial(along_kernel, sizes, steps, turns),
        grid=(steps,),
        in_specs=[smem] + [whole(mixed_rows, LANES)] * grid + [square],
        out_specs=pl.BlockSpec((rows // steps * length, 2 * LANES), lambda i: (i, 0)),
        out_shape=shape(rows * length, 2 * LANES),
        scratch_shapes=[pltpu.VMEM((rows // steps, 2, length, LANES), jnp.float32)],
        compiler_params=PARAMS,
        cost_estimate=cost(2 * 3 * work, 8 << 20),
    )(place, *moved, kin)
    mixed = [send(turn, piece) for turn, piece in zip(turns, mixed)]
    half_spec = pl.BlockSpec((rows // steps * length, LANES), lambda i: (i % (steps // 2), 0))
    update = pl.pallas_call(
        functools.partial(update_kernel, sizes, steps, turns),
        grid=(steps,),
        in_specs=[
            smem,
            pl.BlockSpec((rows // steps * length, 2 * LANES), lambda i: (i, 0)),
            half_spec,
            half_spec,
            square,
        ]
        + [whole(mixed_rows, LANES)] * grid,
        out_specs=whole(2 * field, LANES),
        out_shape=shape(2 * field, LANES),
        scratch_shapes=[pltpu.VMEM((rows // steps, 2, length, LANES), jnp.float32)],
        compiler_params=PARAMS,
        cost_estimate=cost(2 * 3 * work, 14 << 20),
    )(place, along, own, other, kin, *mixed)
    update = swap(update)

    fresh, upper, lower, spectrum = pl.pallas_call(
        functools.partial(fresh_kernel, sizes, bunch),
        grid=(planes // bunch,),
        in_specs=[smem, vmem, pair_spec, table_spec],
        out_specs=[
            psi_spec,
            half_rows,
            half_rows,
            whole(spec_rows, LANES),
        ],
        out_shape=[
            shape(*orbitals.shape),
            shape(field // 2, LANES),
            shape(field // 2, LANES),
            shape(spec_rows, LANES),
        ],
        scratch_shapes=scratch(4),
        compiler_params=PARAMS,
        cost_estimate=cost(2 * 6 * work, 16 << 20),
    )(occupations, update, base, tables)
    upper_other = lax.ppermute(upper, "band", [(0, 1), (1, 0)])
    lower_other = lax.ppermute(lower, "band", [(0, 1), (1, 0)])

    spectrum = swap_all(spectrum)
    cells_np = squares_np[:, None] + squares_np[None, :]
    half = length // 2
    cells_np = np.concatenate(
        [cells_np[:, :LANES], np.concatenate([cells_np[:half, LANES:], cells_np[half:, LANES:]], axis=1)]
    )
    device = lax.axis_index("band") * grid + lax.axis_index("grid")
    cells = lax.dynamic_slice_in_dim(jnp.asarray(cells_np), device * share, share, axis=0)
    first, second = pl.pallas_call(
        functools.partial(filter_kernel, sizes),
        in_specs=[vmem] * 3,
        out_specs=[vmem] * 2,
        out_shape=[shape(part_rows, LANES)] * 2,
        scratch_shapes=[pltpu.VMEM((length, share * LANES), jnp.float32)],
        compiler_params=SMALL,
        cost_estimate=cost(6 * work, 5 << 20),
    )(spectrum, cells.reshape(1, share * LANES), tables)

    def last_part(part, near, far, made):
        cells_spec = pl.BlockSpec((bunch * cell_rows // 2, LANES), lambda i: (i + part * groups, 0))
        return pl.pallas_call(
            functools.partial(last_kernel, sizes, bunch),
            grid=(groups,),
            in_specs=[smem, vmem, vmem]
            + [cells_spec] * 4
            + [table_spec]
            + [pl.BlockSpec(memory_space=pl.ANY)] * len(made),
            out_specs=pl.BlockSpec((bunch, length, length), lambda i: (i + part * groups, 0, 0)),
            out_shape=shape(planes, length, length),
            scratch_shapes=scratch(2),
            input_output_aliases={8: 0} if made else {},
            compiler_params=SMALL,
            cost_estimate=cost(3 * work, 4 << 20),
        )(place, near, far, upper, lower, upper_other, lower_other, tables, *made)

    first, upper_other = lax.optimization_barrier((first, upper_other))
    near = swap(first)
    far = lax.ppermute(near, "band", [(0, 1), (1, 0)])
    second, lower_other = lax.optimization_barrier((second, lower_other))
    near_second = swap(second)
    far_second = lax.ppermute(near_second, "band", [(0, 1), (1, 0)])
    potential = last_part(0, near, far, [])
    potential = last_part(1, near_second, far_second, [potential])
    return (fresh, potential)


def local(orbitals, occupations, ion_potential, hxc_potential):
    length = orbitals.shape[-1]
    parts = 2 * lax.axis_size("grid") * LANES
    fits = lax.axis_size("grid") & (lax.axis_size("grid") - 1) == 0
    fits = fits and orbitals.shape[2] % 2 == 0 and length == LANES + LANES // 2 and lax.axis_size("band") == 2 and length * length % parts == 0
    path = packed_path if fits else general
    return path(orbitals, occupations, ion_potential, hxc_potential)


def solution(mesh):
    placed = (
        P("band", None, "grid", None, None),
        P("band"),
        P("grid", None, None),
        P("grid", None, None),
    )
    return jax.shard_map(
        local,
        mesh=mesh,
        in_specs=placed,
        out_specs=(P("band", None, "grid", None, None), P("grid", None, None)),
        check_vma=False,
    )
```
